512 devices in a mesh: gx: 32 (over y, x, core), gy: 16 (over z).
Axes of the slice: x: 4, y: 4, z: 16, core: 2. Of those that a mesh axis runs over, the one named last changes fastest.
Arguments:
- phi_start: float32 [256, 128, 512], P('gx', 'gy'), may hold values from -6 to 6
- right_side: float32 [256, 128, 512], P('gx', 'gy'), may hold values from -8 to 8
- coefficient: float32 [256, 128, 512], P('gx', 'gy'), may hold values from 0.25 to 4
Outputs:
- phi_fine: float32 [256, 128, 512], P('gx', 'gy')
- correction: float32 [128, 64, 256], P('gx', 'gy')
The draws below stay inside these ranges and needn't reach their ends.
All inputs are finite; a program needn't handle non-finite values.
Results may differ from the reference program's by a relative error of at most 0.0003.
Values sent between devices are 32-bit elements; how exact they have to be, the bound alone decides.
No kernel may reach another device: no remote copies, remote signals or barrier semaphores. Data moves between devices by JAX's collectives and lax.ppermute only.
A program may use at most 64 MiB of HBM per device.

```python
import math
import jax
import jax.numpy as jnp

BOTTOM = 6
NX = 256
NY = 128
NZ = 512


def draw_right_side(key, part):
    key = jax.random.fold_in(key, 11)
    roughness = jax.random.normal(key, (NX, NY, NZ), jnp.float32)
    values = roughness
    return jnp.clip(values, -8.0, 8.0)


def block_levels(rng, extent, split, least, top_value):
    factor_of, own = 1.0, jax.random.fold_in(rng, 6)
    for position, parts in split:
        steps = jnp.exp(jax.random.uniform(jax.random.fold_in(own, position), (parts,), jnp.float32, least / len(split), top_value / len(split)))
        factor_of = factor_of * jnp.repeat(steps, extent[position] // parts).reshape([-1 if axis == position else 1 for axis in range(len(extent))])
    return factor_of


def centred(key, extent, spread, reach, split=(), held_as=jnp.bfloat16):
    entries = jax.random.normal(key, extent, jnp.float32) * spread
    if len(split) > 0:
        entries = block_levels(key, extent, split, -0.22, 0.18) * entries
    return jnp.clip(entries, min=-reach, max=reach).astype(held_as)


def setup_inputs(seed: int = 0) -> dict:
    streams_of = jax.random.split(jax.random.key(seed), 4)
    return {
        "phi_start": centred(streams_of[0], (NX, NY, NZ), 1.0, 6.0, ((0, 32), (1, 16)), jnp.float32),
        "right_side": draw_right_side(jax.random.fold_in(streams_of[3], 71), 0),
        "coefficient": jnp.clip(jnp.exp(math.log(4.0) - 2.7725887 * jax.random.uniform(streams_of[2], (NX, NY, NZ), jnp.float32) ** block_levels(streams_of[2], (NX, NY, NZ), ((0, 32), (1, 16)), -0.2, 0.2)), 0.25, 4.0),
    }


RELAX_WEIGHT = 0.8


def neighbour_views(padded):
    return [padded[2:, 1:-1, 1:-1], padded[:-2, 1:-1, 1:-1],
            padded[1:-1, 2:, 1:-1], padded[1:-1, :-2, 1:-1],
            padded[1:-1, 1:-1, 2:], padded[1:-1, 1:-1, :-2]]


def face_weights(padded_coef):
    centre = padded_coef[1:-1, 1:-1, 1:-1]
    weights = []
    for neighbour in neighbour_views(padded_coef):
        weights.append(jnp.where(neighbour > 0.0, 2.0 * centre * neighbour / (centre + neighbour), centre))
    diagonal = weights[0] + weights[1] + weights[2] + weights[3] + weights[4] + weights[5]
    return weights, diagonal


def apply_operator(padded, weights, diagonal):
    result = diagonal * padded[1:-1, 1:-1, 1:-1]
    for weight, neighbour in zip(weights, neighbour_views(padded)):
        result = result - weight * neighbour
    return result


def relax_once(current, padded, source, weights, diagonal):
    return current + RELAX_WEIGHT * (source - apply_operator(padded, weights, diagonal)) / diagonal


def descend(source, coef_level, start, extend):
    weights, diagonal = face_weights(extend(coef_level))
    if start is None:
        current = RELAX_WEIGHT * source / diagonal
    else:
        current = relax_once(start, extend(start), source, weights, diagonal)
    current = relax_once(current, extend(current), source, weights, diagonal)
    residual = source - apply_operator(extend(current), weights, diagonal)
    return current, residual


def restrict(values, scale):
    size_x, size_y, size_z = values.shape
    blocks = values.reshape(size_x // 2, 2, size_y // 2, 2, size_z // 2, 2)
    return scale * jnp.mean(blocks, axis=(1, 3, 5))


def prolong(values):
    return jnp.repeat(jnp.repeat(jnp.repeat(values, 2, axis=0), 2, axis=1), 2, axis=2)


def pad_zero(values):
    return jnp.pad(values, 1)


def bottom_solve(source, coef_level):
    weights, diagonal = face_weights(pad_zero(coef_level))
    solution = jnp.zeros_like(source)
    residual = source
    direction = source
    norm_now = jnp.sum(residual * residual)
    for iteration in range(BOTTOM):
        image = apply_operator(pad_zero(direction), weights, diagonal)
        step_size = norm_now / jnp.sum(direction * image)
        solution = solution + step_size * direction
        residual = residual - step_size * image
        norm_next = jnp.sum(residual * residual)
        direction = residual + (norm_next / norm_now) * direction
        norm_now = norm_next
    return solution


def reference(phi_start, right_side, coefficient):
    phi_fine, residual = descend(right_side, coefficient, phi_start, pad_zero)
    source_mid = restrict(residual, 4.0)
    coef_mid = restrict(coefficient, 1.0)
    error_mid, residual_mid = descend(source_mid, coef_mid, None, pad_zero)
    source_low = restrict(residual_mid, 4.0)
    coef_low = restrict(coef_mid, 1.0)
    error_low, residual_low = descend(source_low, coef_low, None, pad_zero)
    source_bottom = restrict(residual_low, 4.0)
    coef_bottom = restrict(coef_low, 1.0)
    error_bottom = bottom_solve(source_bottom, coef_bottom)
    error_low_total = error_low + prolong(error_bottom)
    correction = error_mid + prolong(error_low_total)
    return phi_fine, correction
```

```python
import jax
import jax.numpy as jnp
from jax import lax
from jax.experimental import pallas as pl
from jax.experimental.pallas import tpu as pltpu
from jax.sharding import PartitionSpec as P

BOTTOM = 6
RELAX_WEIGHT = 0.8
TINY = 1e-30
F32 = jnp.float32
VMEM = pl.BlockSpec(memory_space=pltpu.VMEM)
SMEM = pl.BlockSpec(memory_space=pltpu.SMEM)
PARAMS = pltpu.CompilerParams(vmem_limit_bytes=24 * 1024 * 1024)


def call(kernel, out_shapes, scratch=(), specs=None, n_in=0):
    return pl.pallas_call(
        kernel,
        out_shape=[jax.ShapeDtypeStruct(s, F32) for s in out_shapes],
        in_specs=specs if specs is not None else [VMEM] * n_in,
        out_specs=[VMEM] * len(out_shapes),
        scratch_shapes=[pltpu.VMEM(s, F32) for s in scratch],
        compiler_params=PARAMS,
    )


def harmonic(a, b):
    return 2.0 * a * b / jnp.maximum(a + b, TINY)


def along(v, axis, step):
    n = v.shape[axis]
    return pltpu.roll(v, (-step) % n, axis)


def positions(shape, axis):
    return lax.broadcasted_iota(jnp.int32, shape, axis)


def halving(rows, cols):
    return (positions((rows, cols), 0) // 2 == positions((rows, cols), 1)).astype(F32)


def doubling(rows, cols, factor):
    return (positions((rows, cols), 1) // factor == positions((rows, cols), 0)).astype(F32)


def matmul(a, b):
    return jnp.dot(a, b, precision=lax.Precision.HIGHEST, preferred_element_type=F32)


def weight(face, centre):
    return jnp.where(face > 0.0, face, centre)


def diagonal_of(c, xp, xm, hy, hz):
    return (weight(xp, c) + weight(xm, c) + weight(hy, c) + weight(along(hy, 0, -1), c)
            + weight(hz, c) + weight(along(hz, 1, -1), c))


def operate(d, v, xp, vp, xm, vm, hy, hz):
    out = d * v - xp * vp - xm * vm
    out = out - hy * along(v, 0, 1) - along(hy * v, 0, -1)
    return out - hz * along(v, 1, 1) - along(hz * v, 1, -1)


def z_face(c):
    nxt = jnp.where(positions(c.shape, 1) < c.shape[1] - 1, along(c, 1, 1), 0.0)
    return harmonic(c, nxt)


NP, NR, NC = 7, 6, 7
NROWS = NP + NR + NC


def pack_y(phi, rhs, coef, up, dn, stage):
    k = 0
    for a, (ref, n) in enumerate(((phi, NP), (rhs, NR), (coef, NC))):
        for q in range(4):
            lanes = slice(128 * q, 128 * q + 128)
            base = 64 * (4 * a + q)
            stage[base:base + 64, :] = ref[:, lanes]
            for j in range(n):
                rows = slice(8 * (k + j), 8 * (k + j) + 8)
                up[rows, lanes] = stage[pl.ds(base + 8 - n + j, 8, stride=8), :]
                dn[rows, lanes] = stage[pl.ds(base + j, 8, stride=8), :]
        k += n


def pack_x(phi, rhs, coef, lo, hi, pe, re, ce, up, dn, stage):
    zero = jnp.zeros((8, 128), F32)
    k = 0
    for a, (ref, ext, n) in enumerate(((phi, pe, NP), (rhs, re, NR), (coef, ce, NC))):
        for x in range(8):
            ext[24 * x:24 * x + 8, :] = ref[8 * x:8 * x + 8, :]
        for q in range(4):
            lanes = slice(128 * q, 128 * q + 128)
            base = 128 * (4 * a + q)
            for j in range(n):
                rows = slice(8 * (k + j), 8 * (k + j) + 8)
                stage[pl.ds(base + j, 8, stride=16), :] = hi[rows, lanes]
                stage[pl.ds(base + 16 - n + j, 8, stride=16), :] = lo[rows, lanes]
            for j in range(n, 16 - n):
                stage[pl.ds(base + j, 8, stride=16), :] = zero
            for x in range(8):
                ext[24 * x + 8:24 * x + 24, lanes] = stage[base + 16 * x:base + 16 * x + 16, :]
        k += n
    up[0:72, :] = pe[120:192, :]
    up[72:120, :] = re[144:192, :]
    up[120:192, :] = ce[120:192, :]
    dn[0:72, :] = pe[0:72, :]
    dn[72:120, :] = re[0:48, :]
    dn[120:192, :] = ce[0:72, :]


def fine(pe, re, ce, lo, hi, phi_out, smid, cmid, mup, mdn,
         p0, rs, c, hx, hy, hz, dg, rd, p1, p2, sums, packed):
    p0[0:3] = lo[0:3]
    p0[3:11] = pe[...]
    p0[11:14] = hi[0:3]
    rs[1:3] = lo[3:5]
    rs[3:11] = re[...]
    rs[11:13] = hi[3:5]
    c[0:3] = lo[5:8]
    c[3:11] = ce[...]
    c[11:14] = hi[5:8]
    hx[0] = harmonic(c[0], c[1])

    def first(i, carry):
        ci = c[i]
        xp, xm = harmonic(ci, c[i + 1]), hx[i - 1]
        hyi = harmonic(ci, along(ci, 0, 1))
        hzi = z_face(ci)
        d = diagonal_of(ci, xp, xm, hyi, hzi)
        r = RELAX_WEIGHT / jnp.maximum(d, TINY)
        hx[i], hy[i], hz[i], dg[i], rd[i] = xp, hyi, hzi, d, r
        v = p0[i]
        p1[i] = v + (rs[i] - operate(d, v, xp, p0[i + 1], xm, p0[i - 1], hyi, hzi)) * r
        return carry

    lax.fori_loop(1, 13, first, 0)

    def second(i, carry):
        v = p1[i]
        image = operate(dg[i], v, hx[i], p1[i + 1], hx[i - 1], p1[i - 1], hy[i], hz[i])
        p2[i] = v + (rs[i] - image) * rd[i]
        return carry

    lax.fori_loop(2, 12, second, 0)
    for x in range(8):
        phi_out[x] = p2[3 + x, 0:8, :]

    def residual(i):
        return rs[i] - operate(dg[i], p2[i], hx[i], p2[i + 1], hx[i - 1], p2[i - 1], hy[i], hz[i])

    def pairs(k, carry):
        i = 3 + 2 * k
        s = residual(i) + residual(i + 1)
        t = c[i] + c[i + 1]
        s = (s + along(s, 0, 1)) * 0.5
        t = (t + along(t, 0, 1)) * 0.125
        for q in range(4):
            sums[q, k] = s[:, 128 * q:128 * q + 128]
            sums[q, 4 + k] = t[:, 128 * q:128 * q + 128]
        return carry

    lax.fori_loop(0, 4, pairs, 0)
    for k in range(8):
        for q in range(4):
            lanes = slice(128 * q, 128 * q + 128)
            packed[16 * k:16 * k + 8, lanes] = sums[q, k, pl.ds(0, 8, stride=2), :]
            packed[16 * k + 8:16 * k + 12, lanes] = jnp.zeros((4, 128), F32)
            packed[16 * k + 12:16 * k + 16, lanes] = sums[q, k, pl.ds(16, 4, stride=2), :]
    mid = matmul(packed[...], halving(512, 256)).reshape(8, 16, 256)
    smid[...] = mid[0:4]
    cmid[...] = mid[4:8]
    mup[0:2] = mid[2:4]
    mup[2:6] = mid[4:8]
    mdn[0:2] = mid[0:2]
    mdn[2:6] = mid[4:8]


def middle(smid, cmid, lo, hi, emid, out, sums):
    s = [lo[0], lo[1]] + [smid[x] for x in range(4)] + [hi[0], hi[1]]
    c = [lo[2 + x] for x in range(4)] + [cmid[x] for x in range(4)] + [hi[2 + x] for x in range(4)]
    hx = [harmonic(c[j], c[j + 1]) for j in range(1, 10)]
    hy, hz, d, r, e1 = [], [], [], [], []
    for i in range(8):
        ci = c[i + 2]
        hy.append(harmonic(ci, along(ci, 0, 1)))
        hz.append(z_face(ci))
        d.append(diagonal_of(ci, hx[i + 1], hx[i], hy[i], hz[i]))
        r.append(RELAX_WEIGHT / jnp.maximum(d[i], TINY))
        e1.append(s[i] * r[i])

    def image(i, e):
        return operate(d[i], e[i], hx[i + 1], e[i + 1], hx[i], e[i - 1], hy[i], hz[i])

    e2 = [None] + [e1[i] + (s[i] - image(i, e1)) * r[i] for i in range(1, 7)] + [None]
    res = [s[i] - image(i, e2) for i in range(2, 6)]
    for x in range(4):
        emid[x] = e2[2 + x][0:4, :]
    groups = [(res[2 * x] + res[2 * x + 1]) * 0.5 for x in range(2)]
    groups += [(c[2 * x] + c[2 * x + 1]) * 0.125 for x in range(6)]
    for g in range(8):
        both = (groups[g] + along(groups[g], 0, 1))[0:8, :]
        sums[8 * g:8 * g + 8, :] = both[:, 0:128]
        sums[64 + 8 * g:72 + 8 * g, :] = both[:, 128:256]

    def rows(y):
        return jnp.concatenate([sums[pl.ds(64 * q + 2 * y, 8, stride=8), :] for q in range(2)], axis=1)

    low0 = matmul(rows(0), halving(256, 128))
    low1 = matmul(rows(1), halving(256, 128))
    for n in range(16):
        out[n, 0:8, :] = low0
        out[n, 8:16, :] = low1


def y_face(c):
    n = c.shape[0]
    return harmonic(c, jnp.where(positions(c.shape, 0) < n - 1, along(c, 0, 1), 0.0))


def columns(gathered, sd, ccol):
    for g in range(8):
        for y in range(2):
            rows = gathered[pl.ds(8 * y + g, 16, stride=16), :]
            if g < 2:
                sd[pl.ds(32 * g + y, 16, stride=2), :] = rows
            else:
                ccol[pl.ds(32 * (g - 2) + y, 16, stride=2), :] = rows
    c = [ccol[32 * j:32 * j + 32, :] for j in range(6)]
    hx = [harmonic(c[j], c[j + 1]) for j in range(1, 4)]
    for x in range(2):
        ci = c[2 + x]
        sd[64 + 32 * x:96 + 32 * x, :] = diagonal_of(ci, hx[x + 1], hx[x], y_face(ci), z_face(ci))


def low(sd, ccol, lo, hi, elow, out, sums):
    def part(ref, k):
        return ref[32 * k:32 * k + 32, :]

    s = [part(ref, k) for ref in (lo, sd, hi) for k in (0, 1)]
    d = [part(ref, k) for ref in (lo, sd, hi) for k in (2, 3)]
    c = [part(ccol, k) for k in range(6)]
    hx = [harmonic(c[j], c[j + 1]) for j in range(5)]
    hy = [y_face(ci) for ci in c]
    hz = [z_face(ci) for ci in c]
    r = [RELAX_WEIGHT / jnp.maximum(di, TINY) for di in d]
    e1 = [s[i] * r[i] for i in range(6)]

    def image(i, e):
        return operate(d[i], e[i], hx[i], e[i + 1], hx[i - 1], e[i - 1], hy[i], hz[i])

    e2 = [None] + [e1[i] + (s[i] - image(i, e1)) * r[i] for i in range(1, 5)] + [None]
    res = [s[i] - image(i, e2) for i in range(2, 4)]
    for x in range(2):
        elow[32 * x:32 * x + 32, :] = e2[2 + x]
    a = (res[0] + res[1]) * 0.5
    b = (c[2] + c[3]) * 0.125
    sums[0:32, :] = a + along(a, 0, 1)
    sums[32:64, :] = b + along(b, 0, 1)
    ra = sums[pl.ds(0, 16, stride=2), :]
    rb = sums[pl.ds(32, 16, stride=2), :]
    both = matmul(jnp.concatenate([ra, rb], axis=1), halving(256, 128))
    for n in range(32):
        out[n] = both


def bottom(place, gathered, elow, emid, out, hx, hy, hz, dg, sol, res, dire, img):
    half = positions((16, 128), 1) < 64
    last_z = positions((16, 128), 1) % 64 == 63
    last_y = positions((16, 128), 0) == 15
    c = []
    for x in range(16):
        a, b = gathered[x], gathered[x + 16]
        source = jnp.where(half, a, along(b, 1, 64))
        c.append(jnp.where(half, along(a, 1, 64), b))
        res[x] = source
        dire[x] = source
        sol[x] = jnp.zeros((16, 128), F32)
    for x in range(16):
        nxt = c[x + 1] if x < 15 else jnp.where(half, along(c[0], 1, 64), 0.0)
        hx[x + 1] = harmonic(c[x], nxt)
    hx[0] = along(hx[16], 1, 64)
    for x in range(16):
        hy[x] = harmonic(c[x], jnp.where(last_y, 0.0, along(c[x], 0, 1)))
        hz[x] = harmonic(c[x], jnp.where(last_z, 0.0, along(c[x], 1, 1)))
        dg[x] = diagonal_of(c[x], hx[x + 1], hx[x], hy[x], hz[x])

    def total(acc):
        return jnp.sum(acc, axis=(0, 1), keepdims=True)

    def dot_image():
        acc = jnp.zeros((16, 128), F32)
        for x in range(16):
            v = dire[x]
            vp = dire[x + 1] if x < 15 else along(dire[0], 1, 64)
            vm = dire[x - 1] if x > 0 else along(dire[15], 1, 64)
            image = operate(dg[x], v, hx[x + 1], vp, hx[x], vm, hy[x], hz[x])
            img[x] = image
            acc = acc + v * image
        return total(acc)

    def norm():
        acc = jnp.zeros((16, 128), F32)
        for x in range(16):
            acc = acc + res[x] * res[x]
        return total(acc)

    def step(_, rr):
        alpha = rr / dot_image()
        acc = jnp.zeros((16, 128), F32)
        for x in range(16):
            sol[x] = sol[x] + alpha * dire[x]
            rx = res[x] - alpha * img[x]
            res[x] = rx
            acc = acc + rx * rx
        new = total(acc)
        beta = new / rr
        for x in range(16):
            dire[x] = res[x] + beta * dire[x]
        return new

    rr = lax.fori_loop(0, BOTTOM - 1, step, norm())
    gx, gy = place[0], place[1]
    xi = lax.rem(gx, 16)
    alpha = rr / dot_image()
    mine = sol[xi] + alpha * dire[xi]
    mine = jnp.where(gx >= 16, along(mine, 1, 64), mine)
    row = positions((16, 128), 0)
    mine = jnp.sum(jnp.where(row == gy, mine, 0.0), axis=0, keepdims=True)
    row = positions((32, 128), 0)
    lows = []
    for x in range(2):
        e = elow[32 * x:32 * x + 32, :]
        for y in range(2):
            lows.append(jnp.sum(jnp.where(row == 2 * gy + y, e, 0.0), axis=0, keepdims=True))
    coarse = matmul(jnp.broadcast_to(mine, (8, 128)), doubling(128, 256, 4))
    finer = matmul(jnp.concatenate(lows + lows, axis=0), doubling(128, 256, 2))
    for x in range(4):
        k = 2 * (x // 2)
        for y in range(4):
            add = finer[k + y // 2:k + y // 2 + 1, :] + coarse[0:1, :]
            out[x, y:y + 1, :] = emid[x, y:y + 1, :] + add


def neighbours(up, dn, axis):
    n = lax.axis_size(axis)
    forth = [(i, i + 1) for i in range(n - 1)]
    back = [(i + 1, i) for i in range(n - 1)]
    return lax.ppermute(up, axis, forth), lax.ppermute(dn, axis, back)


def shards(phi_start, right_side, coefficient):
    own = [a.reshape(64, 512) for a in (phi_start, right_side, coefficient)]
    up, dn = call(pack_y, [(8 * NROWS, 512)] * 2, [(768, 128)], n_in=3)(*own)
    lo, hi = neighbours(up, dn, "gy")
    *ext, up, dn = call(pack_x, [(192, 512)] * 5, [(1536, 128)], n_in=5)(*own, lo, hi)
    lo, hi = neighbours(up, dn, "gx")
    box = (14, 24, 512)
    phi_fine, smid, cmid, up, dn = call(
        fine,
        [(8, 8, 512), (4, 16, 256), (4, 16, 256), (6, 16, 256), (6, 16, 256)],
        [box] * 10 + [(4, 8, 24, 128), (128, 512)],
        n_in=5,
    )(*[a.reshape(8, 24, 512) for a in (*ext, lo, hi)])
    lo, hi = neighbours(up, dn, "gx")
    emid, spread = call(middle, [(4, 4, 256), (16, 16, 128)], [(128, 128)], n_in=4)(smid, cmid, lo, hi)
    gathered = lax.all_to_all(spread, "gy", 0, 0, tiled=True)
    sd, ccol = call(columns, [(128, 128), (192, 128)], n_in=1)(gathered.reshape(256, 128))
    lo, hi = neighbours(sd, sd, "gx")
    elow, spread = call(low, [(64, 128), (32, 16, 128)], [(64, 128)], n_in=4)(sd, ccol, lo, hi)
    gathered = lax.all_to_all(spread, "gx", 0, 0, tiled=True)
    place = jnp.stack([lax.axis_index("gx"), lax.axis_index("gy")]).astype(jnp.int32)
    (correction,) = call(
        bottom,
        [(4, 4, 256)],
        [(17, 16, 128)] + [(16, 16, 128)] * 7,
        specs=[SMEM, VMEM, VMEM, VMEM],
    )(place, gathered, elow, emid)
    return phi_fine, correction


def solution(mesh):
    return jax.shard_map(
        shards,
        mesh=mesh,
        in_specs=(P("gx", "gy", None),) * 3,
        out_specs=(P("gx", "gy", None),) * 2,
        check_vma=False,
    )
```

```python
import jax
import jax.numpy as jnp
from jax import lax
from jax.experimental import pallas as pl
from jax.experimental.pallas import tpu as pltpu
from jax.sharding import PartitionSpec as P

BOTTOM = 6
RELAX_WEIGHT = 0.8
TINY = 1e-30
F32 = jnp.float32
VMEM = pl.BlockSpec(memory_space=pltpu.VMEM)
HBM = pl.BlockSpec(memory_space=pltpu.HBM)


def call(kernel, out_shapes, scratch=(), n_in=0, copies=0, in_hbm=0, out_hbm=0, limit=24 * 1024 * 1024):
    semaphores = [pltpu.SemaphoreType.DMA((copies,))] if copies else []
    return pl.pallas_call(
        kernel,
        out_shape=[jax.ShapeDtypeStruct(s, F32) for s in out_shapes],
        in_specs=[HBM] * in_hbm + [VMEM] * (n_in - in_hbm),
        out_specs=[HBM] * out_hbm + [VMEM] * (len(out_shapes) - out_hbm),
        scratch_shapes=[pltpu.VMEM(s, F32) for s in scratch] + semaphores,
        compiler_params=pltpu.CompilerParams(vmem_limit_bytes=limit),
    )


def harmonic(a, b):
    return 2.0 * a * b / jnp.maximum(a + b, TINY)


def along(v, axis, step):
    n = v.shape[axis]
    return pltpu.roll(v, (-step) % n, axis)


def positions(shape, axis):
    return lax.broadcasted_iota(jnp.int32, shape, axis)


def halving(rows, cols):
    return (positions((rows, cols), 0) // 2 == positions((rows, cols), 1)).astype(F32)


def doubling(rows, cols, factor):
    return (positions((rows, cols), 1) // factor == positions((rows, cols), 0)).astype(F32)


def matmul(a, b):
    return jnp.dot(a, b, precision=lax.Precision.HIGHEST, preferred_element_type=F32)


def weight(face, centre):
    return jnp.where(face > 0.0, face, centre)


def diagonal_of(c, xp, xm, hy, hz):
    return (weight(xp, c) + weight(xm, c) + weight(hy, c) + weight(along(hy, 0, -1), c)
            + weight(hz, c) + weight(along(hz, 1, -1), c))


def operate(d, v, xp, vp, xm, vm, hy, hz):
    out = d * v - xp * vp - xm * vm
    out = out - hy * along(v, 0, 1) - along(hy * v, 0, -1)
    return out - hz * along(v, 1, 1) - along(hz * v, 1, -1)


def z_face(c):
    nxt = jnp.where(positions(c.shape, 1) < c.shape[1] - 1, along(c, 1, 1), 0.0)
    return harmonic(c, nxt)


NP, NR, NC = 7, 6, 7
NROWS = NP + NR + NC


def pack_y(phi_in, rhs_in, coef_in, up_out, dn_out, phi, rhs, coef, stage, up, dn, sem):
    loads = [pltpu.make_async_copy(src, dst, sem.at[a])
             for a, (src, dst) in enumerate(((phi_in, phi), (rhs_in, rhs), (coef_in, coef)))]
    for load in loads:
        load.start()
    stores = []
    k = 0
    for a, (ref, n) in enumerate(((phi, NP), (rhs, NR), (coef, NC))):
        loads[a].wait()
        for q in range(4):
            lanes = slice(128 * q, 128 * q + 128)
            base = 64 * (4 * a + q)
            stage[base:base + 64, :] = ref[:, lanes]
            for j in range(n):
                rows = slice(8 * (k + j), 8 * (k + j) + 8)
                up[rows, lanes] = stage[pl.ds(base + 8 - n + j, 8, stride=8), :]
                dn[rows, lanes] = stage[pl.ds(base + j, 8, stride=8), :]
        for b, (src, dst) in enumerate(((up, up_out), (dn, dn_out))):
            part = pl.ds(8 * k, 8 * n)
            stores.append(pltpu.make_async_copy(src.at[part], dst.at[part], sem.at[3 + 2 * a + b]))
            stores[-1].start()
        k += n
    for store in stores:
        store.wait()


def pack_x(phi, rhs, coef, lo, hi, pe, re, ce, up, dn, stage):
    zero = jnp.zeros((8, 128), F32)
    k = 0
    for a, (ref, ext, n) in enumerate(((phi, pe, NP), (rhs, re, NR), (coef, ce, NC))):
        for x in range(8):
            ext[24 * x:24 * x + 8, :] = ref[8 * x:8 * x + 8, :]
        for q in range(4):
            lanes = slice(128 * q, 128 * q + 128)
            base = 128 * (4 * a + q)
            for j in range(n):
                rows = slice(8 * (k + j), 8 * (k + j) + 8)
                stage[pl.ds(base + j, 8, stride=16), :] = hi[rows, lanes]
                stage[pl.ds(base + 16 - n + j, 8, stride=16), :] = lo[rows, lanes]
            for j in range(n, 16 - n):
                stage[pl.ds(base + j, 8, stride=16), :] = zero
            for x in range(8):
                ext[24 * x + 8:24 * x + 24, lanes] = stage[base + 16 * x:base + 16 * x + 16, :]
        k += n
    up[0:72, :] = pe[120:192, :]
    up[72:120, :] = re[144:192, :]
    up[120:192, :] = ce[120:192, :]
    dn[0:72, :] = pe[0:72, :]
    dn[72:120, :] = re[0:48, :]
    dn[120:192, :] = ce[0:72, :]


def fine(pe, re, ce, lo, hi, phi_out, smid, cmid, mup, mdn,
         p0, rs, c, hx, hy, hz, dg, rd, p1, p2, sums, packed, own, left):
    p0[0:3] = lo[0:3]
    p0[3:11] = pe[...]
    p0[11:14] = hi[0:3]
    rs[1:3] = lo[3:5]
    rs[3:11] = re[...]
    rs[11:13] = hi[3:5]
    c[0:3] = lo[5:8]
    c[3:11] = ce[...]
    c[11:14] = hi[5:8]
    hx[0] = harmonic(c[0], c[1])

    def first(i, carry):
        ci = c[i]
        xp, xm = harmonic(ci, c[i + 1]), hx[i - 1]
        hyi = harmonic(ci, along(ci, 0, 1))
        hzi = z_face(ci)
        d = diagonal_of(ci, xp, xm, hyi, hzi)
        r = RELAX_WEIGHT / jnp.maximum(d, TINY)
        hx[i], hy[i], hz[i], dg[i], rd[i] = xp, hyi, hzi, d, r
        v = p0[i]
        p1[i] = v + (rs[i] - operate(d, v, xp, p0[i + 1], xm, p0[i - 1], hyi, hzi)) * r
        return carry

    lax.fori_loop(1, 13, first, 0)

    def second(i, carry):
        v = p1[i]
        image = operate(dg[i], v, hx[i], p1[i + 1], hx[i - 1], p1[i - 1], hy[i], hz[i])
        p2[i] = v + (rs[i] - image) * rd[i]
        return carry

    lax.fori_loop(2, 12, second, 0)
    for x in range(8):
        own[x] = p2[3 + x, 0:8, :]
    store = pltpu.make_async_copy(own, phi_out, left.at[0])
    store.start()

    def residual(i):
        return rs[i] - operate(dg[i], p2[i], hx[i], p2[i + 1], hx[i - 1], p2[i - 1], hy[i], hz[i])

    def pairs(k, carry):
        i = 3 + 2 * k
        s = residual(i) + residual(i + 1)
        t = c[i] + c[i + 1]
        s = (s + along(s, 0, 1)) * 0.5
        t = (t + along(t, 0, 1)) * 0.125
        for q in range(4):
            sums[q, k] = s[:, 128 * q:128 * q + 128]
            sums[q, 4 + k] = t[:, 128 * q:128 * q + 128]
        return carry

    lax.fori_loop(0, 4, pairs, 0)
    for k in range(8):
        for q in range(4):
            lanes = slice(128 * q, 128 * q + 128)
            packed[16 * k:16 * k + 8, lanes] = sums[q, k, pl.ds(0, 8, stride=2), :]
            packed[16 * k + 8:16 * k + 12, lanes] = jnp.zeros((4, 128), F32)
            packed[16 * k + 12:16 * k + 16, lanes] = sums[q, k, pl.ds(16, 4, stride=2), :]
    mid = matmul(packed[...], halving(512, 256)).reshape(8, 16, 256)
    smid[...] = mid[0:4]
    cmid[...] = mid[4:8]
    mup[0:2] = mid[2:4]
    mup[2:6] = mid[4:8]
    mdn[0:2] = mid[0:2]
    mdn[2:6] = mid[4:8]
    store.wait()


def middle(smid, cmid, lo, hi, emid, out, sums):
    s = [lo[0], lo[1]] + [smid[x] for x in range(4)] + [hi[0], hi[1]]
    c = [lo[2 + x] for x in range(4)] + [cmid[x] for x in range(4)] + [hi[2 + x] for x in range(4)]
    hx = [harmonic(c[j], c[j + 1]) for j in range(1, 10)]
    hy, hz, d, r, e1 = [], [], [], [], []
    for i in range(8):
        ci = c[i + 2]
        hy.append(harmonic(ci, along(ci, 0, 1)))
        hz.append(z_face(ci))
        d.append(diagonal_of(ci, hx[i + 1], hx[i], hy[i], hz[i]))
        r.append(RELAX_WEIGHT / jnp.maximum(d[i], TINY))
        e1.append(s[i] * r[i])

    def image(i, e):
        return operate(d[i], e[i], hx[i + 1], e[i + 1], hx[i], e[i - 1], hy[i], hz[i])

    e2 = [None] + [e1[i] + (s[i] - image(i, e1)) * r[i] for i in range(1, 7)] + [None]
    res = [s[i] - image(i, e2) for i in range(2, 6)]
    for x in range(4):
        emid[x] = e2[2 + x][0:4, :]
    groups = [(res[2 * x] + res[2 * x + 1]) * 0.5 for x in range(2)]
    groups += [(c[2 * x] + c[2 * x + 1]) * 0.125 for x in range(6)]
    for g in range(8):
        both = (groups[g] + along(groups[g], 0, 1))[0:8, :]
        sums[8 * g:8 * g + 8, :] = both[:, 0:128]
        sums[64 + 8 * g:72 + 8 * g, :] = both[:, 128:256]

    def rows(y):
        return jnp.concatenate([sums[pl.ds(64 * q + 2 * y, 8, stride=8), :] for q in range(2)], axis=1)

    low0 = matmul(rows(0), halving(256, 128))
    low1 = matmul(rows(1), halving(256, 128))
    for n in range(16):
        out[n, 0:8, :] = low0
        out[n, 8:16, :] = low1


def y_face(c):
    n = c.shape[0]
    return harmonic(c, jnp.where(positions(c.shape, 0) < n - 1, along(c, 0, 1), 0.0))


def columns(gathered, sd, ccol):
    for g in range(8):
        for y in range(2):
            rows = gathered[pl.ds(8 * y + g, 16, stride=16), :]
            if g < 2:
                sd[pl.ds(32 * g + y, 16, stride=2), :] = rows
            else:
                ccol[pl.ds(32 * (g - 2) + y, 16, stride=2), :] = rows
    c = [ccol[32 * j:32 * j + 32, :] for j in range(6)]
    hx = [harmonic(c[j], c[j + 1]) for j in range(1, 4)]
    for x in range(2):
        ci = c[2 + x]
        sd[64 + 32 * x:96 + 32 * x, :] = diagonal_of(ci, hx[x + 1], hx[x], y_face(ci), z_face(ci))


def low(sd, ccol, lo, hi, elow, out, sums):
    def part(ref, k):
        return ref[32 * k:32 * k + 32, :]

    s = [part(ref, k) for ref in (lo, sd, hi) for k in (0, 1)]
    d = [part(ref, k) for ref in (lo, sd, hi) for k in (2, 3)]
    c = [part(ccol, k) for k in range(6)]
    hx = [harmonic(c[j], c[j + 1]) for j in range(5)]
    hy = [y_face(ci) for ci in c]
    hz = [z_face(ci) for ci in c]
    r = [RELAX_WEIGHT / jnp.maximum(di, TINY) for di in d]
    e1 = [s[i] * r[i] for i in range(6)]

    def image(i, e):
        return operate(d[i], e[i], hx[i], e[i + 1], hx[i - 1], e[i - 1], hy[i], hz[i])

    e2 = [None] + [e1[i] + (s[i] - image(i, e1)) * r[i] for i in range(1, 5)] + [None]
    res = [s[i] - image(i, e2) for i in range(2, 4)]
    for x in range(2):
        elow[32 * x:32 * x + 32, :] = e2[2 + x]
    a = (res[0] + res[1]) * 0.5
    b = (c[2] + c[3]) * 0.125
    sums[0:32, :] = a + along(a, 0, 1)
    sums[32:64, :] = b + along(b, 0, 1)
    ra = sums[pl.ds(0, 16, stride=2), :]
    rb = sums[pl.ds(32, 16, stride=2), :]
    both = matmul(jnp.concatenate([ra, rb], axis=1), halving(256, 128))
    for n in range(32):
        out[n] = both


def bottom(gathered, elow, emid, out, hx, hy, hz, dg, sol, res, dire, img):
    half = positions((16, 128), 1) < 64
    last_z = positions((16, 128), 1) % 64 == 63
    last_y = positions((16, 128), 0) == 15
    c = []
    for x in range(16):
        a, b = gathered[x], gathered[x + 16]
        source = jnp.where(half, a, along(b, 1, 64))
        c.append(jnp.where(half, along(a, 1, 64), b))
        res[x] = source
        dire[x] = source
        sol[x] = jnp.zeros((16, 128), F32)
    for x in range(16):
        nxt = c[x + 1] if x < 15 else jnp.where(half, along(c[0], 1, 64), 0.0)
        hx[x + 1] = harmonic(c[x], nxt)
    hx[0] = along(hx[16], 1, 64)
    for x in range(16):
        hy[x] = harmonic(c[x], jnp.where(last_y, 0.0, along(c[x], 0, 1)))
        hz[x] = harmonic(c[x], jnp.where(last_z, 0.0, along(c[x], 1, 1)))
        dg[x] = diagonal_of(c[x], hx[x + 1], hx[x], hy[x], hz[x])

    def total(acc):
        return jnp.sum(acc, axis=(0, 1), keepdims=True)

    def dot_image():
        acc = jnp.zeros((16, 128), F32)
        for x in range(16):
            v = dire[x]
            vp = dire[x + 1] if x < 15 else along(dire[0], 1, 64)
            vm = dire[x - 1] if x > 0 else along(dire[15], 1, 64)
            image = operate(dg[x], v, hx[x + 1], vp, hx[x], vm, hy[x], hz[x])
            img[x] = image
            acc = acc + v * image
        return total(acc)

    def norm():
        acc = jnp.zeros((16, 128), F32)
        for x in range(16):
            acc = acc + res[x] * res[x]
        return total(acc)

    def step(_, rr):
        alpha = rr / dot_image()
        acc = jnp.zeros((16, 128), F32)
        for x in range(16):
            sol[x] = sol[x] + alpha * dire[x]
            rx = res[x] - alpha * img[x]
            res[x] = rx
            acc = acc + rx * rx
        new = total(acc)
        beta = new / rr
        for x in range(16):
            dire[x] = res[x] + beta * dire[x]
        return new

    rr = lax.fori_loop(0, BOTTOM - 1, step, norm())
    gx, gy = lax.axis_index("gx"), lax.axis_index("gy")
    xi = lax.rem(gx, 16)
    alpha = rr / dot_image()
    mine = sol[xi] + alpha * dire[xi]
    mine = jnp.where(gx >= 16, along(mine, 1, 64), mine)
    row = positions((16, 128), 0)
    mine = jnp.sum(jnp.where(row == gy, mine, 0.0), axis=0, keepdims=True)
    row = positions((32, 128), 0)
    lows = []
    for x in range(2):
        e = elow[32 * x:32 * x + 32, :]
        for y in range(2):
            lows.append(jnp.sum(jnp.where(row == 2 * gy + y, e, 0.0), axis=0, keepdims=True))
    coarse = matmul(jnp.broadcast_to(mine, (8, 128)), doubling(128, 256, 4))
    finer = matmul(jnp.concatenate(lows + lows, axis=0), doubling(128, 256, 2))
    for x in range(4):
        k = 2 * (x // 2)
        for y in range(4):
            add = finer[k + y // 2:k + y // 2 + 1, :] + coarse[0:1, :]
            out[x, y:y + 1, :] = emid[x, y:y + 1, :] + add


def neighbours(up, dn, axis):
    n = lax.axis_size(axis)
    forth = [(i, i + 1) for i in range(n - 1)]
    back = [(i + 1, i) for i in range(n - 1)]
    return lax.ppermute(up, axis, forth), lax.ppermute(dn, axis, back)


def shards(phi_start, right_side, coefficient):
    own = [a.reshape(64, 512) for a in (phi_start, right_side, coefficient)]
    up, dn = call(
        pack_y, [(8 * NROWS, 512)] * 2, [(64, 512)] * 3 + [(768, 128)] + [(8 * NROWS, 512)] * 2,
        n_in=3, copies=9, in_hbm=3, out_hbm=2, limit=64000000)(*own)
    lo, hi = neighbours(up, dn, "gy")
    *ext, up, dn = call(pack_x, [(192, 512)] * 5, [(1536, 128)], n_in=5)(*own, lo, hi)
    lo, hi = neighbours(up, dn, "gx")
    box = (14, 24, 512)
    phi_fine, smid, cmid, up, dn = call(
        fine,
        [(8, 8, 512), (4, 16, 256), (4, 16, 256), (6, 16, 256), (6, 16, 256)],
        [box] * 10 + [(4, 8, 24, 128), (128, 512), (8, 8, 512)],
        n_in=5, copies=1, out_hbm=1,
    )(*[a.reshape(8, 24, 512) for a in (*ext, lo, hi)])
    lo, hi = neighbours(up, dn, "gx")
    emid, spread = call(middle, [(4, 4, 256), (16, 16, 128)], [(128, 128)], n_in=4)(smid, cmid, lo, hi)
    gathered = lax.all_to_all(spread, "gy", 0, 0, tiled=True)
    sd, ccol = call(columns, [(128, 128), (192, 128)], n_in=1)(gathered.reshape(256, 128))
    lo, hi = neighbours(sd, sd, "gx")
    elow, spread = call(low, [(64, 128), (32, 16, 128)], [(64, 128)], n_in=4)(sd, ccol, lo, hi)
    gathered = lax.all_to_all(spread, "gx", 0, 0, tiled=True)
    (correction,) = call(bottom, [(4, 4, 256)], [(17, 16, 128)] + [(16, 16, 128)] * 7, n_in=3)(
        gathered, elow, emid)
    return phi_fine, correction


def solution(mesh):
    return jax.shard_map(
        shards,
        mesh=mesh,
        in_specs=(P("gx", "gy", None),) * 3,
        out_specs=(P("gx", "gy", None),) * 2,
        check_vma=False,
    )
```

```python
import jax
import jax.numpy as jnp
from jax import lax
from jax.experimental import pallas as pl
from jax.experimental.pallas import tpu as pltpu
from jax.sharding import PartitionSpec as P

BOTTOM = 6
RELAX_WEIGHT = 0.8
TINY = 1e-30
F32 = jnp.float32
VMEM = pl.BlockSpec(memory_space=pltpu.VMEM)
HBM = pl.BlockSpec(memory_space=pltpu.HBM)


def call(kernel, out_shapes, scratch=(), n_in=0, copies=0, in_hbm=0, out_hbm=0, limit=24 * 1024 * 1024):
    semaphores = [pltpu.SemaphoreType.DMA((copies,))] if copies else []
    return pl.pallas_call(
        kernel,
        out_shape=[jax.ShapeDtypeStruct(s, F32) for s in out_shapes],
        in_specs=[HBM] * in_hbm + [VMEM] * (n_in - in_hbm),
        out_specs=[HBM] * out_hbm + [VMEM] * (len(out_shapes) - out_hbm),
        scratch_shapes=[pltpu.VMEM(s, F32) for s in scratch] + semaphores,
        compiler_params=pltpu.CompilerParams(vmem_limit_bytes=limit),
    )


def harmonic(a, b):
    return 2.0 * a * b / jnp.maximum(a + b, TINY)


def along(v, axis, step):
    n = v.shape[axis]
    return pltpu.roll(v, (-step) % n, axis)


def is_first():
    return lax.rem(lax.axis_index("gx"), 2) == 0


def positions(shape, axis):
    return lax.broadcasted_iota(jnp.int32, shape, axis)


def halving(rows, cols):
    return (positions((rows, cols), 0) // 2 == positions((rows, cols), 1)).astype(F32)


def doubling(rows, cols, factor):
    return (positions((rows, cols), 1) // factor == positions((rows, cols), 0)).astype(F32)


def matmul(a, b):
    return jnp.dot(a, b, precision=lax.Precision.HIGHEST, preferred_element_type=F32)


def weight(face, centre):
    return jnp.where(face > 0.0, face, centre)


def diagonal_of(c, xp, xm, hy, hz):
    return (weight(xp, c) + weight(xm, c) + weight(hy, c) + weight(along(hy, 0, -1), c)
            + weight(hz, c) + weight(along(hz, 1, -1), c))


def operate(d, v, xp, vp, xm, vm, hy, hz):
    out = d * v - xp * vp - xm * vm
    out = out - hy * along(v, 0, 1) - along(hy * v, 0, -1)
    return out - hz * along(v, 1, 1) - along(hz * v, 1, -1)


def z_face(c):
    nxt = jnp.where(positions(c.shape, 1) < c.shape[1] - 1, along(c, 1, 1), 0.0)
    return harmonic(c, nxt)


NP, NR, NC = 7, 6, 7
NROWS = NP + NR + NC


def pack_y(phi_in, rhs_in, coef_in, up_out, dn_out, phi, rhs, coef, stage, up, dn, sem):
    loads = [pltpu.make_async_copy(src, dst, sem.at[a])
             for a, (src, dst) in enumerate(((phi_in, phi), (rhs_in, rhs), (coef_in, coef)))]
    for load in loads:
        load.start()
    stores = []
    k = 0
    for a, (ref, n) in enumerate(((phi, NP), (rhs, NR), (coef, NC))):
        loads[a].wait()
        for q in range(4):
            lanes = slice(128 * q, 128 * q + 128)
            base = 64 * (4 * a + q)
            stage[base:base + 64, :] = ref[:, lanes]
            for j in range(n):
                rows = slice(8 * (k + j), 8 * (k + j) + 8)
                up[rows, lanes] = stage[pl.ds(base + 8 - n + j, 8, stride=8), :]
                dn[rows, lanes] = stage[pl.ds(base + j, 8, stride=8), :]
        for b, (src, dst) in enumerate(((up, up_out), (dn, dn_out))):
            part = pl.ds(8 * k, 8 * n)
            stores.append(pltpu.make_async_copy(src.at[part], dst.at[part], sem.at[3 + 2 * a + b]))
            stores[-1].start()
        k += n
    for store in stores:
        store.wait()


def pack_x(phi, rhs, coef, lo, hi, pe, re, ce, mate, other, stage):
    zero = jnp.zeros((8, 128), F32)
    k = 0
    for a, (ref, ext, n) in enumerate(((phi, pe, NP), (rhs, re, NR), (coef, ce, NC))):
        for x in range(8):
            ext[24 * x:24 * x + 8, :] = ref[8 * x:8 * x + 8, :]
        for q in range(4):
            lanes = slice(128 * q, 128 * q + 128)
            base = 128 * (4 * a + q)
            for j in range(n):
                rows = slice(8 * (k + j), 8 * (k + j) + 8)
                stage[pl.ds(base + j, 8, stride=16), :] = hi[rows, lanes]
                stage[pl.ds(base + 16 - n + j, 8, stride=16), :] = lo[rows, lanes]
            for j in range(n, 16 - n):
                stage[pl.ds(base + j, 8, stride=16), :] = zero
            for x in range(8):
                ext[24 * x + 8:24 * x + 24, lanes] = stage[base + 16 * x:base + 16 * x + 16, :]
        k += n
    first = is_first()
    for ref, end in ((mate, first), (other, jnp.logical_not(first))):
        three = pl.multiple_of(jnp.where(end, 120, 0), 8)
        two = pl.multiple_of(jnp.where(end, 144, 0), 8)
        ref[0:72, :] = pe[pl.ds(three, 72), :]
        ref[72:120, :] = re[pl.ds(two, 48), :]
        ref[120:192, :] = ce[pl.ds(three, 72), :]


def fine(pe, re, ce, other, mate, phi_out, smid, cmid, mmate, mother,
         p0, rs, c, hx, hy, hz, dg, rd, p1, p2, sums, packed, own, left):
    first = is_first()
    p0[3:11] = pe[...]
    rs[3:11] = re[...]
    c[3:11] = ce[...]
    for ref, end in ((mate, first), (other, jnp.logical_not(first))):
        three = jnp.where(end, 11, 0)
        p0[pl.ds(three, 3)] = ref[0:3]
        rs[pl.ds(jnp.where(end, 11, 1), 2)] = ref[3:5]
        c[pl.ds(three, 3)] = ref[5:8]
    hx[0] = harmonic(c[0], c[1])

    def start(i, carry):
        ci = c[i]
        xp, xm = harmonic(ci, c[i + 1]), hx[i - 1]
        hyi = harmonic(ci, along(ci, 0, 1))
        hzi = z_face(ci)
        d = diagonal_of(ci, xp, xm, hyi, hzi)
        r = RELAX_WEIGHT / jnp.maximum(d, TINY)
        hx[i], hy[i], hz[i], dg[i], rd[i] = xp, hyi, hzi, d, r
        v = p0[i]
        p1[i] = v + (rs[i] - operate(d, v, xp, p0[i + 1], xm, p0[i - 1], hyi, hzi)) * r
        return carry

    lax.fori_loop(1, 13, start, 0)

    def second(i, carry):
        v = p1[i]
        image = operate(dg[i], v, hx[i], p1[i + 1], hx[i - 1], p1[i - 1], hy[i], hz[i])
        p2[i] = v + (rs[i] - image) * rd[i]
        return carry

    lax.fori_loop(2, 12, second, 0)
    for x in range(8):
        own[x] = p2[3 + x, 0:8, :]
    store = pltpu.make_async_copy(own, phi_out, left.at[0])
    store.start()

    def residual(i):
        return rs[i] - operate(dg[i], p2[i], hx[i], p2[i + 1], hx[i - 1], p2[i - 1], hy[i], hz[i])

    def pairs(k, carry):
        i = 3 + 2 * k
        s = residual(i) + residual(i + 1)
        t = c[i] + c[i + 1]
        s = (s + along(s, 0, 1)) * 0.5
        t = (t + along(t, 0, 1)) * 0.125
        for q in range(4):
            sums[q, k] = s[:, 128 * q:128 * q + 128]
            sums[q, 4 + k] = t[:, 128 * q:128 * q + 128]
        return carry

    lax.fori_loop(0, 4, pairs, 0)
    for k in range(8):
        for q in range(4):
            lanes = slice(128 * q, 128 * q + 128)
            packed[16 * k:16 * k + 8, lanes] = sums[q, k, pl.ds(0, 8, stride=2), :]
            packed[16 * k + 8:16 * k + 12, lanes] = jnp.zeros((4, 128), F32)
            packed[16 * k + 12:16 * k + 16, lanes] = sums[q, k, pl.ds(16, 4, stride=2), :]
    mid = matmul(packed[...], halving(512, 256)).reshape(8, 16, 256)
    smid[...] = mid[0:4]
    cmid[...] = mid[4:8]
    mmate[0:2] = jnp.where(first, mid[2:4], mid[0:2])
    mmate[2:6] = mid[4:8]
    mother[0:2] = jnp.where(first, mid[0:2], mid[2:4])
    mother[2:6] = mid[4:8]
    store.wait()


def middle(smid, cmid, other, mate, emid, out, sums):
    first = is_first()
    hi = [jnp.where(first, mate[j], other[j]) for j in range(6)]
    lo = [jnp.where(first, other[j], mate[j]) for j in range(6)]
    s = [lo[0], lo[1]] + [smid[x] for x in range(4)] + [hi[0], hi[1]]
    c = [lo[2 + x] for x in range(4)] + [cmid[x] for x in range(4)] + [hi[2 + x] for x in range(4)]
    hx = [harmonic(c[j], c[j + 1]) for j in range(1, 10)]
    hy, hz, d, r, e1 = [], [], [], [], []
    for i in range(8):
        ci = c[i + 2]
        hy.append(harmonic(ci, along(ci, 0, 1)))
        hz.append(z_face(ci))
        d.append(diagonal_of(ci, hx[i + 1], hx[i], hy[i], hz[i]))
        r.append(RELAX_WEIGHT / jnp.maximum(d[i], TINY))
        e1.append(s[i] * r[i])

    def image(i, e):
        return operate(d[i], e[i], hx[i + 1], e[i + 1], hx[i], e[i - 1], hy[i], hz[i])

    e2 = [None] + [e1[i] + (s[i] - image(i, e1)) * r[i] for i in range(1, 7)] + [None]
    res = [s[i] - image(i, e2) for i in range(2, 6)]
    for x in range(4):
        emid[x] = e2[2 + x][0:4, :]
    groups = [(res[2 * x] + res[2 * x + 1]) * 0.5 for x in range(2)]
    groups += [(c[2 * x] + c[2 * x + 1]) * 0.125 for x in range(6)]
    for g in range(8):
        both = (groups[g] + along(groups[g], 0, 1))[0:8, :]
        sums[8 * g:8 * g + 8, :] = both[:, 0:128]
        sums[64 + 8 * g:72 + 8 * g, :] = both[:, 128:256]

    def rows(y):
        return jnp.concatenate([sums[pl.ds(64 * q + 2 * y, 8, stride=8), :] for q in range(2)], axis=1)

    low0 = matmul(rows(0), halving(256, 128))
    low1 = matmul(rows(1), halving(256, 128))
    for n in range(16):
        out[n, 0:8, :] = low0
        out[n, 8:16, :] = low1


def y_face(c):
    n = c.shape[0]
    return harmonic(c, jnp.where(positions(c.shape, 0) < n - 1, along(c, 0, 1), 0.0))


def columns(gathered, sd, ccol):
    for g in range(8):
        for y in range(2):
            rows = gathered[pl.ds(8 * y + g, 16, stride=16), :]
            if g < 2:
                sd[pl.ds(32 * g + y, 16, stride=2), :] = rows
            else:
                ccol[pl.ds(32 * (g - 2) + y, 16, stride=2), :] = rows
    c = [ccol[32 * j:32 * j + 32, :] for j in range(6)]
    hx = [harmonic(c[j], c[j + 1]) for j in range(1, 4)]
    for x in range(2):
        ci = c[2 + x]
        sd[64 + 32 * x:96 + 32 * x, :] = diagonal_of(ci, hx[x + 1], hx[x], y_face(ci), z_face(ci))


def low(sd, ccol, mate, other, elow, out, sums):
    first = is_first()
    hi = jnp.where(first, mate[...], other[...])
    lo = jnp.where(first, other[...], mate[...])

    def part(ref, k):
        return ref[32 * k:32 * k + 32, :]

    s = [part(ref, k) for ref in (lo, sd, hi) for k in (0, 1)]
    d = [part(ref, k) for ref in (lo, sd, hi) for k in (2, 3)]
    c = [part(ccol, k) for k in range(6)]
    hx = [harmonic(c[j], c[j + 1]) for j in range(5)]
    hy = [y_face(ci) for ci in c]
    hz = [z_face(ci) for ci in c]
    r = [RELAX_WEIGHT / jnp.maximum(di, TINY) for di in d]
    e1 = [s[i] * r[i] for i in range(6)]

    def image(i, e):
        return operate(d[i], e[i], hx[i], e[i + 1], hx[i - 1], e[i - 1], hy[i], hz[i])

    e2 = [None] + [e1[i] + (s[i] - image(i, e1)) * r[i] for i in range(1, 5)] + [None]
    res = [s[i] - image(i, e2) for i in range(2, 4)]
    for x in range(2):
        elow[32 * x:32 * x + 32, :] = e2[2 + x]
    a = (res[0] + res[1]) * 0.5
    b = (c[2] + c[3]) * 0.125
    sums[0:32, :] = a + along(a, 0, 1)
    sums[32:64, :] = b + along(b, 0, 1)
    ra = sums[pl.ds(0, 16, stride=2), :]
    rb = sums[pl.ds(32, 16, stride=2), :]
    both = matmul(jnp.concatenate([ra, rb], axis=1), halving(256, 128))
    for n in range(32):
        out[n] = both


def bottom(gathered, elow, emid, out, hx, hy, hz, dg, sol, res, dire, img):
    half = positions((16, 128), 1) < 64
    last_z = positions((16, 128), 1) % 64 == 63
    last_y = positions((16, 128), 0) == 15
    c = []
    for x in range(16):
        a, b = gathered[x], gathered[x + 16]
        source = jnp.where(half, a, along(b, 1, 64))
        c.append(jnp.where(half, along(a, 1, 64), b))
        res[x] = source
        dire[x] = source
        sol[x] = jnp.zeros((16, 128), F32)
    for x in range(16):
        nxt = c[x + 1] if x < 15 else jnp.where(half, along(c[0], 1, 64), 0.0)
        hx[x + 1] = harmonic(c[x], nxt)
    hx[0] = along(hx[16], 1, 64)
    for x in range(16):
        hy[x] = harmonic(c[x], jnp.where(last_y, 0.0, along(c[x], 0, 1)))
        hz[x] = harmonic(c[x], jnp.where(last_z, 0.0, along(c[x], 1, 1)))
        dg[x] = diagonal_of(c[x], hx[x + 1], hx[x], hy[x], hz[x])

    def total(acc):
        return jnp.sum(acc, axis=(0, 1), keepdims=True)

    def dot_image():
        acc = jnp.zeros((16, 128), F32)
        for x in range(16):
            v = dire[x]
            vp = dire[x + 1] if x < 15 else along(dire[0], 1, 64)
            vm = dire[x - 1] if x > 0 else along(dire[15], 1, 64)
            image = operate(dg[x], v, hx[x + 1], vp, hx[x], vm, hy[x], hz[x])
            img[x] = image
            acc = acc + v * image
        return total(acc)

    def norm():
        acc = jnp.zeros((16, 128), F32)
        for x in range(16):
            acc = acc + res[x] * res[x]
        return total(acc)

    def step(_, rr):
        alpha = rr / dot_image()
        acc = jnp.zeros((16, 128), F32)
        for x in range(16):
            sol[x] = sol[x] + alpha * dire[x]
            rx = res[x] - alpha * img[x]
            res[x] = rx
            acc = acc + rx * rx
        new = total(acc)
        beta = new / rr
        for x in range(16):
            dire[x] = res[x] + beta * dire[x]
        return new

    rr = lax.fori_loop(0, BOTTOM - 1, step, norm())
    gx, gy = lax.axis_index("gx"), lax.axis_index("gy")
    xi = lax.rem(gx, 16)
    alpha = rr / dot_image()
    mine = sol[xi] + alpha * dire[xi]
    mine = jnp.where(gx >= 16, along(mine, 1, 64), mine)
    row = positions((16, 128), 0)
    mine = jnp.sum(jnp.where(row == gy, mine, 0.0), axis=0, keepdims=True)
    row = positions((32, 128), 0)
    lows = []
    for x in range(2):
        e = elow[32 * x:32 * x + 32, :]
        for y in range(2):
            lows.append(jnp.sum(jnp.where(row == 2 * gy + y, e, 0.0), axis=0, keepdims=True))
    coarse = matmul(jnp.broadcast_to(mine, (8, 128)), doubling(128, 256, 4))
    finer = matmul(jnp.concatenate(lows + lows, axis=0), doubling(128, 256, 2))
    for x in range(4):
        k = 2 * (x // 2)
        for y in range(4):
            add = finer[k + y // 2:k + y // 2 + 1, :] + coarse[0:1, :]
            out[x, y:y + 1, :] = emid[x, y:y + 1, :] + add


def neighbours(up, dn, axis):
    n = lax.axis_size(axis)
    forth = [(i, i + 1) for i in range(n - 1)]
    back = [(i + 1, i) for i in range(n - 1)]
    return lax.ppermute(up, axis, forth), lax.ppermute(dn, axis, back)


def neighbours_x(mate, other):
    n = lax.axis_size("gx")
    far = [(i, i + 1) for i in range(1, n - 1, 2)] + [(i + 1, i) for i in range(1, n - 1, 2)]
    other = lax.ppermute(other, "gx", far)
    return lax.ppermute(mate, "gx", [(i, i ^ 1) for i in range(n)]), other


def shards(phi_start, right_side, coefficient):
    own = [a.reshape(64, 512) for a in (phi_start, right_side, coefficient)]
    up, dn = call(
        pack_y, [(8 * NROWS, 512)] * 2, [(64, 512)] * 3 + [(768, 128)] + [(8 * NROWS, 512)] * 2,
        n_in=3, copies=9, in_hbm=3, out_hbm=2, limit=64000000)(*own)
    lo, hi = neighbours(up, dn, "gy")
    *ext, mate, other = call(pack_x, [(192, 512)] * 5, [(1536, 128)], n_in=5)(*own, lo, hi)
    mate, other = neighbours_x(mate, other)
    box = (14, 24, 512)
    phi_fine, smid, cmid, mate, other = call(
        fine,
        [(8, 8, 512), (4, 16, 256), (4, 16, 256), (6, 16, 256), (6, 16, 256)],
        [box] * 10 + [(4, 8, 24, 128), (128, 512), (8, 8, 512)],
        n_in=5, copies=1, out_hbm=1,
    )(*[a.reshape(8, 24, 512) for a in (*ext, other, mate)])
    mate, other = neighbours_x(mate, other)
    emid, spread = call(middle, [(4, 4, 256), (16, 16, 128)], [(128, 128)], n_in=4)(smid, cmid, other, mate)
    gathered = lax.all_to_all(spread, "gy", 0, 0, tiled=True)
    sd, ccol = call(columns, [(128, 128), (192, 128)], n_in=1)(gathered.reshape(256, 128))
    mate, other = neighbours_x(sd, sd)
    elow, spread = call(low, [(64, 128), (32, 16, 128)], [(64, 128)], n_in=4)(sd, ccol, mate, other)
    gathered = lax.all_to_all(spread, "gx", 0, 0, tiled=True)
    (correction,) = call(bottom, [(4, 4, 256)], [(17, 16, 128)] + [(16, 16, 128)] * 7, n_in=3)(
        gathered, elow, emid)
    return phi_fine, correction


def solution(mesh):
    return jax.shard_map(
        shards,
        mesh=mesh,
        in_specs=(P("gx", "gy", None),) * 3,
        out_specs=(P("gx", "gy", None),) * 2,
        check_vma=False,
    )
```

```python
import jax
import jax.numpy as jnp
from jax import lax
from jax.experimental import pallas as pl
from jax.experimental.pallas import tpu as pltpu
from jax.sharding import PartitionSpec as P

BOTTOM = 6
RELAX_WEIGHT = 0.8
FLOOR = 1e-3
F32 = jnp.float32
VMEM = pl.BlockSpec(memory_space=pltpu.VMEM)
HBM = pl.BlockSpec(memory_space=pltpu.HBM)


def call(kernel, out_shapes, scratch=(), n_in=0, copies=0, in_hbm=0, out_hbm=0, limit=24 * 1024 * 1024, cost=None):
    semaphores = [pltpu.SemaphoreType.DMA((copies,))] if copies else []
    return pl.pallas_call(
        kernel,
        out_shape=[jax.ShapeDtypeStruct(s, F32) for s in out_shapes],
        in_specs=[HBM] * in_hbm + [VMEM] * (n_in - in_hbm),
        out_specs=[HBM] * out_hbm + [VMEM] * (len(out_shapes) - out_hbm),
        scratch_shapes=[pltpu.VMEM(s, F32) for s in scratch] + semaphores,
        compiler_params=pltpu.CompilerParams(vmem_limit_bytes=limit),
        cost_estimate=cost,
    )


def harmonic(a, b):
    return 2.0 * a * b / jnp.maximum(a + b, FLOOR)


def along(v, axis, step):
    n = v.shape[axis]
    return pltpu.roll(v, (-step) % n, axis)


def is_first():
    return lax.rem(lax.axis_index("gx"), 2) == 0


def positions(shape, axis):
    return lax.broadcasted_iota(jnp.int32, shape, axis)


def halving(rows, cols):
    return (positions((rows, cols), 0) // 2 == positions((rows, cols), 1)).astype(F32)


def doubling(rows, cols, factor):
    return (positions((rows, cols), 1) // factor == positions((rows, cols), 0)).astype(F32)


def matmul(a, b):
    return jnp.dot(a, b, precision=lax.Precision.HIGHEST, preferred_element_type=F32)


def weight(face, centre):
    return jnp.where(face > 0.0, face, centre)


def diagonal_of(c, xp, xm, hy, hz):
    return (weight(xp, c) + weight(xm, c) + weight(hy, c) + weight(along(hy, 0, -1), c)
            + weight(hz, c) + weight(along(hz, 1, -1), c))


def operate(d, v, xp, vp, xm, vm, hy, hz):
    out = d * v - xp * vp - xm * vm
    out = out - hy * along(v, 0, 1) - along(hy * v, 0, -1)
    return out - hz * along(v, 1, 1) - along(hz * v, 1, -1)


def z_face(c):
    nxt = jnp.where(positions(c.shape, 1) < c.shape[1] - 1, along(c, 1, 1), 0.0)
    return harmonic(c, nxt)


NP, NR, NC = 7, 6, 7
NROWS = NP + NR + NC
PHI_TILES = (3, 3, 2, 2, 2, 2, 1)
RHS_TILES = (3, 2, 2, 2, 2, 1)
END_ROWS = 8 * (2 * sum(PHI_TILES) + sum(RHS_TILES))


def pack_y(phi_in, rhs_in, coef_in, near, far, phi, rhs, coef, stage, ends, sem):
    loads = [pltpu.make_async_copy(src, dst, sem.at[a])
             for a, (src, dst) in enumerate(((phi_in, phi), (rhs_in, rhs), (coef_in, coef)))]
    for load in loads:
        load.start()
    stores = []
    k = 0
    for a, (ref, n) in enumerate(((phi, NP), (rhs, NR), (coef, NC))):
        loads[a].wait()
        for q in range(4):
            lanes = slice(128 * q, 128 * q + 128)
            base = 64 * (4 * a + q)
            stage[base:base + 64, :] = ref[:, lanes]
            for j in range(n):
                rows = slice(8 * (k + j), 8 * (k + j) + 8)
                ends[0, rows, lanes] = stage[pl.ds(base + 8 - n + j, 8, stride=8), :]
                ends[1, rows, lanes] = stage[pl.ds(base + j, 8, stride=8), :]
        for b, dst in enumerate((near, far)):
            part = pl.ds(8 * k, 8 * n)
            src = ends.at[lax.rem(lax.axis_index("gy") + b, 2), part]
            stores.append(pltpu.make_async_copy(src, dst.at[part], sem.at[3 + 2 * a + b]))
            stores[-1].start()
        k += n
    for store in stores:
        store.wait()


def pack_x(phi, rhs, coef, far, near, pe, re, ce, mate, other, stage):
    zero = jnp.zeros((8, 128), F32)
    odd = lax.rem(lax.axis_index("gy"), 2)
    k = 0
    for a, (ref, ext, n) in enumerate(((phi, pe, NP), (rhs, re, NR), (coef, ce, NC))):
        for x in range(8):
            ext[24 * x:24 * x + 8, :] = ref[8 * x:8 * x + 8, :]
        for q in range(4):
            lanes = slice(128 * q, 128 * q + 128)
            base = 128 * (4 * a + q)
            for j in range(n):
                rows = slice(8 * (k + j), 8 * (k + j) + 8)
                stage[pl.ds(base + j + odd * (16 - n), 8, stride=16), :] = near[rows, lanes]
                stage[pl.ds(base + j + (1 - odd) * (16 - n), 8, stride=16), :] = far[rows, lanes]
            for j in range(n, 16 - n):
                stage[pl.ds(base + j, 8, stride=16), :] = zero
            for x in range(8):
                ext[24 * x + 8:24 * x + 24, lanes] = stage[base + 16 * x:base + 16 * x + 16, :]
        k += n
    first = is_first()
    top = positions((8, 512), 0) < 4
    for ref, end in ((mate, first), (other, jnp.logical_not(first))):
        row = 0
        for ext, tiles in ((pe, PHI_TILES), (re, RHS_TILES), (ce, PHI_TILES)):
            for k, n in enumerate(tiles):
                at = 24 * jnp.where(end, 7 - k, k)
                parts = [ext[pl.ds(pl.multiple_of(at + 8 * t, 8), 8), :] for t in range(min(n + n // 2, 3))]
                if n == 2:
                    parts = [parts[0], jnp.where(top, parts[1], parts[2])]
                for part in parts:
                    ref[row:row + 8, :] = part
                    row += 8


def slab_x(side, t):
    return jnp.where(side == 0, 3 - t, 4 + t)


def first_weights(c, xp, xm):
    hy = harmonic(c, along(c, 0, 1))
    hz = z_face(c)
    d = weight(xm, c) + weight(hy, c) + weight(along(hy, 0, -1), c) + weight(hz, c) + weight(along(hz, 1, -1), c)
    return hy, hz, d if xp is None else d + weight(xp, c)


def inverse(d):
    return RELAX_WEIGHT / jnp.maximum(d, FLOOR)


def pair_sums(sums, place, a, b, scale):
    t = a + b
    t = (t + along(t, 0, 1)) * scale
    for q in range(4):
        sums[q, place] = t[:, 128 * q:128 * q + 128]


def halve_fine(sums, packed, n):
    for k in range(n):
        for q in range(4):
            lanes = slice(128 * q, 128 * q + 128)
            packed[16 * k:16 * k + 8, lanes] = sums[q, k, pl.ds(0, 8, stride=2), :]
            packed[16 * k + 8:16 * k + 12, lanes] = jnp.zeros((4, 128), F32)
            packed[16 * k + 12:16 * k + 16, lanes] = sums[q, k, pl.ds(16, 4, stride=2), :]
    return matmul(packed[...], halving(512, 256)).reshape(n, 16, 256)


def inner(pe, re, ce, hx, hc, hy, hz, dg, rd, p1, p2, res, cmid, sums, packed):
    hc[0] = harmonic(ce[3], ce[4])

    def start(side, carry):
        for t in range(4):
            x = slab_x(side, t)
            c = ce[x]
            xm = hc[0] if t == 0 else hx[side, t - 1]
            xp = None
            if t < 3:
                xp = harmonic(c, ce[slab_x(side, t + 1)])
                hx[side, t] = xp
            hyt, hzt, d = first_weights(c, xp, xm)
            hy[side, t], hz[side, t], dg[side, t] = hyt, hzt, d
            if t < 3:
                r = inverse(d)
                rd[side, t] = r
                v = pe[x]
                image = operate(d, v, xp, pe[slab_x(side, t + 1)], xm, pe[slab_x(side, t - 1)], hyt, hzt)
                p1[side, t] = v + (re[x] - image) * r
        for q in range(2):
            pair_sums(sums, jnp.where(side == 0, 1 - q, 2 + q),
                      ce[slab_x(side, 2 * q)], ce[slab_x(side, 2 * q + 1)], 0.125)
        return carry

    lax.fori_loop(0, 2, start, 0)

    def image(side, t, p):
        xm, pm = (hc[0], p[1 - side, 0]) if t == 0 else (hx[side, t - 1], p[side, t - 1])
        return operate(dg[side, t], p[side, t], hx[side, t], p[side, t + 1], xm, pm, hy[side, t], hz[side, t])

    def second(side, carry):
        for t in range(2):
            p2[side, t] = p1[side, t] + (re[slab_x(side, t)] - image(side, t, p1)) * rd[side, t]
        return carry

    lax.fori_loop(0, 2, second, 0)

    def third(side, carry):
        res[side] = re[slab_x(side, 0)] - image(side, 0, p2)
        return carry

    lax.fori_loop(0, 2, third, 0)
    cmid[...] = halve_fine(sums, packed, 4)


def unpack(ref, p0, rs, c, side):
    row = 0
    for dst, tiles in ((p0, PHI_TILES), (rs, RHS_TILES), (c, PHI_TILES)):
        for k, n in enumerate(tiles):
            parts = [ref[row + 8 * t:row + 8 * t + 8, :] for t in range(n)]
            row += 8 * n
            if n == 1:
                parts += [jnp.zeros((8, 512), F32)] * 2
            if n == 2:
                parts += [parts[1]]
            for t in range(3):
                dst[side, k + 1, 8 * t:8 * t + 8, :] = parts[t]


def outer(pe, re, ce, hx, hc, hy, hz, dg, rd, p1, p2, res, other, mate, phi_out, smid, chalo,
          p0h, rsh, ch, hxh, hyh, hzh, dgh, rdh, p1h, p2h, resh, own, sums, packed, left):
    first = is_first()
    near = jnp.where(first, 1, 0)
    unpack(mate, p0h, rsh, ch, near)
    unpack(other, p0h, rsh, ch, 1 - near)

    def sweeps(side, carry):
        x0 = slab_x(side, 3)
        p0h[side, 0], rsh[side, 0], ch[side, 0] = pe[x0], re[x0], ce[x0]
        c = ch[side, 0]
        xp = harmonic(c, ch[side, 1])
        d = dg[side, 3] + weight(xp, c)
        r = inverse(d)
        hxh[side, 0], hyh[side, 0], hzh[side, 0], dgh[side, 0], rdh[side, 0] = xp, hy[side, 3], hz[side, 3], d, r
        v = p0h[side, 0]
        image = operate(d, v, xp, p0h[side, 1], hx[side, 2], pe[slab_x(side, 2)], hy[side, 3], hz[side, 3])
        p1h[side, 0] = v + (rsh[side, 0] - image) * r

        def start(j, carry):
            c = ch[side, j]
            xp, xm = harmonic(c, ch[side, j + 1]), hxh[side, j - 1]
            hyj, hzj, d = first_weights(c, xp, xm)
            r = inverse(d)
            hxh[side, j], hyh[side, j], hzh[side, j], dgh[side, j], rdh[side, j] = xp, hyj, hzj, d, r
            v = p0h[side, j]
            image = operate(d, v, xp, p0h[side, j + 1], xm, p0h[side, j - 1], hyj, hzj)
            p1h[side, j] = v + (rsh[side, j] - image) * r
            return carry

        lax.fori_loop(1, 7, start, 0)

        image = operate(dg[side, 2], p1[side, 2], hx[side, 2], p1h[side, 0], hx[side, 1], p1[side, 1],
                        hy[side, 2], hz[side, 2])
        p2h[side, 1] = p1[side, 2] + (re[slab_x(side, 2)] - image) * rd[side, 2]
        p2h[side, 0] = p2[side, 1]
        image = operate(dgh[side, 0], p1h[side, 0], hxh[side, 0], p1h[side, 1], hx[side, 2], p1[side, 2],
                        hyh[side, 0], hzh[side, 0])
        p2h[side, 2] = p1h[side, 0] + (rsh[side, 0] - image) * rdh[side, 0]

        def second(j, carry):
            v = p1h[side, j]
            image = operate(dgh[side, j], v, hxh[side, j], p1h[side, j + 1], hxh[side, j - 1], p1h[side, j - 1],
                            hyh[side, j], hzh[side, j])
            p2h[side, j + 2] = v + (rsh[side, j] - image) * rdh[side, j]
            return carry

        lax.fori_loop(1, 6, second, 0)
        for t in range(4):
            own[slab_x(side, t)] = (p2[side, t] if t < 2 else p2h[side, t - 1])[0:8, :]

        for t in (1, 2):
            image = operate(dg[side, t], p2h[side, t - 1], hx[side, t], p2h[side, t], hx[side, t - 1],
                            p2[side, 0] if t == 1 else p2h[side, 0], hy[side, t], hz[side, t])
            resh[side, t - 1] = re[slab_x(side, t)] - image
        image = operate(dgh[side, 0], p2h[side, 2], hxh[side, 0], p2h[side, 3], hx[side, 2], p2h[side, 1],
                        hyh[side, 0], hzh[side, 0])
        resh[side, 2] = rsh[side, 0] - image

        def third(j, carry):
            image = operate(dgh[side, j], p2h[side, j + 2], hxh[side, j], p2h[side, j + 3], hxh[side, j - 1],
                            p2h[side, j + 1], hyh[side, j], hzh[side, j])
            resh[side, j + 2] = rsh[side, j] - image
            return carry

        lax.fori_loop(1, 5, third, 0)
        for q in range(4):
            a = res[side] if q == 0 else resh[side, 2 * q - 1]
            pair_sums(sums, jnp.where(side == 0, 3 - q, 4 + q), a, resh[side, 2 * q], 0.5)
        for q in range(3):
            pair_sums(sums, 8 + jnp.where(side == 0, 2 - q, 3 + q), ch[side, 2 * q + 1], ch[side, 2 * q + 2], 0.125)
        return carry

    lax.fori_loop(0, 2, sweeps, 0)
    store = pltpu.make_async_copy(own, phi_out, left.at[0])
    store.start()
    mid = halve_fine(sums, packed, 14)
    smid[...] = mid[0:8]
    chalo[...] = mid[8:14]
    store.wait()


def middle(smid, cmid, chalo, emid, out, sums):
    s = [smid[j] for j in range(8)]
    c = [chalo[j] for j in range(3)] + [cmid[j] for j in range(4)] + [chalo[j] for j in range(3, 6)]
    hx = [harmonic(c[j], c[j + 1]) for j in range(9)]
    hy, hz, d, r, e1 = [], [], [], [], []
    for i in range(8):
        ci = c[i + 1]
        hy.append(harmonic(ci, along(ci, 0, 1)))
        hz.append(z_face(ci))
        d.append(diagonal_of(ci, hx[i + 1], hx[i], hy[i], hz[i]))
        r.append(RELAX_WEIGHT / jnp.maximum(d[i], FLOOR))
        e1.append(s[i] * r[i])

    def image(i, e):
        return operate(d[i], e[i], hx[i + 1], e[i + 1], hx[i], e[i - 1], hy[i], hz[i])

    e2 = [None] + [e1[i] + (s[i] - image(i, e1)) * r[i] for i in range(1, 7)] + [None]
    res = [s[i] - image(i, e2) for i in range(2, 6)]
    for x in range(4):
        emid[x] = e2[2 + x][0:4, :]
    groups = [(res[2 * x] + res[2 * x + 1]) * 0.5 for x in range(2)]
    groups += [(c[2 * x + 1] + c[2 * x + 2]) * 0.125 for x in range(4)]
    groups += groups[0:2]
    for g in range(8):
        both = (groups[g] + along(groups[g], 0, 1))[0:8, :]
        sums[8 * g:8 * g + 8, :] = both[:, 0:128]
        sums[64 + 8 * g:72 + 8 * g, :] = both[:, 128:256]

    def rows(y):
        return jnp.concatenate([sums[pl.ds(64 * q + 2 * y, 8, stride=8), :] for q in range(2)], axis=1)

    low0 = matmul(rows(0), halving(256, 128))
    low1 = matmul(rows(1), halving(256, 128))
    for n in range(16):
        out[n, 0:8, :] = low0
        out[n, 8:16, :] = low1


def y_face(c):
    n = c.shape[0]
    return harmonic(c, jnp.where(positions(c.shape, 0) < n - 1, along(c, 0, 1), 0.0))


def columns(gathered, sdc, ccol):
    for g in range(6):
        for y in range(2):
            rows = gathered[pl.ds(8 * y + g, 16, stride=16), :]
            ref, k = (sdc, g) if g < 2 else (ccol, g - 2)
            ref[pl.ds(32 * k + y, 16, stride=2), :] = rows
    c = [ccol[32 * j:32 * j + 32, :] for j in range(4)]
    hx = [harmonic(c[j], c[j + 1]) for j in range(3)]
    for x in range(2):
        ci = c[1 + x]
        sdc[64 + 32 * x:96 + 32 * x, :] = diagonal_of(ci, hx[x + 1], hx[x], y_face(ci), z_face(ci))
        sdc[128 + 32 * x:160 + 32 * x, :] = ci


def low(sdc, mate, other, elow, out, sums):
    first = is_first()
    hi = jnp.where(first, mate[...], other[...])
    lo = jnp.where(first, other[...], mate[...])

    def part(ref, k):
        return ref[32 * k:32 * k + 32, :]

    s, d, c = ([part(ref, k + j) for ref in (lo, sdc, hi) for j in (0, 1)] for k in (0, 2, 4))
    hx = [harmonic(c[j], c[j + 1]) for j in range(5)]
    hy = [y_face(ci) for ci in c]
    hz = [z_face(ci) for ci in c]
    r = [RELAX_WEIGHT / jnp.maximum(di, FLOOR) for di in d]
    e1 = [s[i] * r[i] for i in range(6)]

    def image(i, e):
        return operate(d[i], e[i], hx[i], e[i + 1], hx[i - 1], e[i - 1], hy[i], hz[i])

    e2 = [None] + [e1[i] + (s[i] - image(i, e1)) * r[i] for i in range(1, 5)] + [None]
    res = [s[i] - image(i, e2) for i in range(2, 4)]
    for x in range(2):
        elow[32 * x:32 * x + 32, :] = e2[2 + x]
    a = (res[0] + res[1]) * 0.5
    b = (c[2] + c[3]) * 0.125
    sums[0:32, :] = a + along(a, 0, 1)
    sums[32:64, :] = b + along(b, 0, 1)
    ra = sums[pl.ds(0, 16, stride=2), :]
    rb = sums[pl.ds(32, 16, stride=2), :]
    both = matmul(jnp.concatenate([ra, rb], axis=1), halving(256, 128))
    for n in range(32):
        out[n] = both


def bottom(gathered, elow, emid, out, hx, hy, hz, dg, sol, res, dire, img):
    half = positions((16, 128), 1) < 64
    last_z = positions((16, 128), 1) % 64 == 63
    last_y = positions((16, 128), 0) == 15
    c = []
    for x in range(16):
        a, b = gathered[x], gathered[x + 16]
        source = jnp.where(half, a, along(b, 1, 64))
        c.append(jnp.where(half, along(a, 1, 64), b))
        res[x] = source
        dire[x] = source
        sol[x] = jnp.zeros((16, 128), F32)
    for x in range(16):
        nxt = c[x + 1] if x < 15 else jnp.where(half, along(c[0], 1, 64), 0.0)
        hx[x + 1] = harmonic(c[x], nxt)
    hx[0] = along(hx[16], 1, 64)
    for x in range(16):
        hy[x] = harmonic(c[x], jnp.where(last_y, 0.0, along(c[x], 0, 1)))
        hz[x] = harmonic(c[x], jnp.where(last_z, 0.0, along(c[x], 1, 1)))
        dg[x] = diagonal_of(c[x], hx[x + 1], hx[x], hy[x], hz[x])

    def total(acc):
        return jnp.sum(acc, axis=(0, 1), keepdims=True)

    def dot_image():
        acc = jnp.zeros((16, 128), F32)
        for x in range(16):
            v = dire[x]
            vp = dire[x + 1] if x < 15 else along(dire[0], 1, 64)
            vm = dire[x - 1] if x > 0 else along(dire[15], 1, 64)
            image = operate(dg[x], v, hx[x + 1], vp, hx[x], vm, hy[x], hz[x])
            img[x] = image
            acc = acc + v * image
        return total(acc)

    def norm():
        acc = jnp.zeros((16, 128), F32)
        for x in range(16):
            acc = acc + res[x] * res[x]
        return total(acc)

    def step(_, rr):
        alpha = rr / dot_image()
        acc = jnp.zeros((16, 128), F32)
        for x in range(16):
            sol[x] = sol[x] + alpha * dire[x]
            rx = res[x] - alpha * img[x]
            res[x] = rx
            acc = acc + rx * rx
        new = total(acc)
        beta = new / rr
        for x in range(16):
            dire[x] = res[x] + beta * dire[x]
        return new

    rr = lax.fori_loop(0, BOTTOM - 1, step, norm())
    gx, gy = lax.axis_index("gx"), lax.axis_index("gy")
    xi = lax.rem(gx, 16)
    alpha = rr / dot_image()
    mine = sol[xi] + alpha * dire[xi]
    mine = jnp.where(gx >= 16, along(mine, 1, 64), mine)
    row = positions((16, 128), 0)
    mine = jnp.sum(jnp.where(row == gy, mine, 0.0), axis=0, keepdims=True)
    row = positions((32, 128), 0)
    lows = []
    for x in range(2):
        e = elow[32 * x:32 * x + 32, :]
        for y in range(2):
            lows.append(jnp.sum(jnp.where(row == 2 * gy + y, e, 0.0), axis=0, keepdims=True))
    coarse = matmul(jnp.broadcast_to(mine, (8, 128)), doubling(128, 256, 4))
    finer = matmul(jnp.concatenate(lows + lows, axis=0), doubling(128, 256, 2))
    for x in range(4):
        k = 2 * (x // 2)
        for y in range(4):
            add = finer[k + y // 2:k + y // 2 + 1, :] + coarse[0:1, :]
            out[x, y:y + 1, :] = emid[x, y:y + 1, :] + add


def swaps(near, far, axis):
    n = lax.axis_size(axis)
    pairs = [(i, i + 1) for i in range(1, n - 1, 2)] + [(i + 1, i) for i in range(1, n - 1, 2)]
    far = lax.ppermute(far, axis, pairs)
    return lax.ppermute(near, axis, [(i, i ^ 1) for i in range(n)]), far


def shards(phi_start, right_side, coefficient):
    own = [a.reshape(64, 512) for a in (phi_start, right_side, coefficient)]
    near, far = call(
        pack_y, [(8 * NROWS, 512)] * 2, [(64, 512)] * 3 + [(768, 128), (2, 8 * NROWS, 512)],
        n_in=3, copies=9, in_hbm=3, out_hbm=2, limit=64000000)(*own)
    near, far = swaps(near, far, "gy")
    *ext, mate, other = call(pack_x, [(192, 512)] * 3 + [(END_ROWS, 512)] * 2, [(1536, 128)], n_in=5)(*own, far, near)
    mate, other = swaps(mate, other, "gx")
    ext = [a.reshape(8, 24, 512) for a in ext]

    def slabs(*n):
        return (*n, 24, 512)

    *inside, cmid = call(
        inner,
        [slabs(2, 3), slabs(1)] + [slabs(2, 4)] * 3 + [slabs(2, 3)] * 2 + [slabs(2, 2), slabs(2), (4, 16, 256)],
        [(4, 4, 24, 128), (64, 512)], n_in=3,
        cost=pl.CostEstimate(flops=16_000_000, bytes_accessed=4_000_000, transcendentals=0),
    )(*ext)
    phi_fine, smid, chalo = call(
        outer,
        [(8, 8, 512), (8, 16, 256), (6, 16, 256)],
        [slabs(2, 8)] * 11 + [(8, 8, 512), (4, 14, 24, 128), (224, 512)],
        n_in=14, copies=1, out_hbm=1,
    )(*ext, *inside, other, mate)
    emid, spread = call(middle, [(4, 4, 256), (16, 16, 128)], [(128, 128)], n_in=3)(smid, cmid, chalo)
    gathered = lax.all_to_all(spread, "gy", 0, 0, tiled=True)
    (sdc,) = call(columns, [(192, 128)], [(128, 128)], n_in=1)(gathered.reshape(256, 128))
    mate, other = swaps(sdc, sdc, "gx")
    elow, spread = call(low, [(64, 128), (32, 16, 128)], [(64, 128)], n_in=3)(sdc, mate, other)
    gathered = lax.all_to_all(spread, "gx", 0, 0, tiled=True)
    (correction,) = call(bottom, [(4, 4, 256)], [(17, 16, 128)] + [(16, 16, 128)] * 7, n_in=3)(
        gathered, elow, emid)
    return phi_fine, correction


def solution(mesh):
    return jax.shard_map(
        shards,
        mesh=mesh,
        in_specs=(P("gx", "gy", None),) * 3,
        out_specs=(P("gx", "gy", None),) * 2,
        check_vma=False,
    )
```

```python
import jax
import jax.numpy as jnp
from jax import lax
from jax.experimental import pallas as pl
from jax.experimental.pallas import tpu as pltpu
from jax.sharding import PartitionSpec as P

BOTTOM = 6
RELAX_WEIGHT = 0.8
FLOOR = 1e-3
F32 = jnp.float32
VMEM = pl.BlockSpec(memory_space=pltpu.VMEM)
HBM = pl.BlockSpec(memory_space=pltpu.HBM)


def call(kernel, out_shapes, scratch=(), n_in=0, copies=0, in_hbm=0, out_hbm=0, limit=24 * 1024 * 1024, cost=None):
    semaphores = [pltpu.SemaphoreType.DMA((copies,))] if copies else []
    return pl.pallas_call(
        kernel,
        out_shape=[jax.ShapeDtypeStruct(s, F32) for s in out_shapes],
        in_specs=[HBM] * in_hbm + [VMEM] * (n_in - in_hbm),
        out_specs=[HBM] * out_hbm + [VMEM] * (len(out_shapes) - out_hbm),
        scratch_shapes=[pltpu.VMEM(s, F32) for s in scratch] + semaphores,
        compiler_params=pltpu.CompilerParams(vmem_limit_bytes=limit),
        cost_estimate=cost,
    )


def reciprocal(x):
    r = pl.reciprocal(x, approx=True)
    return r * (2.0 - x * r)


def harmonic(a, b):
    return 2.0 * a * b * reciprocal(jnp.maximum(a + b, FLOOR))


def along(v, axis, step):
    n = v.shape[axis]
    return pltpu.roll(v, (-step) % n, axis)


def is_first():
    return lax.rem(lax.axis_index("gx"), 2) == 0


def positions(shape, axis):
    return lax.broadcasted_iota(jnp.int32, shape, axis)


def halving(rows, cols):
    return (positions((rows, cols), 0) // 2 == positions((rows, cols), 1)).astype(F32)


def doubling(rows, cols, factor):
    return (positions((rows, cols), 1) // factor == positions((rows, cols), 0)).astype(F32)


def matmul(a, b):
    return jnp.dot(a, b, precision=lax.Precision.HIGHEST, preferred_element_type=F32)


def exact_matmul(a, ones):
    parts = []
    for _ in range(3):
        parts.append(a.astype(jnp.bfloat16))
        a = a - parts[-1].astype(F32)
    ones = ones.astype(jnp.bfloat16)
    return sum(jnp.dot(p, ones, preferred_element_type=F32) for p in reversed(parts))


def weight(face, centre):
    return jnp.where(face > 0.0, face, centre)


def diagonal_of(c, xp, xm, hy, hz):
    return (weight(xp, c) + weight(xm, c) + weight(hy, c) + weight(along(hy, 0, -1), c)
            + weight(hz, c) + weight(along(hz, 1, -1), c))


def operate(d, v, xp, vp, xm, vm, hy, hz):
    out = d * v - xp * vp - xm * vm
    out = out - hy * along(v, 0, 1) - along(hy * v, 0, -1)
    return out - hz * along(v, 1, 1) - along(hz * v, 1, -1)


def z_face(c):
    nxt = jnp.where(positions(c.shape, 1) < c.shape[1] - 1, along(c, 1, 1), 0.0)
    return harmonic(c, nxt)


NP, NR, NC = 7, 6, 7
NROWS = NP + NR + NC
PHI_TILES = (3, 3, 2, 2, 2, 2, 1)
RHS_TILES = (3, 2, 2, 2, 2, 1)
END_ROWS = 8 * (2 * sum(PHI_TILES) + sum(RHS_TILES))


def pack_y(phi_in, rhs_in, coef_in, near, far, phi, rhs, coef, stage, ends, sem):
    loads = [pltpu.make_async_copy(src, dst, sem.at[a])
             for a, (src, dst) in enumerate(((phi_in, phi), (rhs_in, rhs), (coef_in, coef)))]
    for load in loads:
        load.start()
    stores = []
    k = 0
    for a, (ref, n) in enumerate(((phi, NP), (rhs, NR), (coef, NC))):
        loads[a].wait()
        for q in range(4):
            lanes = slice(128 * q, 128 * q + 128)
            base = 64 * (4 * a + q)
            stage[base:base + 64, :] = ref[:, lanes]
            for j in range(n):
                rows = slice(8 * (k + j), 8 * (k + j) + 8)
                ends[0, rows, lanes] = stage[pl.ds(base + 8 - n + j, 8, stride=8), :]
                ends[1, rows, lanes] = stage[pl.ds(base + j, 8, stride=8), :]
        for b, dst in enumerate((near, far)):
            part = pl.ds(8 * k, 8 * n)
            src = ends.at[lax.rem(lax.axis_index("gy") + b, 2), part]
            stores.append(pltpu.make_async_copy(src, dst.at[part], sem.at[3 + 2 * a + b]))
            stores[-1].start()
        k += n
    for store in stores:
        store.wait()


def pack_x(phi, rhs, coef, far, near, pe, re, ce, mate, other, stage):
    zero = jnp.zeros((8, 128), F32)
    odd = lax.rem(lax.axis_index("gy"), 2)
    k = 0
    for a, (ref, ext, n) in enumerate(((phi, pe, NP), (rhs, re, NR), (coef, ce, NC))):
        for x in range(8):
            ext[24 * x:24 * x + 8, :] = ref[8 * x:8 * x + 8, :]
        for q in range(4):
            lanes = slice(128 * q, 128 * q + 128)
            base = 128 * (4 * a + q)
            for j in range(n):
                rows = slice(8 * (k + j), 8 * (k + j) + 8)
                stage[pl.ds(base + j + odd * (16 - n), 8, stride=16), :] = near[rows, lanes]
                stage[pl.ds(base + j + (1 - odd) * (16 - n), 8, stride=16), :] = far[rows, lanes]
            for j in range(n, 16 - n):
                stage[pl.ds(base + j, 8, stride=16), :] = zero
            for x in range(8):
                ext[24 * x + 8:24 * x + 24, lanes] = stage[base + 16 * x:base + 16 * x + 16, :]
        k += n
    first = is_first()
    top = positions((8, 512), 0) < 4
    for ref, end in ((mate, first), (other, jnp.logical_not(first))):
        row = 0
        for ext, tiles in ((pe, PHI_TILES), (re, RHS_TILES), (ce, PHI_TILES)):
            for k, n in enumerate(tiles):
                at = 24 * jnp.where(end, 7 - k, k)
                parts = [ext[pl.ds(pl.multiple_of(at + 8 * t, 8), 8), :] for t in range(min(n + n // 2, 3))]
                if n == 2:
                    parts = [parts[0], jnp.where(top, parts[1], parts[2])]
                for part in parts:
                    ref[row:row + 8, :] = part
                    row += 8


def slab_x(side, t):
    return jnp.where(side == 0, 3 - t, 4 + t)


def first_weights(c, xp, xm):
    hy = harmonic(c, along(c, 0, 1))
    hz = z_face(c)
    d = weight(xm, c) + weight(hy, c) + weight(along(hy, 0, -1), c) + weight(hz, c) + weight(along(hz, 1, -1), c)
    return hy, hz, d if xp is None else d + weight(xp, c)


def inverse(d):
    return RELAX_WEIGHT * reciprocal(jnp.maximum(d, FLOOR))


def pair_sums(sums, place, a, b, scale):
    t = a + b
    t = (t + along(t, 0, 1)) * scale
    for q in range(4):
        sums[q, place] = t[:, 128 * q:128 * q + 128]


def halve_fine(sums, packed, n):
    for k in range(n):
        for q in range(4):
            lanes = slice(128 * q, 128 * q + 128)
            packed[16 * k:16 * k + 8, lanes] = sums[q, k, pl.ds(0, 8, stride=2), :]
            packed[16 * k + 8:16 * k + 12, lanes] = jnp.zeros((4, 128), F32)
            packed[16 * k + 12:16 * k + 16, lanes] = sums[q, k, pl.ds(16, 4, stride=2), :]
    return exact_matmul(packed[...], halving(512, 256)).reshape(n, 16, 256)


def inner(pe, re, ce, hx, hc, hy, hz, dg, rd, p1, p2, res, cmid, sums, packed):
    hc[0] = harmonic(ce[3], ce[4])

    def start(side, carry):
        for t in range(4):
            x = slab_x(side, t)
            c = ce[x]
            xm = hc[0] if t == 0 else hx[side, t - 1]
            xp = None
            if t < 3:
                xp = harmonic(c, ce[slab_x(side, t + 1)])
                hx[side, t] = xp
            hyt, hzt, d = first_weights(c, xp, xm)
            hy[side, t], hz[side, t], dg[side, t] = hyt, hzt, d
            if t < 3:
                r = inverse(d)
                rd[side, t] = r
                v = pe[x]
                image = operate(d, v, xp, pe[slab_x(side, t + 1)], xm, pe[slab_x(side, t - 1)], hyt, hzt)
                p1[side, t] = v + (re[x] - image) * r
        for q in range(2):
            pair_sums(sums, jnp.where(side == 0, 1 - q, 2 + q),
                      ce[slab_x(side, 2 * q)], ce[slab_x(side, 2 * q + 1)], 0.125)
        return carry

    lax.fori_loop(0, 2, start, 0)

    def image(side, t, p):
        xm, pm = (hc[0], p[1 - side, 0]) if t == 0 else (hx[side, t - 1], p[side, t - 1])
        return operate(dg[side, t], p[side, t], hx[side, t], p[side, t + 1], xm, pm, hy[side, t], hz[side, t])

    def second(side, carry):
        for t in range(2):
            p2[side, t] = p1[side, t] + (re[slab_x(side, t)] - image(side, t, p1)) * rd[side, t]
        return carry

    lax.fori_loop(0, 2, second, 0)

    def third(side, carry):
        res[side] = re[slab_x(side, 0)] - image(side, 0, p2)
        return carry

    lax.fori_loop(0, 2, third, 0)
    cmid[...] = halve_fine(sums, packed, 4)


def unpack(ref, p0, rs, c, side):
    row = 0
    for dst, tiles in ((p0, PHI_TILES), (rs, RHS_TILES), (c, PHI_TILES)):
        for k, n in enumerate(tiles):
            parts = [ref[row + 8 * t:row + 8 * t + 8, :] for t in range(n)]
            row += 8 * n
            if n == 1:
                parts += [jnp.zeros((8, 512), F32)] * 2
            if n == 2:
                parts += [parts[1]]
            for t in range(3):
                dst[side, k + 1, 8 * t:8 * t + 8, :] = parts[t]


def outer(pe, re, ce, hx, hc, hy, hz, dg, rd, p1, p2, res, other, mate, phi_out, smid, chalo,
          p0h, rsh, ch, hxh, hyh, hzh, dgh, rdh, p1h, p2h, resh, own, sums, packed, left):
    first = is_first()
    near = jnp.where(first, 1, 0)
    unpack(mate, p0h, rsh, ch, near)
    unpack(other, p0h, rsh, ch, 1 - near)

    def sweeps(side, carry):
        x0 = slab_x(side, 3)
        p0h[side, 0], rsh[side, 0], ch[side, 0] = pe[x0], re[x0], ce[x0]
        c = ch[side, 0]
        xp = harmonic(c, ch[side, 1])
        d = dg[side, 3] + weight(xp, c)
        r = inverse(d)
        hxh[side, 0], hyh[side, 0], hzh[side, 0], dgh[side, 0], rdh[side, 0] = xp, hy[side, 3], hz[side, 3], d, r
        v = p0h[side, 0]
        image = operate(d, v, xp, p0h[side, 1], hx[side, 2], pe[slab_x(side, 2)], hy[side, 3], hz[side, 3])
        p1h[side, 0] = v + (rsh[side, 0] - image) * r

        def start(j, carry):
            c = ch[side, j]
            xp, xm = harmonic(c, ch[side, j + 1]), hxh[side, j - 1]
            hyj, hzj, d = first_weights(c, xp, xm)
            r = inverse(d)
            hxh[side, j], hyh[side, j], hzh[side, j], dgh[side, j], rdh[side, j] = xp, hyj, hzj, d, r
            v = p0h[side, j]
            image = operate(d, v, xp, p0h[side, j + 1], xm, p0h[side, j - 1], hyj, hzj)
            p1h[side, j] = v + (rsh[side, j] - image) * r
            return carry

        lax.fori_loop(1, 7, start, 0, unroll=True)

        image = operate(dg[side, 2], p1[side, 2], hx[side, 2], p1h[side, 0], hx[side, 1], p1[side, 1],
                        hy[side, 2], hz[side, 2])
        p2h[side, 1] = p1[side, 2] + (re[slab_x(side, 2)] - image) * rd[side, 2]
        p2h[side, 0] = p2[side, 1]
        image = operate(dgh[side, 0], p1h[side, 0], hxh[side, 0], p1h[side, 1], hx[side, 2], p1[side, 2],
                        hyh[side, 0], hzh[side, 0])
        p2h[side, 2] = p1h[side, 0] + (rsh[side, 0] - image) * rdh[side, 0]

        def second(j, carry):
            v = p1h[side, j]
            image = operate(dgh[side, j], v, hxh[side, j], p1h[side, j + 1], hxh[side, j - 1], p1h[side, j - 1],
                            hyh[side, j], hzh[side, j])
            p2h[side, j + 2] = v + (rsh[side, j] - image) * rdh[side, j]
            return carry

        lax.fori_loop(1, 6, second, 0, unroll=True)
        for t in range(4):
            own[slab_x(side, t)] = (p2[side, t] if t < 2 else p2h[side, t - 1])[0:8, :]

        for t in (1, 2):
            image = operate(dg[side, t], p2h[side, t - 1], hx[side, t], p2h[side, t], hx[side, t - 1],
                            p2[side, 0] if t == 1 else p2h[side, 0], hy[side, t], hz[side, t])
            resh[side, t - 1] = re[slab_x(side, t)] - image
        image = operate(dgh[side, 0], p2h[side, 2], hxh[side, 0], p2h[side, 3], hx[side, 2], p2h[side, 1],
                        hyh[side, 0], hzh[side, 0])
        resh[side, 2] = rsh[side, 0] - image

        def third(j, carry):
            image = operate(dgh[side, j], p2h[side, j + 2], hxh[side, j], p2h[side, j + 3], hxh[side, j - 1],
                            p2h[side, j + 1], hyh[side, j], hzh[side, j])
            resh[side, j + 2] = rsh[side, j] - image
            return carry

        lax.fori_loop(1, 5, third, 0, unroll=True)
        for q in range(4):
            a = res[side] if q == 0 else resh[side, 2 * q - 1]
            pair_sums(sums, jnp.where(side == 0, 3 - q, 4 + q), a, resh[side, 2 * q], 0.5)
        for q in range(3):
            pair_sums(sums, 8 + jnp.where(side == 0, 2 - q, 3 + q), ch[side, 2 * q + 1], ch[side, 2 * q + 2], 0.125)
        return carry

    lax.fori_loop(0, 2, sweeps, 0)
    store = pltpu.make_async_copy(own, phi_out, left.at[0])
    store.start()
    mid = halve_fine(sums, packed, 14)
    smid[...] = mid[0:8]
    chalo[...] = mid[8:14]
    store.wait()


def middle(smid, cmid, chalo, emid, out, sums):
    s = [smid[j] for j in range(8)]
    c = [chalo[j] for j in range(3)] + [cmid[j] for j in range(4)] + [chalo[j] for j in range(3, 6)]
    hx = [harmonic(c[j], c[j + 1]) for j in range(9)]
    hy, hz, d, r, e1 = [], [], [], [], []
    for i in range(8):
        ci = c[i + 1]
        hy.append(harmonic(ci, along(ci, 0, 1)))
        hz.append(z_face(ci))
        d.append(diagonal_of(ci, hx[i + 1], hx[i], hy[i], hz[i]))
        r.append(inverse(d[i]))
        e1.append(s[i] * r[i])

    def image(i, e):
        return operate(d[i], e[i], hx[i + 1], e[i + 1], hx[i], e[i - 1], hy[i], hz[i])

    e2 = [None] + [e1[i] + (s[i] - image(i, e1)) * r[i] for i in range(1, 7)] + [None]
    res = [s[i] - image(i, e2) for i in range(2, 6)]
    for x in range(4):
        emid[x] = e2[2 + x][0:4, :]
    groups = [(res[2 * x] + res[2 * x + 1]) * 0.5 for x in range(2)]
    groups += [(c[2 * x + 1] + c[2 * x + 2]) * 0.125 for x in range(4)]
    groups += groups[0:2]
    for g in range(8):
        both = (groups[g] + along(groups[g], 0, 1))[0:8, :]
        sums[8 * g:8 * g + 8, :] = both[:, 0:128]
        sums[64 + 8 * g:72 + 8 * g, :] = both[:, 128:256]

    def rows(y):
        return jnp.concatenate([sums[pl.ds(64 * q + 2 * y, 8, stride=8), :] for q in range(2)], axis=1)

    low0 = matmul(rows(0), halving(256, 128))
    low1 = matmul(rows(1), halving(256, 128))
    for n in range(16):
        out[n, 0:8, :] = low0
        out[n, 8:16, :] = low1


def y_face(c):
    n = c.shape[0]
    return harmonic(c, jnp.where(positions(c.shape, 0) < n - 1, along(c, 0, 1), 0.0))


def columns(gathered, sdc, ccol):
    for g in range(6):
        for y in range(2):
            rows = gathered[pl.ds(8 * y + g, 16, stride=16), :]
            ref, k = (sdc, g) if g < 2 else (ccol, g - 2)
            ref[pl.ds(32 * k + y, 16, stride=2), :] = rows
    c = [ccol[32 * j:32 * j + 32, :] for j in range(4)]
    hx = [harmonic(c[j], c[j + 1]) for j in range(3)]
    for x in range(2):
        ci = c[1 + x]
        sdc[64 + 32 * x:96 + 32 * x, :] = diagonal_of(ci, hx[x + 1], hx[x], y_face(ci), z_face(ci))
        sdc[128 + 32 * x:160 + 32 * x, :] = ci


def low(sdc, mate, other, elow, out, sums):
    first = is_first()
    hi = jnp.where(first, mate[...], other[...])
    lo = jnp.where(first, other[...], mate[...])

    def part(ref, k):
        return ref[32 * k:32 * k + 32, :]

    s, d, c = ([part(ref, k + j) for ref in (lo, sdc, hi) for j in (0, 1)] for k in (0, 2, 4))
    hx = [harmonic(c[j], c[j + 1]) for j in range(5)]
    hy = [y_face(ci) for ci in c]
    hz = [z_face(ci) for ci in c]
    r = [inverse(di) for di in d]
    e1 = [s[i] * r[i] for i in range(6)]

    def image(i, e):
        return operate(d[i], e[i], hx[i], e[i + 1], hx[i - 1], e[i - 1], hy[i], hz[i])

    e2 = [None] + [e1[i] + (s[i] - image(i, e1)) * r[i] for i in range(1, 5)] + [None]
    res = [s[i] - image(i, e2) for i in range(2, 4)]
    for x in range(2):
        elow[32 * x:32 * x + 32, :] = e2[2 + x]
    a = (res[0] + res[1]) * 0.5
    b = (c[2] + c[3]) * 0.125
    sums[0:32, :] = a + along(a, 0, 1)
    sums[32:64, :] = b + along(b, 0, 1)
    ra = sums[pl.ds(0, 16, stride=2), :]
    rb = sums[pl.ds(32, 16, stride=2), :]
    both = matmul(jnp.concatenate([ra, rb], axis=1), halving(256, 128))
    for n in range(32):
        out[n] = both


def bottom(gathered, elow, emid, out, hx, hy, hz, dg, sol, res, dire, img):
    half = positions((16, 128), 1) < 64
    last_z = positions((16, 128), 1) % 64 == 63
    last_y = positions((16, 128), 0) == 15
    c = []
    for x in range(16):
        a, b = gathered[x], gathered[x + 16]
        source = jnp.where(half, a, along(b, 1, 64))
        c.append(jnp.where(half, along(a, 1, 64), b))
        res[x] = source
        dire[x] = source
        sol[x] = jnp.zeros((16, 128), F32)
    for x in range(16):
        nxt = c[x + 1] if x < 15 else jnp.where(half, along(c[0], 1, 64), 0.0)
        hx[x + 1] = harmonic(c[x], nxt)
    hx[0] = along(hx[16], 1, 64)
    for x in range(16):
        hy[x] = harmonic(c[x], jnp.where(last_y, 0.0, along(c[x], 0, 1)))
        hz[x] = harmonic(c[x], jnp.where(last_z, 0.0, along(c[x], 1, 1)))
        dg[x] = diagonal_of(c[x], hx[x + 1], hx[x], hy[x], hz[x])

    def total(acc):
        return jnp.sum(jnp.sum(acc, axis=0, keepdims=True), axis=1, keepdims=True)

    def dot_image():
        acc = jnp.zeros((16, 128), F32)
        for x in range(16):
            v = dire[x]
            vp = dire[x + 1] if x < 15 else along(dire[0], 1, 64)
            vm = dire[x - 1] if x > 0 else along(dire[15], 1, 64)
            image = operate(dg[x], v, hx[x + 1], vp, hx[x], vm, hy[x], hz[x])
            img[x] = image
            acc = acc + v * image
        return total(acc)

    def norm():
        acc = jnp.zeros((16, 128), F32)
        for x in range(16):
            acc = acc + res[x] * res[x]
        return total(acc)

    def step(_, rr):
        alpha = rr / dot_image()
        acc = jnp.zeros((16, 128), F32)
        for x in range(16):
            sol[x] = sol[x] + alpha * dire[x]
            rx = res[x] - alpha * img[x]
            res[x] = rx
            acc = acc + rx * rx
        new = total(acc)
        beta = new / rr
        for x in range(16):
            dire[x] = res[x] + beta * dire[x]
        return new

    rr = lax.fori_loop(0, BOTTOM - 1, step, norm())
    gx, gy = lax.axis_index("gx"), lax.axis_index("gy")
    xi = lax.rem(gx, 16)
    alpha = rr / dot_image()
    mine = sol[xi] + alpha * dire[xi]
    mine = jnp.where(gx >= 16, along(mine, 1, 64), mine)
    row = positions((16, 128), 0)
    mine = jnp.sum(jnp.where(row == gy, mine, 0.0), axis=0, keepdims=True)
    row = positions((32, 128), 0)
    lows = []
    for x in range(2):
        e = elow[32 * x:32 * x + 32, :]
        for y in range(2):
            lows.append(jnp.sum(jnp.where(row == 2 * gy + y, e, 0.0), axis=0, keepdims=True))
    coarse = matmul(jnp.broadcast_to(mine, (8, 128)), doubling(128, 256, 4))
    finer = matmul(jnp.concatenate(lows + lows, axis=0), doubling(128, 256, 2))
    for x in range(4):
        k = 2 * (x // 2)
        for y in range(4):
            add = finer[k + y // 2:k + y // 2 + 1, :] + coarse[0:1, :]
            out[x, y:y + 1, :] = emid[x, y:y + 1, :] + add


def swaps(near, far, axis):
    n = lax.axis_size(axis)
    pairs = [(i, i + 1) for i in range(1, n - 1, 2)] + [(i + 1, i) for i in range(1, n - 1, 2)]
    far = lax.ppermute(far, axis, pairs)
    return lax.ppermute(near, axis, [(i, i ^ 1) for i in range(n)]), far


def shards(phi_start, right_side, coefficient):
    own = [a.reshape(64, 512) for a in (phi_start, right_side, coefficient)]
    near, far = call(
        pack_y, [(8 * NROWS, 512)] * 2, [(64, 512)] * 3 + [(768, 128), (2, 8 * NROWS, 512)],
        n_in=3, copies=9, in_hbm=3, out_hbm=2, limit=64000000)(*own)
    near, far = swaps(near, far, "gy")
    *ext, mate, other = call(pack_x, [(192, 512)] * 3 + [(END_ROWS, 512)] * 2, [(1536, 128)], n_in=5)(*own, far, near)
    mate, other = swaps(mate, other, "gx")
    ext = [a.reshape(8, 24, 512) for a in ext]

    def slabs(*n):
        return (*n, 24, 512)

    *inside, cmid = call(
        inner,
        [slabs(2, 3), slabs(1)] + [slabs(2, 4)] * 3 + [slabs(2, 3)] * 2 + [slabs(2, 2), slabs(2), (4, 16, 256)],
        [(4, 4, 24, 128), (64, 512)], n_in=3,
        cost=pl.CostEstimate(flops=16_000_000, bytes_accessed=4_000_000, transcendentals=0),
    )(*ext)
    phi_fine, smid, chalo = call(
        outer,
        [(8, 8, 512), (8, 16, 256), (6, 16, 256)],
        [slabs(2, 8)] * 11 + [(8, 8, 512), (4, 14, 24, 128), (224, 512)],
        n_in=14, copies=1, out_hbm=1,
    )(*ext, *inside, other, mate)
    emid, spread = call(middle, [(4, 4, 256), (16, 16, 128)], [(128, 128)], n_in=3)(smid, cmid, chalo)
    gathered = lax.all_to_all(spread, "gy", 0, 0, tiled=True)
    (sdc,) = call(columns, [(192, 128)], [(128, 128)], n_in=1)(gathered.reshape(256, 128))
    mate, other = swaps(sdc, sdc, "gx")
    elow, spread = call(low, [(64, 128), (32, 16, 128)], [(64, 128)], n_in=3)(sdc, mate, other)
    gathered = lax.all_to_all(spread, "gx", 0, 0, tiled=True)
    (correction,) = call(bottom, [(4, 4, 256)], [(17, 16, 128)] + [(16, 16, 128)] * 7, n_in=3)(
        gathered, elow, emid)
    return phi_fine, correction


def solution(mesh):
    return jax.shard_map(
        shards,
        mesh=mesh,
        in_specs=(P("gx", "gy", None),) * 3,
        out_specs=(P("gx", "gy", None),) * 2,
        check_vma=False,
    )
```

```python
import jax
import jax.numpy as jnp
from jax import lax
from jax.experimental import pallas as pl
from jax.experimental.pallas import tpu as pltpu
from jax.sharding import PartitionSpec as P

BOTTOM = 6
RELAX_WEIGHT = 0.8
FLOOR = 1e-3
F32 = jnp.float32
VMEM = pl.BlockSpec(memory_space=pltpu.VMEM)
HBM = pl.BlockSpec(memory_space=pltpu.HBM)


def call(kernel, out_shapes, scratch=(), n_in=0, copies=0, in_hbm=0, out_hbm=0, limit=24 * 1024 * 1024, cost=None):
    semaphores = [pltpu.SemaphoreType.DMA((copies,))] if copies else []
    return pl.pallas_call(
        kernel,
        out_shape=[jax.ShapeDtypeStruct(s, F32) for s in out_shapes],
        in_specs=[HBM] * in_hbm + [VMEM] * (n_in - in_hbm),
        out_specs=[HBM] * out_hbm + [VMEM] * (len(out_shapes) - out_hbm),
        scratch_shapes=[pltpu.VMEM(s, F32) for s in scratch] + semaphores,
        compiler_params=pltpu.CompilerParams(vmem_limit_bytes=limit),
        cost_estimate=cost,
    )


def reciprocal(x):
    r = pl.reciprocal(x, approx=True)
    return r * (2.0 - x * r)


def harmonic(a, b):
    return 2.0 * a * b * reciprocal(jnp.maximum(a + b, FLOOR))


def along(v, axis, step):
    n = v.shape[axis]
    return pltpu.roll(v, (-step) % n, axis)


def is_first():
    return lax.rem(lax.axis_index("gx"), 2) == 0


def positions(shape, axis):
    return lax.broadcasted_iota(jnp.int32, shape, axis)


def halving(rows, cols):
    return (positions((rows, cols), 0) // 2 == positions((rows, cols), 1)).astype(F32)


def doubling(rows, cols, factor):
    return (positions((rows, cols), 1) // factor == positions((rows, cols), 0)).astype(F32)


def matmul(a, b):
    return jnp.dot(a, b, precision=lax.Precision.HIGHEST, preferred_element_type=F32)


def exact_matmul(a, ones):
    parts = []
    for _ in range(3):
        parts.append(a.astype(jnp.bfloat16))
        a = a - parts[-1].astype(F32)
    ones = ones.astype(jnp.bfloat16)
    return sum(jnp.dot(p, ones, preferred_element_type=F32) for p in reversed(parts))


def weight(face, centre):
    return jnp.where(face > 0.0, face, centre)


def diagonal_of(c, xp, xm, hy, hz):
    return (weight(xp, c) + weight(xm, c) + weight(hy, c) + weight(along(hy, 0, -1), c)
            + weight(hz, c) + weight(along(hz, 1, -1), c))


def operate(d, v, xp, vp, xm, vm, hy, hz):
    out = d * v - xp * vp - xm * vm
    out = out - hy * along(v, 0, 1) - along(hy * v, 0, -1)
    return out - hz * along(v, 1, 1) - along(hz * v, 1, -1)


def z_face(c):
    nxt = jnp.where(positions(c.shape, 1) < c.shape[1] - 1, along(c, 1, 1), 0.0)
    return harmonic(c, nxt)


NP, NR, NC = 7, 6, 7
NROWS = NP + NR + NC
PHI_TILES = (3, 3, 2, 2, 2, 2, 1)
RHS_TILES = (3, 2, 2, 2, 2, 1)
COEF_TILES = (3, 3, 2, 2, 2, 2, 1, 1)
END_ROWS = 8 * (sum(PHI_TILES) + sum(RHS_TILES) + sum(COEF_TILES))


def pack_y(phi_in, rhs_in, coef_in, near, far, phi, rhs, coef, stage, ends, sem):
    loads = [pltpu.make_async_copy(src, dst, sem.at[a])
             for a, (src, dst) in enumerate(((phi_in, phi), (rhs_in, rhs), (coef_in, coef)))]
    for load in loads:
        load.start()
    stores = []
    k = 0
    for a, (ref, n) in enumerate(((phi, NP), (rhs, NR), (coef, NC))):
        loads[a].wait()
        for q in range(4):
            lanes = slice(128 * q, 128 * q + 128)
            base = 64 * (4 * a + q)
            stage[base:base + 64, :] = ref[:, lanes]
            for j in range(n):
                rows = slice(8 * (k + j), 8 * (k + j) + 8)
                ends[0, rows, lanes] = stage[pl.ds(base + 8 - n + j, 8, stride=8), :]
                ends[1, rows, lanes] = stage[pl.ds(base + j, 8, stride=8), :]
        for b, dst in enumerate((near, far)):
            part = pl.ds(8 * k, 8 * n)
            src = ends.at[lax.rem(lax.axis_index("gy") + b, 2), part]
            stores.append(pltpu.make_async_copy(src, dst.at[part], sem.at[3 + 2 * a + b]))
            stores[-1].start()
        k += n
    for store in stores:
        store.wait()


def pack_x(phi, rhs, coef, far, near, pe, re, ce, mate, other, stage):
    zero = jnp.zeros((8, 128), F32)
    odd = lax.rem(lax.axis_index("gy"), 2)
    k = 0
    for a, (ref, ext, n) in enumerate(((phi, pe, NP), (rhs, re, NR), (coef, ce, NC))):
        for x in range(8):
            ext[24 * x:24 * x + 8, :] = ref[8 * x:8 * x + 8, :]
        for q in range(4):
            lanes = slice(128 * q, 128 * q + 128)
            base = 128 * (4 * a + q)
            for j in range(n):
                rows = slice(8 * (k + j), 8 * (k + j) + 8)
                stage[pl.ds(base + j + odd * (16 - n), 8, stride=16), :] = near[rows, lanes]
                stage[pl.ds(base + j + (1 - odd) * (16 - n), 8, stride=16), :] = far[rows, lanes]
            for j in range(n, 16 - n):
                stage[pl.ds(base + j, 8, stride=16), :] = zero
            for x in range(8):
                ext[24 * x + 8:24 * x + 24, lanes] = stage[base + 16 * x:base + 16 * x + 16, :]
        k += n
    first = is_first()
    top = positions((8, 512), 0) < 4
    for ref, end in ((mate, first), (other, jnp.logical_not(first))):
        row = 0
        for ext, tiles in ((pe, PHI_TILES), (re, RHS_TILES), (ce, COEF_TILES)):
            for k, n in enumerate(tiles):
                at = 24 * jnp.where(end, 7 - k, k)
                parts = [ext[pl.ds(pl.multiple_of(at + 8 * t, 8), 8), :] for t in range(min(n + n // 2, 3))]
                if n == 2:
                    parts = [parts[0], jnp.where(top, parts[1], parts[2])]
                for part in parts:
                    ref[row:row + 8, :] = part
                    row += 8


def slab_x(side, t):
    return jnp.where(side == 0, 3 - t, 4 + t)


def first_weights(c, xp, xm):
    hy = harmonic(c, along(c, 0, 1))
    hz = z_face(c)
    d = weight(xm, c) + weight(hy, c) + weight(along(hy, 0, -1), c) + weight(hz, c) + weight(along(hz, 1, -1), c)
    return hy, hz, d if xp is None else d + weight(xp, c)


def inverse(d):
    return RELAX_WEIGHT * reciprocal(jnp.maximum(d, FLOOR))


def pair_sums(sums, place, a, b, scale):
    t = a + b
    t = (t + along(t, 0, 1)) * scale
    for q in range(4):
        sums[q, place] = t[:, 128 * q:128 * q + 128]


def halve_fine(sums, packed, n):
    for k in range(n):
        for q in range(4):
            lanes = slice(128 * q, 128 * q + 128)
            packed[16 * k:16 * k + 8, lanes] = sums[q, k, pl.ds(0, 8, stride=2), :]
            packed[16 * k + 8:16 * k + 12, lanes] = jnp.zeros((4, 128), F32)
            packed[16 * k + 12:16 * k + 16, lanes] = sums[q, k, pl.ds(16, 4, stride=2), :]
    return exact_matmul(packed[...], halving(512, 256)).reshape(n, 16, 256)


def inner(pe, re, ce, hx, hc, hy, hz, dg, rd, p1, p2, res, cmid, sums, packed):
    hc[0] = harmonic(ce[3], ce[4])

    def start(side, carry):
        for t in range(4):
            x = slab_x(side, t)
            c = ce[x]
            xm = hc[0] if t == 0 else hx[side, t - 1]
            xp = None
            if t < 3:
                xp = harmonic(c, ce[slab_x(side, t + 1)])
                hx[side, t] = xp
            hyt, hzt, d = first_weights(c, xp, xm)
            hy[side, t], hz[side, t], dg[side, t] = hyt, hzt, d
            if t < 3:
                r = inverse(d)
                rd[side, t] = r
                v = pe[x]
                image = operate(d, v, xp, pe[slab_x(side, t + 1)], xm, pe[slab_x(side, t - 1)], hyt, hzt)
                p1[side, t] = v + (re[x] - image) * r
        for q in range(2):
            pair_sums(sums, jnp.where(side == 0, 1 - q, 2 + q),
                      ce[slab_x(side, 2 * q)], ce[slab_x(side, 2 * q + 1)], 0.125)
        return carry

    lax.fori_loop(0, 2, start, 0)

    def image(side, t, p):
        xm, pm = (hc[0], p[1 - side, 0]) if t == 0 else (hx[side, t - 1], p[side, t - 1])
        return operate(dg[side, t], p[side, t], hx[side, t], p[side, t + 1], xm, pm, hy[side, t], hz[side, t])

    def second(side, carry):
        for t in range(2):
            p2[side, t] = p1[side, t] + (re[slab_x(side, t)] - image(side, t, p1)) * rd[side, t]
        return carry

    lax.fori_loop(0, 2, second, 0)

    def third(side, carry):
        res[side] = re[slab_x(side, 0)] - image(side, 0, p2)
        return carry

    lax.fori_loop(0, 2, third, 0)
    cmid[...] = halve_fine(sums, packed, 4)


def unpack(ref, p0, rs, c, side):
    row = 0
    for dst, tiles in ((p0, PHI_TILES), (rs, RHS_TILES), (c, COEF_TILES)):
        for k, n in enumerate(tiles):
            parts = [ref[row + 8 * t:row + 8 * t + 8, :] for t in range(n)]
            row += 8 * n
            if n == 1:
                parts += [jnp.zeros((8, 512), F32)] * 2
            if n == 2:
                parts += [parts[1]]
            for t in range(3):
                dst[side, k + 1, 8 * t:8 * t + 8, :] = parts[t]


def outer(pe, re, ce, hx, hc, hy, hz, dg, rd, p1, p2, res, other, mate, phi_out, smid, chalo,
          p0h, rsh, ch, hxh, hyh, hzh, dgh, rdh, p1h, p2h, resh, own, sums, packed, left):
    first = is_first()
    near = jnp.where(first, 1, 0)
    unpack(mate, p0h, rsh, ch, near)
    unpack(other, p0h, rsh, ch, 1 - near)

    def sweeps(side, carry):
        x0 = slab_x(side, 3)
        p0h[side, 0], rsh[side, 0], ch[side, 0] = pe[x0], re[x0], ce[x0]
        c = ch[side, 0]
        xp = harmonic(c, ch[side, 1])
        d = dg[side, 3] + weight(xp, c)
        r = inverse(d)
        hxh[side, 0], hyh[side, 0], hzh[side, 0], dgh[side, 0], rdh[side, 0] = xp, hy[side, 3], hz[side, 3], d, r
        v = p0h[side, 0]
        image = operate(d, v, xp, p0h[side, 1], hx[side, 2], pe[slab_x(side, 2)], hy[side, 3], hz[side, 3])
        p1h[side, 0] = v + (rsh[side, 0] - image) * r

        def start(j, carry):
            c = ch[side, j]
            xp, xm = harmonic(c, ch[side, j + 1]), hxh[side, j - 1]
            hyj, hzj, d = first_weights(c, xp, xm)
            r = inverse(d)
            hxh[side, j], hyh[side, j], hzh[side, j], dgh[side, j], rdh[side, j] = xp, hyj, hzj, d, r
            v = p0h[side, j]
            image = operate(d, v, xp, p0h[side, j + 1], xm, p0h[side, j - 1], hyj, hzj)
            p1h[side, j] = v + (rsh[side, j] - image) * r
            return carry

        lax.fori_loop(1, 7, start, 0, unroll=True)

        image = operate(dg[side, 2], p1[side, 2], hx[side, 2], p1h[side, 0], hx[side, 1], p1[side, 1],
                        hy[side, 2], hz[side, 2])
        p2h[side, 1] = p1[side, 2] + (re[slab_x(side, 2)] - image) * rd[side, 2]
        p2h[side, 0] = p2[side, 1]
        image = operate(dgh[side, 0], p1h[side, 0], hxh[side, 0], p1h[side, 1], hx[side, 2], p1[side, 2],
                        hyh[side, 0], hzh[side, 0])
        p2h[side, 2] = p1h[side, 0] + (rsh[side, 0] - image) * rdh[side, 0]

        def second(j, carry):
            v = p1h[side, j]
            image = operate(dgh[side, j], v, hxh[side, j], p1h[side, j + 1], hxh[side, j - 1], p1h[side, j - 1],
                            hyh[side, j], hzh[side, j])
            p2h[side, j + 2] = v + (rsh[side, j] - image) * rdh[side, j]
            return carry

        lax.fori_loop(1, 6, second, 0, unroll=True)
        for t in range(4):
            own[slab_x(side, t)] = (p2[side, t] if t < 2 else p2h[side, t - 1])[0:8, :]

        for t in (1, 2):
            image = operate(dg[side, t], p2h[side, t - 1], hx[side, t], p2h[side, t], hx[side, t - 1],
                            p2[side, 0] if t == 1 else p2h[side, 0], hy[side, t], hz[side, t])
            resh[side, t - 1] = re[slab_x(side, t)] - image
        image = operate(dgh[side, 0], p2h[side, 2], hxh[side, 0], p2h[side, 3], hx[side, 2], p2h[side, 1],
                        hyh[side, 0], hzh[side, 0])
        resh[side, 2] = rsh[side, 0] - image

        def third(j, carry):
            image = operate(dgh[side, j], p2h[side, j + 2], hxh[side, j], p2h[side, j + 3], hxh[side, j - 1],
                            p2h[side, j + 1], hyh[side, j], hzh[side, j])
            resh[side, j + 2] = rsh[side, j] - image
            return carry

        lax.fori_loop(1, 5, third, 0, unroll=True)
        for q in range(4):
            a = res[side] if q == 0 else resh[side, 2 * q - 1]
            pair_sums(sums, jnp.where(side == 0, 3 - q, 4 + q), a, resh[side, 2 * q], 0.5)
        for q in range(4):
            pair_sums(sums, 8 + jnp.where(side == 0, 3 - q, 4 + q), ch[side, 2 * q + 1], ch[side, 2 * q + 2], 0.125)
        return carry

    lax.fori_loop(0, 2, sweeps, 0)
    store = pltpu.make_async_copy(own, phi_out, left.at[0])
    store.start()
    mid = halve_fine(sums, packed, 16)
    smid[...] = mid[0:8]
    chalo[...] = mid[8:16]
    store.wait()


def middle(smid, cmid, chalo, emid, out, sums):
    s = [smid[j] for j in range(8)]
    c = [chalo[j] for j in range(4)] + [cmid[j] for j in range(4)] + [chalo[j] for j in range(4, 8)]
    hx = [harmonic(c[j], c[j + 1]) for j in range(1, 10)]
    hy, hz, d, r, e1 = [], [], [], [], []
    for i in range(8):
        ci = c[i + 2]
        hy.append(harmonic(ci, along(ci, 0, 1)))
        hz.append(z_face(ci))
        d.append(diagonal_of(ci, hx[i + 1], hx[i], hy[i], hz[i]))
        r.append(inverse(d[i]))
        e1.append(s[i] * r[i])

    def image(i, e):
        return operate(d[i], e[i], hx[i + 1], e[i + 1], hx[i], e[i - 1], hy[i], hz[i])

    e2 = [None] + [e1[i] + (s[i] - image(i, e1)) * r[i] for i in range(1, 7)] + [None]
    res = [s[i] - image(i, e2) for i in range(2, 6)]
    for x in range(4):
        emid[x] = e2[2 + x][0:4, :]
    groups = [(res[2 * x] + res[2 * x + 1]) * 0.5 for x in range(2)]
    groups += [(c[2 * x] + c[2 * x + 1]) * 0.125 for x in range(6)]
    for g in range(8):
        both = (groups[g] + along(groups[g], 0, 1))[0:8, :]
        sums[8 * g:8 * g + 8, :] = both[:, 0:128]
        sums[64 + 8 * g:72 + 8 * g, :] = both[:, 128:256]

    def rows(y):
        return jnp.concatenate([sums[pl.ds(64 * q + 2 * y, 8, stride=8), :] for q in range(2)], axis=1)

    low0 = matmul(rows(0), halving(256, 128))
    low1 = matmul(rows(1), halving(256, 128))
    for n in range(16):
        out[n, 0:8, :] = low0
        out[n, 8:16, :] = low1


def y_face(c):
    n = c.shape[0]
    return harmonic(c, jnp.where(positions(c.shape, 0) < n - 1, along(c, 0, 1), 0.0))


def low(gathered, elow, out, scol, ccol, sums):
    for g in range(8):
        for y in range(2):
            ref, k = (scol, g) if g < 2 else (ccol, g - 2)
            ref[pl.ds(32 * k + y, 16, stride=2), :] = gathered[pl.ds(8 * y + g, 16, stride=16), :]
    c = [ccol[32 * j:32 * j + 32, :] for j in range(6)]
    zero = jnp.zeros((32, 128), F32)
    s = [zero, zero, scol[0:32, :], scol[32:64, :], zero, zero]
    hx = [harmonic(c[j], c[j + 1]) for j in range(5)]
    hy, hz, d, r = [None], [None], [None], [None]
    for j in range(1, 5):
        hy.append(y_face(c[j]))
        hz.append(z_face(c[j]))
        d.append(diagonal_of(c[j], hx[j], hx[j - 1], hy[j], hz[j]))
        r.append(inverse(d[j]))
    e1 = [zero, zero, s[2] * r[2], s[3] * r[3], zero, zero]

    def image(j, e):
        return operate(d[j], e[j], hx[j], e[j + 1], hx[j - 1], e[j - 1], hy[j], hz[j])

    e2 = [zero, hx[1] * e1[2] * r[1]]
    e2 += [e1[j] + (s[j] - image(j, e1)) * r[j] for j in (2, 3)]
    e2 += [hx[3] * e1[3] * r[4], zero]
    res = [hx[0] * e2[1]] + [s[j] - image(j, e2) for j in range(1, 5)] + [hx[4] * e2[4]]

    quads = [(res[2] + res[3]) * 0.5, (c[2] + c[3]) * 0.125, (res[0] + res[1]) * 0.5, (res[4] + res[5]) * 0.5]
    for k in range(4):
        sums[32 * k:32 * k + 32, :] = quads[k] + along(quads[k], 0, 1)
    rows = [sums[pl.ds(32 * k, 16, stride=2), :] for k in range(4)]
    both = matmul(jnp.concatenate([jnp.concatenate(rows[0:2], axis=1), jnp.concatenate(rows[2:4], axis=1)], axis=0),
                  halving(256, 128))
    row = positions((32, 128), 0) - 2 * lax.axis_index("gy")
    errors = [jnp.sum(jnp.where(row == y, e2[j], 0.0), axis=0, keepdims=True) for j in (2, 3, 1, 4) for y in range(2)]
    errors = jnp.concatenate(errors, axis=0)
    elow[...] = errors
    for n in range(32):
        out[n, 0:32, :] = both
        out[n, 32:40, :] = errors


def bottom(gathered, elow, emid, out, hx, hy, hz, dg, sol, res, dire, img):
    half = positions((16, 128), 1) < 64
    last_z = positions((16, 128), 1) % 64 == 63
    last_y = positions((16, 128), 0) == 15
    c = []
    for x in range(16):
        a, b = gathered[x, 0:16, :], gathered[x + 16, 0:16, :]
        source = jnp.where(half, a, along(b, 1, 64))
        c.append(jnp.where(half, along(a, 1, 64), b))
        b = along(gathered[x + 17, 16:32, :], 1, 64) if x < 15 else 0.0
        source = source + jnp.where(half, gathered[x + 1, 16:32, :], b)
        a = along(gathered[x - 1, 16:32, :], 1, 64) if x > 0 else 0.0
        source = source + jnp.where(half, a, gathered[x + 15, 16:32, :])
        res[x] = source
        dire[x] = source
        sol[x] = jnp.zeros((16, 128), F32)
    for x in range(16):
        nxt = c[x + 1] if x < 15 else jnp.where(half, along(c[0], 1, 64), 0.0)
        hx[x + 1] = harmonic(c[x], nxt)
    hx[0] = along(hx[16], 1, 64)
    for x in range(16):
        hy[x] = harmonic(c[x], jnp.where(last_y, 0.0, along(c[x], 0, 1)))
        hz[x] = harmonic(c[x], jnp.where(last_z, 0.0, along(c[x], 1, 1)))
        dg[x] = diagonal_of(c[x], hx[x + 1], hx[x], hy[x], hz[x])

    def total(acc):
        return jnp.sum(jnp.sum(acc, axis=0, keepdims=True), axis=1, keepdims=True)

    def dot_image():
        acc = jnp.zeros((16, 128), F32)
        for x in range(16):
            v = dire[x]
            vp = dire[x + 1] if x < 15 else along(dire[0], 1, 64)
            vm = dire[x - 1] if x > 0 else along(dire[15], 1, 64)
            image = operate(dg[x], v, hx[x + 1], vp, hx[x], vm, hy[x], hz[x])
            img[x] = image
            acc = acc + v * image
        return total(acc)

    def norm():
        acc = jnp.zeros((16, 128), F32)
        for x in range(16):
            acc = acc + res[x] * res[x]
        return total(acc)

    def step(_, rr):
        alpha = rr / dot_image()
        acc = jnp.zeros((16, 128), F32)
        for x in range(16):
            sol[x] = sol[x] + alpha * dire[x]
            rx = res[x] - alpha * img[x]
            res[x] = rx
            acc = acc + rx * rx
        new = total(acc)
        beta = new / rr
        for x in range(16):
            dire[x] = res[x] + beta * dire[x]
        return new

    rr = lax.fori_loop(0, BOTTOM - 1, step, norm())
    gx, gy = lax.axis_index("gx"), lax.axis_index("gy")
    xi = lax.rem(gx, 16)
    alpha = rr / dot_image()
    mine = sol[xi] + alpha * dire[xi]
    mine = jnp.where(gx >= 16, along(mine, 1, 64), mine)
    row = positions((16, 128), 0)
    mine = jnp.sum(jnp.where(row == gy, mine, 0.0), axis=0, keepdims=True)
    after = jnp.where(gx < 31, gathered[jnp.minimum(gx + 1, 31), 32:40, :], 0.0)
    before = jnp.where(gx > 0, gathered[jnp.maximum(gx - 1, 0), 32:40, :], 0.0)
    lows = elow[0:4, :] + jnp.concatenate([before[6:8, :], after[4:6, :]], axis=0)
    coarse = matmul(jnp.broadcast_to(mine, (8, 128)), doubling(128, 256, 4))
    finer = matmul(jnp.concatenate([lows, lows], axis=0), doubling(128, 256, 2))
    for x in range(4):
        k = 2 * (x // 2)
        for y in range(4):
            add = finer[k + y // 2:k + y // 2 + 1, :] + coarse[0:1, :]
            out[x, y:y + 1, :] = emid[x, y:y + 1, :] + add


def swaps(near, far, axis):
    n = lax.axis_size(axis)
    pairs = [(i, i + 1) for i in range(1, n - 1, 2)] + [(i + 1, i) for i in range(1, n - 1, 2)]
    far = lax.ppermute(far, axis, pairs)
    return lax.ppermute(near, axis, [(i, i ^ 1) for i in range(n)]), far


def shards(phi_start, right_side, coefficient):
    own = [a.reshape(64, 512) for a in (phi_start, right_side, coefficient)]
    near, far = call(
        pack_y, [(8 * NROWS, 512)] * 2, [(64, 512)] * 3 + [(768, 128), (2, 8 * NROWS, 512)],
        n_in=3, copies=9, in_hbm=3, out_hbm=2, limit=64000000)(*own)
    near, far = swaps(near, far, "gy")
    *ext, mate, other = call(pack_x, [(192, 512)] * 3 + [(END_ROWS, 512)] * 2, [(1536, 128)], n_in=5)(*own, far, near)
    mate, other = swaps(mate, other, "gx")
    ext = [a.reshape(8, 24, 512) for a in ext]

    def slabs(*n):
        return (*n, 24, 512)

    *inside, cmid = call(
        inner,
        [slabs(2, 3), slabs(1)] + [slabs(2, 4)] * 3 + [slabs(2, 3)] * 2 + [slabs(2, 2), slabs(2), (4, 16, 256)],
        [(4, 4, 24, 128), (64, 512)], n_in=3,
        cost=pl.CostEstimate(flops=16_000_000, bytes_accessed=4_000_000, transcendentals=0),
    )(*ext)
    phi_fine, smid, chalo = call(
        outer,
        [(8, 8, 512), (8, 16, 256), (8, 16, 256)],
        [slabs(2, 9)] * 11 + [(8, 8, 512), (4, 16, 24, 128), (256, 512)],
        n_in=14, copies=1, out_hbm=1,
    )(*ext, *inside, other, mate)
    emid, spread = call(middle, [(4, 4, 256), (16, 16, 128)], [(128, 128)], n_in=3)(smid, cmid, chalo)
    gathered = lax.all_to_all(spread, "gy", 0, 0, tiled=True)
    elow, spread = call(low, [(8, 128), (32, 40, 128)], [(64, 128), (192, 128), (128, 128)], n_in=1)(
        gathered.reshape(256, 128))
    gathered = lax.all_to_all(spread, "gx", 0, 0, tiled=True)
    (correction,) = call(bottom, [(4, 4, 256)], [(17, 16, 128)] + [(16, 16, 128)] * 7, n_in=3)(
        gathered, elow, emid)
    return phi_fine, correction


def solution(mesh):
    return jax.shard_map(
        shards,
        mesh=mesh,
        in_specs=(P("gx", "gy", None),) * 3,
        out_specs=(P("gx", "gy", None),) * 2,
        check_vma=False,
    )
```

```python
import jax
import jax.numpy as jnp
from jax import lax
from jax.experimental import pallas as pl
from jax.experimental.pallas import tpu as pltpu
from jax.sharding import PartitionSpec as P

BOTTOM = 6
RELAX_WEIGHT = 0.8
FLOOR = 1e-3
F32 = jnp.float32
VMEM = pl.BlockSpec(memory_space=pltpu.VMEM)
HBM = pl.BlockSpec(memory_space=pltpu.HBM)


def call(kernel, out_shapes, scratch=(), n_in=0, copies=0, in_hbm=0, out_hbm=0, limit=24 * 1024 * 1024, cost=None):
    semaphores = [pltpu.SemaphoreType.DMA((copies,))] if copies else []
    return pl.pallas_call(
        kernel,
        out_shape=[jax.ShapeDtypeStruct(s, F32) for s in out_shapes],
        in_specs=[HBM] * in_hbm + [VMEM] * (n_in - in_hbm),
        out_specs=[HBM] * out_hbm + [VMEM] * (len(out_shapes) - out_hbm),
        scratch_shapes=[pltpu.VMEM(s, F32) for s in scratch] + semaphores,
        compiler_params=pltpu.CompilerParams(vmem_limit_bytes=limit),
        cost_estimate=cost,
    )


def reciprocal(x):
    r = pl.reciprocal(x, approx=True)
    return r * (2.0 - x * r)


def harmonic(a, b):
    return 2.0 * a * b * reciprocal(jnp.maximum(a + b, FLOOR))


def along(v, axis, step):
    n = v.shape[axis]
    return pltpu.roll(v, (-step) % n, axis)


def is_first():
    return lax.rem(lax.axis_index("gx"), 2) == 0


def positions(shape, axis):
    return lax.broadcasted_iota(jnp.int32, shape, axis)


def halving(rows, cols):
    return (positions((rows, cols), 0) // 2 == positions((rows, cols), 1)).astype(F32)


def doubling(rows, cols, factor):
    return (positions((rows, cols), 1) // factor == positions((rows, cols), 0)).astype(F32)


def matmul(a, b):
    return exact_matmul(a, b)


def exact_matmul(a, ones):
    parts = []
    for _ in range(3):
        parts.append(a.astype(jnp.bfloat16))
        a = a - parts[-1].astype(F32)
    ones = ones.astype(jnp.bfloat16)
    return sum(jnp.dot(p, ones, preferred_element_type=F32) for p in reversed(parts))


def weight(face, centre):
    return jnp.where(face > 0.0, face, centre)


def diagonal_of(c, xp, xm, hy, hz):
    return (weight(xp, c) + weight(xm, c) + weight(hy, c) + weight(along(hy, 0, -1), c)
            + weight(hz, c) + weight(along(hz, 1, -1), c))


def operate(d, v, xp, vp, xm, vm, hy, hz):
    out = d * v - xp * vp - xm * vm
    out = out - hy * along(v, 0, 1) - along(hy * v, 0, -1)
    return out - hz * along(v, 1, 1) - along(hz * v, 1, -1)


def z_face(c):
    nxt = jnp.where(positions(c.shape, 1) < c.shape[1] - 1, along(c, 1, 1), 0.0)
    return harmonic(c, nxt)


NP, NR, NC = 7, 6, 7
NROWS = NP + NR + NC
PHI_TILES = (3, 3, 2, 2, 2, 2, 1)
RHS_TILES = (3, 2, 2, 2, 2, 1)
COEF_TILES = (3, 3, 2, 2, 2, 2, 1, 1)
END_ROWS = 8 * (sum(PHI_TILES) + sum(RHS_TILES) + sum(COEF_TILES))


def pack_y(phi_in, rhs_in, coef_in, near, far, phi, rhs, coef, stage, ends, sem):
    loads = [pltpu.make_async_copy(src, dst, sem.at[a])
             for a, (src, dst) in enumerate(((phi_in, phi), (rhs_in, rhs), (coef_in, coef)))]
    for load in loads:
        load.start()
    stores = []
    k = 0
    for a, (ref, n) in enumerate(((phi, NP), (rhs, NR), (coef, NC))):
        loads[a].wait()
        for q in range(4):
            lanes = slice(128 * q, 128 * q + 128)
            base = 64 * (4 * a + q)
            stage[base:base + 64, :] = ref[:, lanes]
            for j in range(n):
                rows = slice(8 * (k + j), 8 * (k + j) + 8)
                ends[0, rows, lanes] = stage[pl.ds(base + 8 - n + j, 8, stride=8), :]
                ends[1, rows, lanes] = stage[pl.ds(base + j, 8, stride=8), :]
        for b, dst in enumerate((near, far)):
            part = pl.ds(8 * k, 8 * n)
            src = ends.at[lax.rem(lax.axis_index("gy") + b, 2), part]
            stores.append(pltpu.make_async_copy(src, dst.at[part], sem.at[3 + 2 * a + b]))
            stores[-1].start()
        k += n
    for store in stores:
        store.wait()


def hold(*refs):
    for src, dst in zip(refs[:3], refs[3:]):
        dst[...] = src[...]


def pack_x(phi, rhs, coef, far, near, pe, re, ce, other, stage):
    zero = jnp.zeros((8, 128), F32)
    odd = lax.rem(lax.axis_index("gy"), 2)
    k = 0
    for a, (ref, ext, n) in enumerate(((phi, pe, NP), (rhs, re, NR), (coef, ce, NC))):
        for x in range(8):
            ext[24 * x:24 * x + 8, :] = ref[8 * x:8 * x + 8, :]
        for q in range(4):
            lanes = slice(128 * q, 128 * q + 128)
            base = 128 * (4 * a + q)
            for j in range(n):
                rows = slice(8 * (k + j), 8 * (k + j) + 8)
                stage[pl.ds(base + j + odd * (16 - n), 8, stride=16), :] = near[rows, lanes]
                stage[pl.ds(base + j + (1 - odd) * (16 - n), 8, stride=16), :] = far[rows, lanes]
            for j in range(n, 16 - n):
                stage[pl.ds(base + j, 8, stride=16), :] = zero
            for x in range(8):
                ext[24 * x + 8:24 * x + 24, lanes] = stage[base + 16 * x:base + 16 * x + 16, :]
        k += n
    first = is_first()
    pack_end(other, lambda ext, x, t: ext[pl.ds(pl.multiple_of(24 * x + 8 * t, 8), 8), :], pe, re, ce, first)


def pack_end(out, tile, pe, re, ce, is_low):
    top = positions((8, 512), 0) < 4
    row = 0
    for ext, tiles in ((pe, PHI_TILES), (re, RHS_TILES), (ce, COEF_TILES)):
        for k, n in enumerate(tiles):
            x = jnp.where(is_low, k, 7 - k)
            parts = [tile(ext, x, t) for t in range(min(n + n // 2, 3))]
            if n == 2:
                parts = [parts[0], jnp.where(top, parts[1], parts[2])]
            for part in parts:
                out[row:row + 8, :] = part
                row += 8


def slab_x(side, t):
    return jnp.where(side == 0, 3 - t, 4 + t)


def first_weights(c, xp, xm):
    hy = harmonic(c, along(c, 0, 1))
    hz = z_face(c)
    d = weight(xm, c) + weight(hy, c) + weight(along(hy, 0, -1), c) + weight(hz, c) + weight(along(hz, 1, -1), c)
    return hy, hz, d if xp is None else d + weight(xp, c)


def inverse(d):
    return RELAX_WEIGHT * reciprocal(jnp.maximum(d, FLOOR))


def pair_sums(sums, place, a, b, scale):
    t = a + b
    t = (t + along(t, 0, 1)) * scale
    for q in range(4):
        sums[q, place] = t[:, 128 * q:128 * q + 128]


def halve_fine(sums, packed, n):
    for k in range(n):
        for q in range(4):
            lanes = slice(128 * q, 128 * q + 128)
            packed[16 * k:16 * k + 8, lanes] = sums[q, k, pl.ds(0, 8, stride=2), :]
            packed[16 * k + 8:16 * k + 12, lanes] = jnp.zeros((4, 128), F32)
            packed[16 * k + 12:16 * k + 16, lanes] = sums[q, k, pl.ds(16, 4, stride=2), :]
    return exact_matmul(packed[...], halving(512, 256)).reshape(n, 16, 256)


def inner(pe, re, ce, hx, hc, hy, hz, dg, rd, p1, p2, res, cmid, mate, sums, packed):
    first = is_first()
    block = mate.at[jnp.where(first, 1, 0)]
    pack_end(block, lambda ext, x, t: ext[x, 8 * t:8 * t + 8, :], pe, re, ce, jnp.logical_not(first))
    hc[0] = harmonic(ce[3], ce[4])

    def start(side, carry):
        for t in range(4):
            x = slab_x(side, t)
            c = ce[x]
            xm = hc[0] if t == 0 else hx[side, t - 1]
            xp = None
            if t < 3:
                xp = harmonic(c, ce[slab_x(side, t + 1)])
                hx[side, t] = xp
            hyt, hzt, d = first_weights(c, xp, xm)
            hy[side, t], hz[side, t], dg[side, t] = hyt, hzt, d
            if t < 3:
                r = inverse(d)
                rd[side, t] = r
                v = pe[x]
                image = operate(d, v, xp, pe[slab_x(side, t + 1)], xm, pe[slab_x(side, t - 1)], hyt, hzt)
                p1[side, t] = v + (re[x] - image) * r
        for q in range(2):
            pair_sums(sums, jnp.where(side == 0, 1 - q, 2 + q),
                      ce[slab_x(side, 2 * q)], ce[slab_x(side, 2 * q + 1)], 0.125)
        return carry

    lax.fori_loop(0, 2, start, 0)

    def image(side, t, p):
        xm, pm = (hc[0], p[1 - side, 0]) if t == 0 else (hx[side, t - 1], p[side, t - 1])
        return operate(dg[side, t], p[side, t], hx[side, t], p[side, t + 1], xm, pm, hy[side, t], hz[side, t])

    def second(side, carry):
        for t in range(2):
            p2[side, t] = p1[side, t] + (re[slab_x(side, t)] - image(side, t, p1)) * rd[side, t]
        return carry

    lax.fori_loop(0, 2, second, 0)

    def third(side, carry):
        res[side] = re[slab_x(side, 0)] - image(side, 0, p2)
        return carry

    lax.fori_loop(0, 2, third, 0)
    cmid[...] = halve_fine(sums, packed, 4)


def unpack(ref, p0, rs, c):
    row = 0
    for dst, tiles in ((p0, PHI_TILES), (rs, RHS_TILES), (c, COEF_TILES)):
        for k, n in enumerate(tiles):
            parts = [ref[row + 8 * t:row + 8 * t + 8, :] for t in range(n)]
            row += 8 * n
            if n == 1:
                parts += [jnp.zeros((8, 512), F32)] * 2
            if n == 2:
                parts += [parts[1]]
            for t in range(3):
                dst[k + 1, 8 * t:8 * t + 8, :] = parts[t]


def one_side(side, received, done, pe, re, ce, hx, hc, hy, hz, dg, rd, p1, p2, res, phi, half,
             p0h, rsh, ch, hxh, hyh, hzh, dgh, rdh, p1h, p2h, resh, sums, packed):
    unpack(received, p0h, rsh, ch)
    x0 = slab_x(side, 3)
    p0h[0], rsh[0], ch[0] = pe[x0], re[x0], ce[x0]
    c = ch[0]
    xp = harmonic(c, ch[1])
    d = dg[side, 3] + weight(xp, c)
    r = inverse(d)
    hxh[0], hyh[0], hzh[0], dgh[0], rdh[0] = xp, hy[side, 3], hz[side, 3], d, r
    v = p0h[0]
    image = operate(d, v, xp, p0h[1], hx[side, 2], pe[slab_x(side, 2)], hy[side, 3], hz[side, 3])
    p1h[0] = v + (rsh[0] - image) * r

    def start(j, carry):
        c = ch[j]
        xp, xm = harmonic(c, ch[j + 1]), hxh[j - 1]
        hyj, hzj, d = first_weights(c, xp, xm)
        r = inverse(d)
        hxh[j], hyh[j], hzh[j], dgh[j], rdh[j] = xp, hyj, hzj, d, r
        v = p0h[j]
        image = operate(d, v, xp, p0h[j + 1], xm, p0h[j - 1], hyj, hzj)
        p1h[j] = v + (rsh[j] - image) * r
        return carry

    lax.fori_loop(1, 7, start, 0, unroll=True)

    image = operate(dg[side, 2], p1[side, 2], hx[side, 2], p1h[0], hx[side, 1], p1[side, 1],
                    hy[side, 2], hz[side, 2])
    p2h[1] = p1[side, 2] + (re[slab_x(side, 2)] - image) * rd[side, 2]
    p2h[0] = p2[side, 1]
    image = operate(dgh[0], p1h[0], hxh[0], p1h[1], hx[side, 2], p1[side, 2],
                    hyh[0], hzh[0])
    p2h[2] = p1h[0] + (rsh[0] - image) * rdh[0]

    def second(j, carry):
        v = p1h[j]
        image = operate(dgh[j], v, hxh[j], p1h[j + 1], hxh[j - 1], p1h[j - 1],
                        hyh[j], hzh[j])
        p2h[j + 2] = v + (rsh[j] - image) * rdh[j]
        return carry

    lax.fori_loop(1, 6, second, 0, unroll=True)
    for t in range(4):
        phi[jnp.where(side == 0, 3 - t, t)] = (p2[side, t] if t < 2 else p2h[t - 1])[0:8, :]

    for t in (1, 2):
        image = operate(dg[side, t], p2h[t - 1], hx[side, t], p2h[t], hx[side, t - 1],
                        p2[side, 0] if t == 1 else p2h[0], hy[side, t], hz[side, t])
        resh[t - 1] = re[slab_x(side, t)] - image
    image = operate(dgh[0], p2h[2], hxh[0], p2h[3], hx[side, 2], p2h[1],
                    hyh[0], hzh[0])
    resh[2] = rsh[0] - image

    def third(j, carry):
        image = operate(dgh[j], p2h[j + 2], hxh[j], p2h[j + 3], hxh[j - 1],
                        p2h[j + 1], hyh[j], hzh[j])
        resh[j + 2] = rsh[j] - image
        return carry

    lax.fori_loop(1, 5, third, 0, unroll=True)
    if done is not None:
        done()
    for q in range(4):
        a = res[side] if q == 0 else resh[2 * q - 1]
        pair_sums(sums, q, a, resh[2 * q], 0.5)
        pair_sums(sums, 4 + q, ch[2 * q + 1], ch[2 * q + 2], 0.125)
    half[...] = halve_fine(sums, packed, 8)


def mate_side(*refs):
    inputs, received, rest = refs[:12], refs[12], refs[13:]
    side = jnp.where(is_first(), 1, 0)
    one_side(side, received.at[side], None, *inputs, *rest)


def other_side(*refs):
    inputs, (received, phi_mate, phi_out, half), scratch = refs[:12], refs[12:16], refs[16:-2]
    phi, left = refs[-2:]
    side = jnp.where(is_first(), 0, 1)
    stores = [pltpu.make_async_copy(src, phi_out.at[pl.ds(4 * at, 4)], left.at[k])
              for k, (src, at) in enumerate(((phi_mate, 1 - side), (phi, side)))]
    stores[0].start()
    one_side(side, received, stores[1].start, *inputs, phi, half, *scratch)
    for store in stores:
        store.wait()


def middle(mate, other, cmid, emid, out, sums):
    first = is_first()
    lo = [jnp.where(first, other[j], mate[j]) for j in range(8)]
    hi = [jnp.where(first, mate[j], other[j]) for j in range(8)]
    s = lo[3::-1] + hi[0:4]
    c = lo[:3:-1] + [cmid[j] for j in range(4)] + hi[4:8]
    hx = [harmonic(c[j], c[j + 1]) for j in range(1, 10)]
    hy, hz, d, r, e1 = [], [], [], [], []
    for i in range(8):
        ci = c[i + 2]
        hy.append(harmonic(ci, along(ci, 0, 1)))
        hz.append(z_face(ci))
        d.append(diagonal_of(ci, hx[i + 1], hx[i], hy[i], hz[i]))
        r.append(inverse(d[i]))
        e1.append(s[i] * r[i])

    def image(i, e):
        return operate(d[i], e[i], hx[i + 1], e[i + 1], hx[i], e[i - 1], hy[i], hz[i])

    e2 = [None] + [e1[i] + (s[i] - image(i, e1)) * r[i] for i in range(1, 7)] + [None]
    res = [s[i] - image(i, e2) for i in range(2, 6)]
    for x in range(4):
        emid[x] = e2[2 + x][0:4, :]
    groups = [(res[2 * x] + res[2 * x + 1]) * 0.5 for x in range(2)]
    groups += [(c[2 * x] + c[2 * x + 1]) * 0.125 for x in range(6)]
    for g in range(8):
        both = (groups[g] + along(groups[g], 0, 1))[0:8, :]
        sums[8 * g:8 * g + 8, :] = both[:, 0:128]
        sums[64 + 8 * g:72 + 8 * g, :] = both[:, 128:256]

    def rows(y):
        return jnp.concatenate([sums[pl.ds(64 * q + 2 * y, 8, stride=8), :] for q in range(2)], axis=1)

    low0 = matmul(rows(0), halving(256, 128))
    low1 = matmul(rows(1), halving(256, 128))
    for n in range(16):
        out[n, 0:8, :] = low0
        out[n, 8:16, :] = low1


def y_face(c):
    n = c.shape[0]
    return harmonic(c, jnp.where(positions(c.shape, 0) < n - 1, along(c, 0, 1), 0.0))


def low(gathered, elow, out, scol, ccol, sums):
    for g in range(8):
        for y in range(2):
            ref, k = (scol, g) if g < 2 else (ccol, g - 2)
            ref[pl.ds(32 * k + y, 16, stride=2), :] = gathered[pl.ds(8 * y + g, 16, stride=16), :]
    c = [ccol[32 * j:32 * j + 32, :] for j in range(6)]
    zero = jnp.zeros((32, 128), F32)
    s = [zero, zero, scol[0:32, :], scol[32:64, :], zero, zero]
    hx = [harmonic(c[j], c[j + 1]) for j in range(5)]
    hy, hz, d, r = [None], [None], [None], [None]
    for j in range(1, 5):
        hy.append(y_face(c[j]))
        hz.append(z_face(c[j]))
        d.append(diagonal_of(c[j], hx[j], hx[j - 1], hy[j], hz[j]))
        r.append(inverse(d[j]))
    e1 = [zero, zero, s[2] * r[2], s[3] * r[3], zero, zero]

    def image(j, e):
        return operate(d[j], e[j], hx[j], e[j + 1], hx[j - 1], e[j - 1], hy[j], hz[j])

    e2 = [zero, hx[1] * e1[2] * r[1]]
    e2 += [e1[j] + (s[j] - image(j, e1)) * r[j] for j in (2, 3)]
    e2 += [hx[3] * e1[3] * r[4], zero]
    res = [hx[0] * e2[1]] + [s[j] - image(j, e2) for j in range(1, 5)] + [hx[4] * e2[4]]

    quads = [(res[2] + res[3]) * 0.5, (c[2] + c[3]) * 0.125, (res[0] + res[1]) * 0.5, (res[4] + res[5]) * 0.5]
    for k in range(4):
        sums[32 * k:32 * k + 32, :] = quads[k] + along(quads[k], 0, 1)
    rows = [sums[pl.ds(32 * k, 16, stride=2), :] for k in range(4)]
    both = matmul(jnp.concatenate([jnp.concatenate(rows[0:2], axis=1), jnp.concatenate(rows[2:4], axis=1)], axis=0),
                  halving(256, 128))
    row = positions((32, 128), 0) - 2 * lax.axis_index("gy")
    errors = [jnp.sum(jnp.where(row == y, e2[j], 0.0), axis=0, keepdims=True) for j in (2, 3, 1, 4) for y in range(2)]
    errors = jnp.concatenate(errors, axis=0)
    elow[...] = errors
    for n in range(32):
        out[n, 0:32, :] = both
        out[n, 32:40, :] = errors


def bottom(gathered, elow, emid, out, hx, hy, hz, dg, sol, res, dire, img):
    half = positions((16, 128), 1) < 64
    last_z = positions((16, 128), 1) % 64 == 63
    last_y = positions((16, 128), 0) == 15
    c = []
    for x in range(16):
        a, b = gathered[x, 0:16, :], gathered[x + 16, 0:16, :]
        source = jnp.where(half, a, along(b, 1, 64))
        c.append(jnp.where(half, along(a, 1, 64), b))
        b = along(gathered[x + 17, 16:32, :], 1, 64) if x < 15 else 0.0
        source = source + jnp.where(half, gathered[x + 1, 16:32, :], b)
        a = along(gathered[x - 1, 16:32, :], 1, 64) if x > 0 else 0.0
        source = source + jnp.where(half, a, gathered[x + 15, 16:32, :])
        res[x] = source
        dire[x] = source
        sol[x] = jnp.zeros((16, 128), F32)
    for x in range(16):
        nxt = c[x + 1] if x < 15 else jnp.where(half, along(c[0], 1, 64), 0.0)
        hx[x + 1] = harmonic(c[x], nxt)
    hx[0] = along(hx[16], 1, 64)
    for x in range(16):
        hy[x] = harmonic(c[x], jnp.where(last_y, 0.0, along(c[x], 0, 1)))
        hz[x] = harmonic(c[x], jnp.where(last_z, 0.0, along(c[x], 1, 1)))
        dg[x] = diagonal_of(c[x], hx[x + 1], hx[x], hy[x], hz[x])

    def total(acc):
        return jnp.sum(jnp.sum(acc, axis=0, keepdims=True), axis=1, keepdims=True)

    def dot_image():
        acc = jnp.zeros((16, 128), F32)
        for x in range(16):
            v = dire[x]
            vp = dire[x + 1] if x < 15 else along(dire[0], 1, 64)
            vm = dire[x - 1] if x > 0 else along(dire[15], 1, 64)
            image = operate(dg[x], v, hx[x + 1], vp, hx[x], vm, hy[x], hz[x])
            img[x] = image
            acc = acc + v * image
        return total(acc)

    def norm():
        acc = jnp.zeros((16, 128), F32)
        for x in range(16):
            acc = acc + res[x] * res[x]
        return total(acc)

    def step(_, rr):
        alpha = rr / dot_image()
        acc = jnp.zeros((16, 128), F32)
        for x in range(16):
            sol[x] = sol[x] + alpha * dire[x]
            rx = res[x] - alpha * img[x]
            res[x] = rx
            acc = acc + rx * rx
        new = total(acc)
        beta = new / rr
        for x in range(16):
            dire[x] = res[x] + beta * dire[x]
        return new

    gx, gy = lax.axis_index("gx"), lax.axis_index("gy")
    after = jnp.where(gx < 31, gathered[jnp.minimum(gx + 1, 31), 32:40, :], 0.0)
    before = jnp.where(gx > 0, gathered[jnp.maximum(gx - 1, 0), 32:40, :], 0.0)
    lows = elow[0:4, :] + jnp.concatenate([before[6:8, :], after[4:6, :]], axis=0)
    finer = matmul(jnp.concatenate([lows, lows], axis=0), doubling(128, 256, 2))
    rr = lax.fori_loop(0, BOTTOM - 1, step, norm(), unroll=True)
    xi = lax.rem(gx, 16)
    alpha = rr / dot_image()
    mine = sol[xi] + alpha * dire[xi]
    mine = jnp.where(gx >= 16, along(mine, 1, 64), mine)
    row = positions((16, 128), 0)
    mine = jnp.sum(jnp.where(row == gy, mine, 0.0), axis=0, keepdims=True)
    coarse = matmul(jnp.broadcast_to(mine, (8, 128)), doubling(128, 256, 4))
    for x in range(4):
        k = 2 * (x // 2)
        for y in range(4):
            add = finer[k + y // 2:k + y // 2 + 1, :] + coarse[0:1, :]
            out[x, y:y + 1, :] = emid[x, y:y + 1, :] + add


def swap(values, axis, far):
    n = lax.axis_size(axis)
    pairs = [(i, i + 1) for i in range(int(far), n - 1, 2)]
    return lax.ppermute(values, axis, pairs + [(j, i) for i, j in pairs])


def shards(phi_start, right_side, coefficient):
    own = [a.reshape(64, 512) for a in (phi_start, right_side, coefficient)]
    near, far = call(
        pack_y, [(8 * NROWS, 512)] * 2, [(64, 512)] * 3 + [(768, 128), (2, 8 * NROWS, 512)],
        n_in=3, copies=9, in_hbm=3, out_hbm=2, limit=64000000)(*own)
    far = swap(far, "gy", True)
    near = swap(near, "gy", False)
    own = call(hold, [(64, 512)] * 3, n_in=3,
               cost=pl.CostEstimate(flops=16_000_000, bytes_accessed=4_000_000, transcendentals=0))(*own)
    *ext, other = call(pack_x, [(192, 512)] * 3 + [(END_ROWS, 512)], [(1536, 128)], n_in=5)(*own, far, near)
    other = swap(other, "gx", True)
    ext = [a.reshape(8, 24, 512) for a in ext]

    def slabs(*n):
        return (*n, 24, 512)

    *inside, cmid, mate = call(
        inner,
        [slabs(2, 3), slabs(1)] + [slabs(2, 4)] * 3 + [slabs(2, 3)] * 2 + [slabs(2, 2), slabs(2), (4, 16, 256), (2, END_ROWS, 512)],
        [(4, 4, 24, 128), (64, 512)], n_in=3,
        cost=pl.CostEstimate(flops=1_000, bytes_accessed=1_000, transcendentals=0),
    )(*ext)
    chips = [[i, i + 1] for i in range(0, lax.axis_size("gx"), 2)]
    mate = lax.all_to_all(mate, "gx", 0, 0, tiled=True, axis_index_groups=chips)
    scratch = [slabs(9)] * 11 + [(4, 8, 24, 128), (128, 512)]
    phi_half, half = call(
        mate_side, [(4, 8, 512), (8, 16, 256)], scratch, n_in=13,
        cost=pl.CostEstimate(flops=1_000, bytes_accessed=1_000, transcendentals=0),
    )(*ext, *inside, mate)
    phi_fine, other_half = call(
        other_side, [(8, 8, 512), (8, 16, 256)], scratch + [(4, 8, 512)], n_in=14, copies=2, out_hbm=1,
    )(*ext, *inside, other, phi_half)
    emid, spread = call(middle, [(4, 4, 256), (16, 16, 128)], [(128, 128)], n_in=3)(half, other_half, cmid)
    gathered = lax.all_to_all(spread, "gy", 0, 0, tiled=True)
    elow, spread = call(low, [(8, 128), (32, 40, 128)], [(64, 128), (192, 128), (128, 128)], n_in=1)(
        gathered.reshape(256, 128))
    gathered = lax.all_to_all(spread, "gx", 0, 0, tiled=True)
    (correction,) = call(bottom, [(4, 4, 256)], [(17, 16, 128)] + [(16, 16, 128)] * 7, n_in=3)(
        gathered, elow, emid)
    return phi_fine, correction


def solution(mesh):
    return jax.shard_map(
        shards,
        mesh=mesh,
        in_specs=(P("gx", "gy", None),) * 3,
        out_specs=(P("gx", "gy", None),) * 2,
        check_vma=False,
    )
```

```python
import jax
import jax.numpy as jnp
from jax import lax
from jax.experimental import pallas as pl
from jax.experimental.pallas import tpu as pltpu
from jax.sharding import PartitionSpec as P

BOTTOM = 6
RELAX_WEIGHT = 0.8
FLOOR = 1e-3
F32 = jnp.float32
VMEM = pl.BlockSpec(memory_space=pltpu.VMEM)
HBM = pl.BlockSpec(memory_space=pltpu.HBM)


def call(kernel, out_shapes, scratch=(), n_in=0, copies=0, in_hbm=0, out_hbm=0, limit=24 * 1024 * 1024, cost=None):
    semaphores = [pltpu.SemaphoreType.DMA((copies,))] if copies else []
    return pl.pallas_call(
        kernel,
        out_shape=[jax.ShapeDtypeStruct(s, F32) for s in out_shapes],
        in_specs=[HBM] * in_hbm + [VMEM] * (n_in - in_hbm),
        out_specs=[HBM] * out_hbm + [VMEM] * (len(out_shapes) - out_hbm),
        scratch_shapes=[pltpu.VMEM(s, F32) for s in scratch] + semaphores,
        compiler_params=pltpu.CompilerParams(vmem_limit_bytes=limit),
        cost_estimate=cost,
    )


def reciprocal(x):
    r = pl.reciprocal(x, approx=True)
    return r * (2.0 - x * r)


def harmonic(a, b):
    return 2.0 * a * b * reciprocal(jnp.maximum(a + b, FLOOR))


def along(v, axis, step):
    n = v.shape[axis]
    return pltpu.roll(v, (-step) % n, axis)


def is_first():
    return lax.rem(lax.axis_index("gx"), 2) == 0


def positions(shape, axis):
    return lax.broadcasted_iota(jnp.int32, shape, axis)


def halving(rows, cols):
    return (positions((rows, cols), 0) // 2 == positions((rows, cols), 1)).astype(F32)


def doubling(rows, cols, factor):
    return (positions((rows, cols), 1) // factor == positions((rows, cols), 0)).astype(F32)


def matmul(a, b):
    return exact_matmul(a, b)


def exact_matmul(a, ones):
    parts = []
    for _ in range(3):
        parts.append(a.astype(jnp.bfloat16))
        a = a - parts[-1].astype(F32)
    ones = ones.astype(jnp.bfloat16)
    return sum(jnp.dot(p, ones, preferred_element_type=F32) for p in reversed(parts))


def weight(face, centre):
    return jnp.where(face > 0.0, face, centre)


def diagonal_of(c, xp, xm, hy, hz):
    return (weight(xp, c) + weight(xm, c) + weight(hy, c) + weight(along(hy, 0, -1), c)
            + weight(hz, c) + weight(along(hz, 1, -1), c))


def operate(d, v, xp, vp, xm, vm, hy, hz):
    out = d * v - xp * vp - xm * vm
    out = out - hy * along(v, 0, 1) - along(hy * v, 0, -1)
    return out - hz * along(v, 1, 1) - along(hz * v, 1, -1)


def z_face(c):
    nxt = jnp.where(positions(c.shape, 1) < c.shape[1] - 1, along(c, 1, 1), 0.0)
    return harmonic(c, nxt)


NP, NR, NC = 7, 6, 7
NROWS = NP + NR + NC
PHI_TILES = (2, 2, 2, 2, 2, 2, 1)
RHS_TILES = (2, 2, 2, 2, 2, 1)
COEF_TILES = (2, 2, 2, 2, 2, 2, 1, 1)
PHI_MORE = 8 * (sum(PHI_TILES) + sum(RHS_TILES) + sum(COEF_TILES))
COEF_MORE = PHI_MORE + 8
END_ROWS = PHI_MORE + 16


def pack_y(phi_in, rhs_in, coef_in, near, far, phi, rhs, coef, stage, ends, sem):
    loads = [pltpu.make_async_copy(src, dst, sem.at[a])
             for a, (src, dst) in enumerate(((phi_in, phi), (rhs_in, rhs), (coef_in, coef)))]
    for load in loads:
        load.start()
    stores = []
    k = 0
    for a, (ref, n) in enumerate(((phi, NP), (rhs, NR), (coef, NC))):
        loads[a].wait()
        for q in range(4):
            lanes = slice(128 * q, 128 * q + 128)
            base = 64 * (4 * a + q)
            stage[base:base + 64, :] = ref[:, lanes]
            for j in range(n):
                rows = slice(8 * (k + j), 8 * (k + j) + 8)
                ends[0, rows, lanes] = stage[pl.ds(base + 8 - n + j, 8, stride=8), :]
                ends[1, rows, lanes] = stage[pl.ds(base + j, 8, stride=8), :]
        for b, dst in enumerate((near, far)):
            part = pl.ds(8 * k, 8 * n)
            src = ends.at[lax.rem(lax.axis_index("gy") + b, 2), part]
            stores.append(pltpu.make_async_copy(src, dst.at[part], sem.at[3 + 2 * a + b]))
            stores[-1].start()
        k += n
    for store in stores:
        store.wait()


def hold(*refs):
    for src, dst in zip(refs[:3], refs[3:]):
        dst[...] = src[...]


def pack_x(phi, rhs, coef, far, near, pe, re, ce, other, stage):
    zero = jnp.zeros((8, 128), F32)
    odd = lax.rem(lax.axis_index("gy"), 2)
    k = 0
    for a, (ref, ext, n) in enumerate(((phi, pe, NP), (rhs, re, NR), (coef, ce, NC))):
        for x in range(8):
            ext[24 * x:24 * x + 8, :] = ref[8 * x:8 * x + 8, :]
        for q in range(4):
            lanes = slice(128 * q, 128 * q + 128)
            base = 128 * (4 * a + q)
            for j in range(n):
                rows = slice(8 * (k + j), 8 * (k + j) + 8)
                stage[pl.ds(base + j + odd * (16 - n), 8, stride=16), :] = near[rows, lanes]
                stage[pl.ds(base + j + (1 - odd) * (16 - n), 8, stride=16), :] = far[rows, lanes]
            for j in range(n, 16 - n):
                stage[pl.ds(base + j, 8, stride=16), :] = zero
            for x in range(8):
                ext[24 * x + 8:24 * x + 24, lanes] = stage[base + 16 * x:base + 16 * x + 16, :]
        k += n
    first = is_first()
    pack_end(other, lambda ext, x, t: ext[pl.ds(pl.multiple_of(24 * x + 8 * t, 8), 8), :], pe, re, ce, first)


def pack_end(out, tile, pe, re, ce, is_low):
    top = positions((8, 512), 0) < 4
    row = 0
    for ext, tiles in ((pe, PHI_TILES), (re, RHS_TILES), (ce, COEF_TILES)):
        for k, n in enumerate(tiles):
            x = jnp.where(is_low, k, 7 - k)
            parts = [tile(ext, x, 0)]
            if n == 2:
                parts.append(jnp.where(top, tile(ext, x, 1), tile(ext, x, 2)))
            for part in parts:
                out[row:row + 8, :] = part
                row += 8

    def beyond(ext, k):
        x = jnp.where(is_low, k, 7 - k)
        return jnp.where(top, tile(ext, x, 2), tile(ext, x, 1))

    at = positions((8, 512), 0)
    ends = (at == 0) | (at == 7)
    more = jnp.where(ends, along(beyond(pe, 1), 0, 4), beyond(pe, 0))
    source = beyond(re, 0)
    more = jnp.where(at == 1, along(source, 0, 2), jnp.where(at == 6, along(source, 0, -2), more))
    out[PHI_MORE:PHI_MORE + 8, :] = more
    out[COEF_MORE:COEF_MORE + 8, :] = jnp.where(ends, along(beyond(ce, 1), 0, 4), beyond(ce, 0))


def slab_x(side, t):
    return jnp.where(side == 0, 3 - t, 4 + t)


def first_weights(c, xp, xm):
    hy = harmonic(c, along(c, 0, 1))
    hz = z_face(c)
    d = weight(xm, c) + weight(hy, c) + weight(along(hy, 0, -1), c) + weight(hz, c) + weight(along(hz, 1, -1), c)
    return hy, hz, d if xp is None else d + weight(xp, c)


def inverse(d):
    return RELAX_WEIGHT * reciprocal(jnp.maximum(d, FLOOR))


def pair_sums(sums, place, a, b, scale):
    t = a + b
    t = (t + along(t, 0, 1)) * scale
    for q in range(4):
        sums[q, place] = t[:, 128 * q:128 * q + 128]


def halve_fine(sums, packed, n):
    for k in range(n):
        for q in range(4):
            lanes = slice(128 * q, 128 * q + 128)
            packed[16 * k:16 * k + 8, lanes] = sums[q, k, pl.ds(0, 8, stride=2), :]
            packed[16 * k + 8:16 * k + 12, lanes] = jnp.zeros((4, 128), F32)
            packed[16 * k + 12:16 * k + 16, lanes] = sums[q, k, pl.ds(16, 4, stride=2), :]
    return exact_matmul(packed[...], halving(512, 256)).reshape(n, 16, 256)


def inner(pe, re, ce, hx, hc, hy, hz, dg, rd, p1, p2, res, cmid, mate, sums, packed):
    first = is_first()
    block = mate.at[jnp.where(first, 1, 0)]
    pack_end(block, lambda ext, x, t: ext[x, 8 * t:8 * t + 8, :], pe, re, ce, jnp.logical_not(first))
    hc[0] = harmonic(ce[3], ce[4])

    def start(side, carry):
        for t in range(4):
            x = slab_x(side, t)
            c = ce[x]
            xm = hc[0] if t == 0 else hx[side, t - 1]
            xp = None
            if t < 3:
                xp = harmonic(c, ce[slab_x(side, t + 1)])
                hx[side, t] = xp
            hyt, hzt, d = first_weights(c, xp, xm)
            hy[side, t], hz[side, t], dg[side, t] = hyt, hzt, d
            if t < 3:
                r = inverse(d)
                rd[side, t] = r
                v = pe[x]
                image = operate(d, v, xp, pe[slab_x(side, t + 1)], xm, pe[slab_x(side, t - 1)], hyt, hzt)
                p1[side, t] = v + (re[x] - image) * r
        for q in range(2):
            pair_sums(sums, jnp.where(side == 0, 1 - q, 2 + q),
                      ce[slab_x(side, 2 * q)], ce[slab_x(side, 2 * q + 1)], 0.125)
        return carry

    lax.fori_loop(0, 2, start, 0)

    def image(side, t, p):
        xm, pm = (hc[0], p[1 - side, 0]) if t == 0 else (hx[side, t - 1], p[side, t - 1])
        return operate(dg[side, t], p[side, t], hx[side, t], p[side, t + 1], xm, pm, hy[side, t], hz[side, t])

    def second(side, carry):
        for t in range(2):
            p2[side, t] = p1[side, t] + (re[slab_x(side, t)] - image(side, t, p1)) * rd[side, t]
        return carry

    lax.fori_loop(0, 2, second, 0)

    def third(side, carry):
        res[side] = re[slab_x(side, 0)] - image(side, 0, p2)
        return carry

    lax.fori_loop(0, 2, third, 0)
    cmid[...] = halve_fine(sums, packed, 4)


def one_side(side, received, pe, re, ce, hx, hc, hy, hz, dg, rd, p1, p2, res, phi, half,
             hxh, hyh, hzh, dgh, rdh, p1h, p2h, resh, sums, packed):
    at = positions((8, 512), 0)
    top = at < 4

    def slabs_of(own, first_row, tiles, more):
        def load(j):
            if j == 0:
                return own[slab_x(side, 3)]
            n, row = tiles[j - 1], first_row + 8 * sum(tiles[:j - 1])
            parts = [received[row + 8 * t:row + 8 * t + 8, :] for t in range(n)]
            if n == 1:
                parts += [jnp.zeros((8, 512), F32)] * 2
            elif j <= len(more):
                parts += [jnp.where(top, more[j - 1], parts[1])]
                parts[1] = jnp.where(top, parts[1], more[j - 1])
            else:
                parts += [parts[1]]
            return jnp.concatenate(parts, axis=0)
        return load

    more_p, more_c = received[PHI_MORE:PHI_MORE + 8, :], received[COEF_MORE:COEF_MORE + 8, :]
    more_r = jnp.where(top, along(more_p, 0, -2), along(more_p, 0, 2))
    p0h = slabs_of(pe, 0, PHI_TILES, (more_p, along(more_p, 0, 4)))
    rsh = slabs_of(re, 8 * sum(PHI_TILES), RHS_TILES, (more_r,))
    ch = slabs_of(ce, 8 * (sum(PHI_TILES) + sum(RHS_TILES)), COEF_TILES, (more_c, along(more_c, 0, 4)))
    c = ch(0)
    xp = harmonic(c, ch(1))
    d = dg[side, 3] + weight(xp, c)
    r = inverse(d)
    hxh[0], hyh[0], hzh[0], dgh[0], rdh[0] = xp, hy[side, 3], hz[side, 3], d, r
    v = p0h(0)
    image = operate(d, v, xp, p0h(1), hx[side, 2], pe[slab_x(side, 2)], hy[side, 3], hz[side, 3])
    p1h[0] = v + (rsh(0) - image) * r

    for j in range(1, 7):
        c = ch(j)
        xp, xm = harmonic(c, ch(j + 1)), hxh[j - 1]
        hyj, hzj, d = first_weights(c, xp, xm)
        r = inverse(d)
        hxh[j], hyh[j], hzh[j], dgh[j], rdh[j] = xp, hyj, hzj, d, r
        v = p0h(j)
        image = operate(d, v, xp, p0h(j + 1), xm, p0h(j - 1), hyj, hzj)
        p1h[j] = v + (rsh(j) - image) * r

    image = operate(dg[side, 2], p1[side, 2], hx[side, 2], p1h[0], hx[side, 1], p1[side, 1],
                    hy[side, 2], hz[side, 2])
    p2h[1] = p1[side, 2] + (re[slab_x(side, 2)] - image) * rd[side, 2]
    p2h[0] = p2[side, 1]
    image = operate(dgh[0], p1h[0], hxh[0], p1h[1], hx[side, 2], p1[side, 2],
                    hyh[0], hzh[0])
    p2h[2] = p1h[0] + (rsh(0) - image) * rdh[0]

    for j in range(1, 6):
        v = p1h[j]
        image = operate(dgh[j], v, hxh[j], p1h[j + 1], hxh[j - 1], p1h[j - 1],
                        hyh[j], hzh[j])
        p2h[j + 2] = v + (rsh(j) - image) * rdh[j]
    for t in range(4):
        phi[jnp.where(side == 0, 3 - t, t)] = (p2[side, t] if t < 2 else p2h[t - 1])[0:8, :]

    for t in (1, 2):
        image = operate(dg[side, t], p2h[t - 1], hx[side, t], p2h[t], hx[side, t - 1],
                        p2[side, 0] if t == 1 else p2h[0], hy[side, t], hz[side, t])
        resh[t - 1] = re[slab_x(side, t)] - image
    image = operate(dgh[0], p2h[2], hxh[0], p2h[3], hx[side, 2], p2h[1],
                    hyh[0], hzh[0])
    resh[2] = rsh(0) - image

    for j in range(1, 5):
        image = operate(dgh[j], p2h[j + 2], hxh[j], p2h[j + 3], hxh[j - 1],
                        p2h[j + 1], hyh[j], hzh[j])
        resh[j + 2] = rsh(j) - image
    for q in range(4):
        a = res[side] if q == 0 else resh[2 * q - 1]
        pair_sums(sums, q, a, resh[2 * q], 0.5)
        pair_sums(sums, 4 + q, ch(2 * q + 1), ch(2 * q + 2), 0.125)
    half[...] = halve_fine(sums, packed, 8)


def mate_side(*refs):
    side = jnp.where(is_first(), 1, 0)
    one_side(side, refs[12].at[side], *refs[:12], *refs[13:])


def other_side(*refs):
    one_side(jnp.where(is_first(), 0, 1), refs[12], *refs[:12], *refs[13:])


def middle(mate, other, cmid, phi_mate, phi_other, phi_out, emid, out, sums, left):
    side = jnp.where(is_first(), 1, 0)
    stores = [pltpu.make_async_copy(src, phi_out.at[pl.ds(4 * at, 4)], left.at[k])
              for k, (src, at) in enumerate(((phi_mate, side), (phi_other, 1 - side)))]
    for store in stores:
        store.start()
    first = is_first()
    lo = [jnp.where(first, other[j], mate[j]) for j in range(8)]
    hi = [jnp.where(first, mate[j], other[j]) for j in range(8)]
    s = lo[3::-1] + hi[0:4]
    c = lo[:3:-1] + [cmid[j] for j in range(4)] + hi[4:8]
    hx = [harmonic(c[j], c[j + 1]) for j in range(1, 10)]
    hy, hz, d, r, e1 = [], [], [], [], []
    for i in range(8):
        ci = c[i + 2]
        hy.append(harmonic(ci, along(ci, 0, 1)))
        hz.append(z_face(ci))
        d.append(diagonal_of(ci, hx[i + 1], hx[i], hy[i], hz[i]))
        r.append(inverse(d[i]))
        e1.append(s[i] * r[i])

    def image(i, e):
        return operate(d[i], e[i], hx[i + 1], e[i + 1], hx[i], e[i - 1], hy[i], hz[i])

    e2 = [None] + [e1[i] + (s[i] - image(i, e1)) * r[i] for i in range(1, 7)] + [None]
    res = [s[i] - image(i, e2) for i in range(2, 6)]
    for x in range(4):
        emid[x] = e2[2 + x][0:4, :]
    groups = [(res[2 * x] + res[2 * x + 1]) * 0.5 for x in range(2)]
    groups += [(c[2 * x] + c[2 * x + 1]) * 0.125 for x in range(6)]
    for g in range(8):
        both = (groups[g] + along(groups[g], 0, 1))[0:8, :]
        sums[8 * g:8 * g + 8, :] = both[:, 0:128]
        sums[64 + 8 * g:72 + 8 * g, :] = both[:, 128:256]

    def rows(y):
        return jnp.concatenate([sums[pl.ds(64 * q + 2 * y, 8, stride=8), :] for q in range(2)], axis=1)

    low0 = matmul(rows(0), halving(256, 128))
    low1 = matmul(rows(1), halving(256, 128))
    for n in range(16):
        out[n, 0:8, :] = low0
        out[n, 8:16, :] = low1
    for store in stores:
        store.wait()


def y_face(c):
    n = c.shape[0]
    return harmonic(c, jnp.where(positions(c.shape, 0) < n - 1, along(c, 0, 1), 0.0))


def low(gathered, elow, out, scol, ccol, sums):
    for g in range(8):
        for y in range(2):
            ref, k = (scol, g) if g < 2 else (ccol, g - 2)
            ref[pl.ds(32 * k + y, 16, stride=2), :] = gathered[pl.ds(8 * y + g, 16, stride=16), :]
    c = [ccol[32 * j:32 * j + 32, :] for j in range(6)]
    zero = jnp.zeros((32, 128), F32)
    s = [zero, zero, scol[0:32, :], scol[32:64, :], zero, zero]
    hx = [harmonic(c[j], c[j + 1]) for j in range(5)]
    hy, hz, d, r = [None], [None], [None], [None]
    for j in range(1, 5):
        hy.append(y_face(c[j]))
        hz.append(z_face(c[j]))
        d.append(diagonal_of(c[j], hx[j], hx[j - 1], hy[j], hz[j]))
        r.append(inverse(d[j]))
    e1 = [zero, zero, s[2] * r[2], s[3] * r[3], zero, zero]

    def image(j, e):
        return operate(d[j], e[j], hx[j], e[j + 1], hx[j - 1], e[j - 1], hy[j], hz[j])

    e2 = [zero, hx[1] * e1[2] * r[1]]
    e2 += [e1[j] + (s[j] - image(j, e1)) * r[j] for j in (2, 3)]
    e2 += [hx[3] * e1[3] * r[4], zero]
    res = [hx[0] * e2[1]] + [s[j] - image(j, e2) for j in range(1, 5)] + [hx[4] * e2[4]]

    quads = [(res[2] + res[3]) * 0.5, (c[2] + c[3]) * 0.125, (res[0] + res[1]) * 0.5, (res[4] + res[5]) * 0.5]
    for k in range(4):
        sums[32 * k:32 * k + 32, :] = quads[k] + along(quads[k], 0, 1)
    rows = [sums[pl.ds(32 * k, 16, stride=2), :] for k in range(4)]
    both = matmul(jnp.concatenate([jnp.concatenate(rows[0:2], axis=1), jnp.concatenate(rows[2:4], axis=1)], axis=0),
                  halving(256, 128))
    row = positions((32, 128), 0) - 2 * lax.axis_index("gy")
    errors = [jnp.sum(jnp.where(row == y, e2[j], 0.0), axis=0, keepdims=True) for j in (2, 3, 1, 4) for y in range(2)]
    errors = jnp.concatenate(errors, axis=0)
    elow[...] = errors
    for n in range(32):
        out[n, 0:32, :] = both
        out[n, 32:40, :] = errors


def bottom(gathered, elow, emid, out, hx, hy, hz, dg, sol, res, dire, img):
    half = positions((16, 128), 1) < 64
    last_z = positions((16, 128), 1) % 64 == 63
    last_y = positions((16, 128), 0) == 15
    c = []
    for x in range(16):
        a, b = gathered[x, 0:16, :], gathered[x + 16, 0:16, :]
        source = jnp.where(half, a, along(b, 1, 64))
        c.append(jnp.where(half, along(a, 1, 64), b))
        b = along(gathered[x + 17, 16:32, :], 1, 64) if x < 15 else 0.0
        source = source + jnp.where(half, gathered[x + 1, 16:32, :], b)
        a = along(gathered[x - 1, 16:32, :], 1, 64) if x > 0 else 0.0
        source = source + jnp.where(half, a, gathered[x + 15, 16:32, :])
        res[x] = source
        dire[x] = source
        sol[x] = jnp.zeros((16, 128), F32)
    for x in range(16):
        nxt = c[x + 1] if x < 15 else jnp.where(half, along(c[0], 1, 64), 0.0)
        hx[x + 1] = harmonic(c[x], nxt)
    hx[0] = along(hx[16], 1, 64)
    for x in range(16):
        hy[x] = harmonic(c[x], jnp.where(last_y, 0.0, along(c[x], 0, 1)))
        hz[x] = harmonic(c[x], jnp.where(last_z, 0.0, along(c[x], 1, 1)))
        dg[x] = diagonal_of(c[x], hx[x + 1], hx[x], hy[x], hz[x])

    def total(acc):
        return jnp.sum(jnp.sum(acc, axis=0, keepdims=True), axis=1, keepdims=True)

    def dot_image():
        acc = jnp.zeros((16, 128), F32)
        for x in range(16):
            v = dire[x]
            vp = dire[x + 1] if x < 15 else along(dire[0], 1, 64)
            vm = dire[x - 1] if x > 0 else along(dire[15], 1, 64)
            image = operate(dg[x], v, hx[x + 1], vp, hx[x], vm, hy[x], hz[x])
            img[x] = image
            acc = acc + v * image
        return total(acc)

    def norm():
        acc = jnp.zeros((16, 128), F32)
        for x in range(16):
            acc = acc + res[x] * res[x]
        return total(acc)

    def step(_, rr):
        alpha = rr / dot_image()
        acc = jnp.zeros((16, 128), F32)
        for x in range(16):
            sol[x] = sol[x] + alpha * dire[x]
            rx = res[x] - alpha * img[x]
            res[x] = rx
            acc = acc + rx * rx
        new = total(acc)
        beta = new / rr
        for x in range(16):
            dire[x] = res[x] + beta * dire[x]
        return new

    gx, gy = lax.axis_index("gx"), lax.axis_index("gy")
    after = jnp.where(gx < 31, gathered[jnp.minimum(gx + 1, 31), 32:40, :], 0.0)
    before = jnp.where(gx > 0, gathered[jnp.maximum(gx - 1, 0), 32:40, :], 0.0)
    lows = elow[0:4, :] + jnp.concatenate([before[6:8, :], after[4:6, :]], axis=0)
    finer = matmul(jnp.concatenate([lows, lows], axis=0), doubling(128, 256, 2))
    rr = lax.fori_loop(0, BOTTOM - 1, step, norm(), unroll=True)
    xi = lax.rem(gx, 16)
    alpha = rr / dot_image()
    mine = sol[xi] + alpha * dire[xi]
    mine = jnp.where(gx >= 16, along(mine, 1, 64), mine)
    row = positions((16, 128), 0)
    mine = jnp.sum(jnp.where(row == gy, mine, 0.0), axis=0, keepdims=True)
    coarse = matmul(jnp.broadcast_to(mine, (8, 128)), doubling(128, 256, 4))
    for x in range(4):
        k = 2 * (x // 2)
        for y in range(4):
            add = finer[k + y // 2:k + y // 2 + 1, :] + coarse[0:1, :]
            out[x, y:y + 1, :] = emid[x, y:y + 1, :] + add


def swap(values, axis, far):
    n = lax.axis_size(axis)
    pairs = [(i, i + 1) for i in range(int(far), n - 1, 2)]
    return lax.ppermute(values, axis, pairs + [(j, i) for i, j in pairs])


def shards(phi_start, right_side, coefficient):
    own = [a.reshape(64, 512) for a in (phi_start, right_side, coefficient)]
    near, far = call(
        pack_y, [(8 * NROWS, 512)] * 2, [(64, 512)] * 3 + [(768, 128), (2, 8 * NROWS, 512)],
        n_in=3, copies=9, in_hbm=3, out_hbm=2, limit=64000000)(*own)
    far = swap(far, "gy", True)
    near = swap(near, "gy", False)
    own = call(hold, [(64, 512)] * 3, n_in=3,
               cost=pl.CostEstimate(flops=16_000_000, bytes_accessed=4_000_000, transcendentals=0))(*own)
    *ext, other = call(pack_x, [(192, 512)] * 3 + [(END_ROWS, 512)], [(1536, 128)], n_in=5)(*own, far, near)
    other = swap(other, "gx", True)
    ext = [a.reshape(8, 24, 512) for a in ext]

    def slabs(*n):
        return (*n, 24, 512)

    *inside, cmid, mate = call(
        inner,
        [slabs(2, 3), slabs(1)] + [slabs(2, 4)] * 3 + [slabs(2, 3)] * 2 + [slabs(2, 2), slabs(2), (4, 16, 256), (2, END_ROWS, 512)],
        [(4, 4, 24, 128), (64, 512)], n_in=3,
        cost=pl.CostEstimate(flops=1_000, bytes_accessed=1_000, transcendentals=0),
    )(*ext)
    chips = [[i, i + 1] for i in range(0, lax.axis_size("gx"), 2)]
    mate = lax.all_to_all(mate, "gx", 0, 0, tiled=True, axis_index_groups=chips)
    scratch = [slabs(9)] * 8 + [(4, 8, 24, 128), (128, 512)]
    phi_mate, half = call(
        mate_side, [(4, 8, 512), (8, 16, 256)], scratch, n_in=13,
        cost=pl.CostEstimate(flops=1_000, bytes_accessed=1_000, transcendentals=0),
    )(*ext, *inside, mate)
    phi_other, other_half = call(
        other_side, [(4, 8, 512), (8, 16, 256)], scratch, n_in=13)(*ext, *inside, other)
    phi_fine, emid, spread = call(
        middle, [(8, 8, 512), (4, 4, 256), (16, 16, 128)], [(128, 128)], n_in=5, copies=2, out_hbm=1)(
        half, other_half, cmid, phi_mate, phi_other)
    gathered = lax.all_to_all(spread, "gy", 0, 0, tiled=True)
    elow, spread = call(low, [(8, 128), (32, 40, 128)], [(64, 128), (192, 128), (128, 128)], n_in=1)(
        gathered.reshape(256, 128))
    gathered = lax.all_to_all(spread, "gx", 0, 0, tiled=True)
    (correction,) = call(bottom, [(4, 4, 256)], [(17, 16, 128)] + [(16, 16, 128)] * 7, n_in=3)(
        gathered, elow, emid)
    return phi_fine, correction


def solution(mesh):
    return jax.shard_map(
        shards,
        mesh=mesh,
        in_specs=(P("gx", "gy", None),) * 3,
        out_specs=(P("gx", "gy", None),) * 2,
        check_vma=False,
    )
```

```python
import jax
import jax.numpy as jnp
from jax import lax
from jax.experimental import pallas as pl
from jax.experimental.pallas import tpu as pltpu
from jax.sharding import PartitionSpec as P

BOTTOM = 6
RELAX_WEIGHT = 0.8
FLOOR = 1e-3
F32 = jnp.float32
VMEM = pl.BlockSpec(memory_space=pltpu.VMEM)
HBM = pl.BlockSpec(memory_space=pltpu.HBM)


def call(kernel, out_shapes, scratch=(), n_in=0, copies=0, in_hbm=0, out_hbm=0, limit=24 * 1024 * 1024, cost=None):
    semaphores = [pltpu.SemaphoreType.DMA((copies,))] if copies else []
    return pl.pallas_call(
        kernel,
        out_shape=[jax.ShapeDtypeStruct(s, F32) for s in out_shapes],
        in_specs=[HBM] * in_hbm + [VMEM] * (n_in - in_hbm),
        out_specs=[HBM] * out_hbm + [VMEM] * (len(out_shapes) - out_hbm),
        scratch_shapes=[pltpu.VMEM(s, F32) for s in scratch] + semaphores,
        compiler_params=pltpu.CompilerParams(vmem_limit_bytes=limit),
        cost_estimate=cost,
    )


def reciprocal(x):
    r = pl.reciprocal(x, approx=True)
    return r * (2.0 - x * r)


def harmonic(a, b):
    return 2.0 * a * b * reciprocal(jnp.maximum(a + b, FLOOR))


def along(v, axis, step):
    n = v.shape[axis]
    return pltpu.roll(v, (-step) % n, axis)


def is_first():
    return lax.rem(lax.axis_index("gx"), 2) == 0


def positions(shape, axis):
    return lax.broadcasted_iota(jnp.int32, shape, axis)


def halving(rows, cols):
    return (positions((rows, cols), 0) // 2 == positions((rows, cols), 1)).astype(F32)


def doubling(rows, cols, factor):
    return (positions((rows, cols), 1) // factor == positions((rows, cols), 0)).astype(F32)


def matmul(a, b):
    return exact_matmul(a, b)


def exact_matmul(a, ones):
    parts = []
    for _ in range(3):
        parts.append(a.astype(jnp.bfloat16))
        a = a - parts[-1].astype(F32)
    ones = ones.astype(jnp.bfloat16)
    return sum(jnp.dot(p, ones, preferred_element_type=F32) for p in reversed(parts))


def weight(face, centre):
    return jnp.where(face > 0.0, face, centre)


def diagonal_of(c, xp, xm, hy, hz):
    return (weight(xp, c) + weight(xm, c) + weight(hy, c) + weight(along(hy, 0, -1), c)
            + weight(hz, c) + weight(along(hz, 1, -1), c))


def operate(d, v, xp, vp, xm, vm, hy, hz):
    out = d * v - xp * vp - xm * vm
    out = out - hy * along(v, 0, 1) - along(hy * v, 0, -1)
    return out - hz * along(v, 1, 1) - along(hz * v, 1, -1)


def z_face(c):
    nxt = jnp.where(positions(c.shape, 1) < c.shape[1] - 1, along(c, 1, 1), 0.0)
    return harmonic(c, nxt)


NP, NR, NC = 7, 6, 7
NROWS = NP + NR + NC
PHI_TILES = (2, 2, 2, 2, 2, 2, 1)
RHS_TILES = (2, 2, 2, 2, 2, 1)
COEF_TILES = (2, 2, 2, 2, 2, 2, 1, 1)
PHI_MORE = 8 * (sum(PHI_TILES) + sum(RHS_TILES) + sum(COEF_TILES))
COEF_MORE = PHI_MORE + 8
END_ROWS = PHI_MORE + 16


def pack_y(phi_in, rhs_in, coef_in, near, far, phi, rhs, coef, stage, ends, sem):
    loads = [pltpu.make_async_copy(src, dst, sem.at[a])
             for a, (src, dst) in enumerate(((phi_in, phi), (rhs_in, rhs), (coef_in, coef)))]
    for load in loads:
        load.start()
    stores = []
    k = 0
    for a, (ref, n) in enumerate(((phi, NP), (rhs, NR), (coef, NC))):
        loads[a].wait()
        for q in range(4):
            lanes = slice(128 * q, 128 * q + 128)
            base = 64 * (4 * a + q)
            stage[base:base + 64, :] = ref[:, lanes]
            for j in range(n):
                rows = slice(8 * (k + j), 8 * (k + j) + 8)
                ends[0, rows, lanes] = stage[pl.ds(base + 8 - n + j, 8, stride=8), :]
                ends[1, rows, lanes] = stage[pl.ds(base + j, 8, stride=8), :]
        for b, dst in enumerate((near, far)):
            part = pl.ds(8 * k, 8 * n)
            src = ends.at[lax.rem(lax.axis_index("gy") + b, 2), part]
            stores.append(pltpu.make_async_copy(src, dst.at[part], sem.at[3 + 2 * a + b]))
            stores[-1].start()
        k += n
    for store in stores:
        store.wait()


def hold(*refs):
    for src, dst in zip(refs[:3], refs[3:]):
        dst[...] = src[...]


def pack_x(phi, rhs, coef, far, near, pe, re, ce, other, stage):
    zero = jnp.zeros((8, 128), F32)
    odd = lax.rem(lax.axis_index("gy"), 2)
    k = 0
    for a, (ref, ext, n) in enumerate(((phi, pe, NP), (rhs, re, NR), (coef, ce, NC))):
        for x in range(8):
            ext[24 * x:24 * x + 8, :] = ref[8 * x:8 * x + 8, :]
        for q in range(4):
            lanes = slice(128 * q, 128 * q + 128)
            base = 128 * (4 * a + q)
            for j in range(n):
                rows = slice(8 * (k + j), 8 * (k + j) + 8)
                stage[pl.ds(base + j + odd * (16 - n), 8, stride=16), :] = near[rows, lanes]
                stage[pl.ds(base + j + (1 - odd) * (16 - n), 8, stride=16), :] = far[rows, lanes]
            for j in range(n, 16 - n):
                stage[pl.ds(base + j, 8, stride=16), :] = zero
            for x in range(8):
                ext[24 * x + 8:24 * x + 24, lanes] = stage[base + 16 * x:base + 16 * x + 16, :]
        k += n
    first = is_first()
    pack_end(other, lambda ext, x, t: ext[pl.ds(pl.multiple_of(24 * x + 8 * t, 8), 8), :], pe, re, ce, first)


def pack_end(out, tile, pe, re, ce, is_low):
    top = positions((8, 512), 0) < 4
    row = 0
    for ext, tiles in ((pe, PHI_TILES), (re, RHS_TILES), (ce, COEF_TILES)):
        for k, n in enumerate(tiles):
            x = jnp.where(is_low, k, 7 - k)
            parts = [tile(ext, x, 0)]
            if n == 2:
                parts.append(jnp.where(top, tile(ext, x, 1), tile(ext, x, 2)))
            for part in parts:
                out[row:row + 8, :] = part
                row += 8

    def beyond(ext, k):
        x = jnp.where(is_low, k, 7 - k)
        return jnp.where(top, tile(ext, x, 2), tile(ext, x, 1))

    at = positions((8, 512), 0)
    ends = (at == 0) | (at == 7)
    more = jnp.where(ends, along(beyond(pe, 1), 0, 4), beyond(pe, 0))
    source = beyond(re, 0)
    more = jnp.where(at == 1, along(source, 0, 2), jnp.where(at == 6, along(source, 0, -2), more))
    out[PHI_MORE:PHI_MORE + 8, :] = more
    out[COEF_MORE:COEF_MORE + 8, :] = jnp.where(ends, along(beyond(ce, 1), 0, 4), beyond(ce, 0))


def slab_x(side, t):
    return jnp.where(side == 0, 3 - t, 4 + t)


def first_weights(c, xp, xm):
    hy = harmonic(c, along(c, 0, 1))
    hz = z_face(c)
    d = weight(xm, c) + weight(hy, c) + weight(along(hy, 0, -1), c) + weight(hz, c) + weight(along(hz, 1, -1), c)
    return hy, hz, d if xp is None else d + weight(xp, c)


def inverse(d):
    return RELAX_WEIGHT * reciprocal(jnp.maximum(d, FLOOR))


def pair_sums(sums, place, a, b, scale):
    t = a + b
    t = (t + along(t, 0, 1)) * scale
    for q in range(4):
        sums[q, place] = t[:, 128 * q:128 * q + 128]


def halve_fine(sums, packed, n):
    for k in range(n):
        for q in range(4):
            lanes = slice(128 * q, 128 * q + 128)
            packed[16 * k:16 * k + 8, lanes] = sums[q, k, pl.ds(0, 8, stride=2), :]
            packed[16 * k + 8:16 * k + 12, lanes] = jnp.zeros((4, 128), F32)
            packed[16 * k + 12:16 * k + 16, lanes] = sums[q, k, pl.ds(16, 4, stride=2), :]
    return exact_matmul(packed[...], halving(512, 256)).reshape(n, 16, 256)


def inner(pe, re, ce, hx, hc, hy, hz, dg, rd, p1, p2, res, cmid, mate, sums, packed):
    first = is_first()
    block = mate.at[jnp.where(first, 1, 0)]
    pack_end(block, lambda ext, x, t: ext[x, 8 * t:8 * t + 8, :], pe, re, ce, jnp.logical_not(first))
    hc[0] = harmonic(ce[3], ce[4])

    def start(side, carry):
        for t in range(4):
            x = slab_x(side, t)
            c = ce[x]
            xm = hc[0] if t == 0 else hx[side, t - 1]
            xp = None
            if t < 3:
                xp = harmonic(c, ce[slab_x(side, t + 1)])
                hx[side, t] = xp
            hyt, hzt, d = first_weights(c, xp, xm)
            hy[side, t], hz[side, t], dg[side, t] = hyt, hzt, d
            if t < 3:
                r = inverse(d)
                rd[side, t] = r
                v = pe[x]
                image = operate(d, v, xp, pe[slab_x(side, t + 1)], xm, pe[slab_x(side, t - 1)], hyt, hzt)
                p1[side, t] = v + (re[x] - image) * r
        for q in range(2):
            pair_sums(sums, jnp.where(side == 0, 1 - q, 2 + q),
                      ce[slab_x(side, 2 * q)], ce[slab_x(side, 2 * q + 1)], 0.125)
        return carry

    lax.fori_loop(0, 2, start, 0)

    def image(side, t, p):
        xm, pm = (hc[0], p[1 - side, 0]) if t == 0 else (hx[side, t - 1], p[side, t - 1])
        return operate(dg[side, t], p[side, t], hx[side, t], p[side, t + 1], xm, pm, hy[side, t], hz[side, t])

    def second(side, carry):
        for t in range(2):
            p2[side, t] = p1[side, t] + (re[slab_x(side, t)] - image(side, t, p1)) * rd[side, t]
        return carry

    lax.fori_loop(0, 2, second, 0)

    def third(side, carry):
        res[side] = re[slab_x(side, 0)] - image(side, 0, p2)
        return carry

    lax.fori_loop(0, 2, third, 0)
    cmid[...] = halve_fine(sums, packed, 4)


def one_side(side, received, pe, re, ce, hx, hc, hy, hz, dg, rd, p1, p2, res, phi, half,
             hxh, hyh, hzh, dgh, rdh, p1h, p2h, resh, sums, packed):
    at = positions((8, 512), 0)
    top = at < 4

    def slabs_of(own, first_row, tiles, more):
        def load(j):
            if j == 0:
                return own[slab_x(side, 3)]
            n, row = tiles[j - 1], first_row + 8 * sum(tiles[:j - 1])
            parts = [received[row + 8 * t:row + 8 * t + 8, :] for t in range(n)]
            if n == 1:
                parts += [jnp.zeros((8, 512), F32)] * 2
            elif j <= len(more):
                parts += [jnp.where(top, more[j - 1], parts[1])]
                parts[1] = jnp.where(top, parts[1], more[j - 1])
            else:
                parts += [parts[1]]
            return jnp.concatenate(parts, axis=0)
        return load

    more_p, more_c = received[PHI_MORE:PHI_MORE + 8, :], received[COEF_MORE:COEF_MORE + 8, :]
    more_r = jnp.where(top, along(more_p, 0, -2), along(more_p, 0, 2))
    p0h = slabs_of(pe, 0, PHI_TILES, (more_p, along(more_p, 0, 4)))
    rsh = slabs_of(re, 8 * sum(PHI_TILES), RHS_TILES, (more_r,))
    ch = slabs_of(ce, 8 * (sum(PHI_TILES) + sum(RHS_TILES)), COEF_TILES, (more_c, along(more_c, 0, 4)))
    c = ch(0)
    xp = harmonic(c, ch(1))
    d = dg[side, 3] + weight(xp, c)
    r = inverse(d)
    hxh[0], hyh[0], hzh[0], dgh[0], rdh[0] = xp, hy[side, 3], hz[side, 3], d, r
    v = p0h(0)
    image = operate(d, v, xp, p0h(1), hx[side, 2], pe[slab_x(side, 2)], hy[side, 3], hz[side, 3])
    p1h[0] = v + (rsh(0) - image) * r

    for j in range(1, 7):
        c = ch(j)
        xp, xm = harmonic(c, ch(j + 1)), hxh[j - 1]
        hyj, hzj, d = first_weights(c, xp, xm)
        r = inverse(d)
        hxh[j], hyh[j], hzh[j], dgh[j], rdh[j] = xp, hyj, hzj, d, r
        v = p0h(j)
        image = operate(d, v, xp, p0h(j + 1), xm, p0h(j - 1), hyj, hzj)
        p1h[j] = v + (rsh(j) - image) * r

    image = operate(dg[side, 2], p1[side, 2], hx[side, 2], p1h[0], hx[side, 1], p1[side, 1],
                    hy[side, 2], hz[side, 2])
    p2h[1] = p1[side, 2] + (re[slab_x(side, 2)] - image) * rd[side, 2]
    p2h[0] = p2[side, 1]
    image = operate(dgh[0], p1h[0], hxh[0], p1h[1], hx[side, 2], p1[side, 2],
                    hyh[0], hzh[0])
    p2h[2] = p1h[0] + (rsh(0) - image) * rdh[0]

    for j in range(1, 6):
        v = p1h[j]
        image = operate(dgh[j], v, hxh[j], p1h[j + 1], hxh[j - 1], p1h[j - 1],
                        hyh[j], hzh[j])
        p2h[j + 2] = v + (rsh(j) - image) * rdh[j]
    for t in range(4):
        phi[jnp.where(side == 0, 3 - t, t)] = (p2[side, t] if t < 2 else p2h[t - 1])[0:8, :]

    for t in (1, 2):
        image = operate(dg[side, t], p2h[t - 1], hx[side, t], p2h[t], hx[side, t - 1],
                        p2[side, 0] if t == 1 else p2h[0], hy[side, t], hz[side, t])
        resh[t - 1] = re[slab_x(side, t)] - image
    image = operate(dgh[0], p2h[2], hxh[0], p2h[3], hx[side, 2], p2h[1],
                    hyh[0], hzh[0])
    resh[2] = rsh(0) - image

    for j in range(1, 5):
        image = operate(dgh[j], p2h[j + 2], hxh[j], p2h[j + 3], hxh[j - 1],
                        p2h[j + 1], hyh[j], hzh[j])
        resh[j + 2] = rsh(j) - image
    for q in range(4):
        a = res[side] if q == 0 else resh[2 * q - 1]
        pair_sums(sums, q, a, resh[2 * q], 0.5)
        pair_sums(sums, 4 + q, ch(2 * q + 1), ch(2 * q + 2), 0.125)
    half[...] = halve_fine(sums, packed, 8)


def mate_side(*refs):
    side = jnp.where(is_first(), 1, 0)
    one_side(side, refs[12].at[side], *refs[:12], *refs[13:])


def other_side(*refs):
    one_side(jnp.where(is_first(), 0, 1), refs[12], *refs[:12], *refs[13:])


def middle(mate, other, cmid, phi_mate, phi_other, phi_out, emid, out, sums, left):
    side = jnp.where(is_first(), 1, 0)
    stores = [pltpu.make_async_copy(src, phi_out.at[pl.ds(4 * at, 4)], left.at[k])
              for k, (src, at) in enumerate(((phi_mate, side), (phi_other, 1 - side)))]
    for store in stores:
        store.start()
    first = is_first()
    lo = [jnp.where(first, other[j], mate[j]) for j in range(8)]
    hi = [jnp.where(first, mate[j], other[j]) for j in range(8)]
    s = lo[3::-1] + hi[0:4]
    c = lo[:3:-1] + [cmid[j] for j in range(4)] + hi[4:8]
    hx = [harmonic(c[j], c[j + 1]) for j in range(1, 10)]
    hy, hz, d, r, e1 = [], [], [], [], []
    for i in range(8):
        ci = c[i + 2]
        hy.append(harmonic(ci, along(ci, 0, 1)))
        hz.append(z_face(ci))
        d.append(diagonal_of(ci, hx[i + 1], hx[i], hy[i], hz[i]))
        r.append(inverse(d[i]))
        e1.append(s[i] * r[i])

    def image(i, e):
        return operate(d[i], e[i], hx[i + 1], e[i + 1], hx[i], e[i - 1], hy[i], hz[i])

    e2 = [None] + [e1[i] + (s[i] - image(i, e1)) * r[i] for i in range(1, 7)] + [None]
    res = [s[i] - image(i, e2) for i in range(2, 6)]
    for x in range(4):
        emid[x] = e2[2 + x][0:4, :]
    groups = [(res[2 * x] + res[2 * x + 1]) * 0.5 for x in range(2)]
    groups += [(c[2 * x] + c[2 * x + 1]) * 0.125 for x in range(6)]
    for g in range(8):
        both = (groups[g] + along(groups[g], 0, 1))[0:8, :]
        sums[8 * g:8 * g + 8, :] = both[:, 0:128]
        sums[64 + 8 * g:72 + 8 * g, :] = both[:, 128:256]

    def rows(y):
        return jnp.concatenate([sums[pl.ds(64 * q + 2 * y, 8, stride=8), :] for q in range(2)], axis=1)

    low0 = matmul(rows(0), halving(256, 128))
    low1 = matmul(rows(1), halving(256, 128))
    for n in range(16):
        out[n, 0:8, :] = low0
        out[n, 8:16, :] = low1
    for store in stores:
        store.wait()


def y_face(c):
    n = c.shape[0]
    return harmonic(c, jnp.where(positions(c.shape, 0) < n - 1, along(c, 0, 1), 0.0))


def low(gathered, elow, cnear, out, scol, ccol, sums):
    for g in range(8):
        for y in range(2):
            ref, k = (scol, g) if g < 2 else (ccol, g - 2)
            ref[pl.ds(32 * k + y, 16, stride=2), :] = gathered[pl.ds(8 * y + g, 16, stride=16), :]
    c = [ccol[32 * j:32 * j + 32, :] for j in range(6)]
    zero = jnp.zeros((32, 128), F32)
    s = [zero, zero, scol[0:32, :], scol[32:64, :], zero, zero]
    hx = [harmonic(c[j], c[j + 1]) for j in range(5)]
    hy, hz, d, r = [None], [None], [None], [None]
    for j in range(1, 5):
        hy.append(y_face(c[j]))
        hz.append(z_face(c[j]))
        d.append(diagonal_of(c[j], hx[j], hx[j - 1], hy[j], hz[j]))
        r.append(inverse(d[j]))
    e1 = [zero, zero, s[2] * r[2], s[3] * r[3], zero, zero]

    def image(j, e):
        return operate(d[j], e[j], hx[j], e[j + 1], hx[j - 1], e[j - 1], hy[j], hz[j])

    e2 = [zero, hx[1] * e1[2] * r[1]]
    e2 += [e1[j] + (s[j] - image(j, e1)) * r[j] for j in (2, 3)]
    e2 += [hx[3] * e1[3] * r[4], zero]
    res = [hx[0] * e2[1]] + [s[j] - image(j, e2) for j in range(1, 5)] + [hx[4] * e2[4]]

    quads = [(res[2] + res[3]) * 0.5, (c[2] + c[3]) * 0.125, (res[0] + res[1]) * 0.5, (res[4] + res[5]) * 0.5]
    quads += [(c[0] + c[1]) * 0.125, (c[4] + c[5]) * 0.125]
    for k in range(6):
        sums[32 * k:32 * k + 32, :] = quads[k] + along(quads[k], 0, 1)
    rows = [sums[pl.ds(32 * k, 16, stride=2), :] for k in range(6)]
    rows = [jnp.concatenate(rows[k:k + 2], axis=1) for k in (0, 2, 4)]
    both = matmul(jnp.concatenate(rows, axis=0), halving(256, 128))
    cnear[...] = both[32:48, :]
    row = positions((32, 128), 0) - 2 * lax.axis_index("gy")
    errors = [jnp.sum(jnp.where(row == y, e2[j], 0.0), axis=0, keepdims=True) for j in (2, 3, 1, 4) for y in range(2)]
    errors = jnp.concatenate(errors, axis=0)
    elow[...] = errors
    for n in range(32):
        out[n] = both[0:32, :]
    send = errors[4:8, :]
    send = jnp.concatenate([along(send, 1, 64), send], axis=0)
    send = jnp.where(positions((8, 128), 1) < 64, both[0:8, :], send)
    gx = lax.axis_index("gx")

    @pl.when(gx > 0)
    def _():
        out[gx - 1, 0:8, :] = send

    @pl.when(gx < 31)
    def _():
        out[gx + 1, 0:8, :] = send


def bottom(gathered, elow, cnear, emid, out, cc, hx, hy, hz, dg, sol, res, dire, img):
    half = positions((16, 128), 1) < 64
    last_z = positions((16, 128), 1) % 64 == 63
    last_y = positions((16, 128), 0) == 15
    for x in range(16):
        a, b = gathered[x, 0:16, :], gathered[x + 16, 0:16, :]
        source = jnp.where(half, a, along(b, 1, 64))
        cc[x] = jnp.where(half, along(a, 1, 64), b)
        b = along(gathered[x + 17, 16:32, :], 1, 64) if x < 15 else 0.0
        source = source + jnp.where(half, gathered[x + 1, 16:32, :], b)
        a = along(gathered[x - 1, 16:32, :], 1, 64) if x > 0 else 0.0
        source = source + jnp.where(half, a, gathered[x + 15, 16:32, :])
        res[x] = source
        dire[x] = source
        sol[x] = jnp.zeros((16, 128), F32)
    gx, gy = lax.axis_index("gx"), lax.axis_index("gy")

    def put_coefficient(x, where_from):
        at = x // 16
        value = jnp.where(at == where_from, cnear[...], along(cnear[...], 1, 64))
        i = lax.rem(x, 16)
        cc[i] = jnp.where(positions((16, 128), 1) // 64 == at, value, cc[i])

    @pl.when(gx > 0)
    def _():
        put_coefficient(gx - 1, 0)

    @pl.when(gx < 31)
    def _():
        put_coefficient(gx + 1, 1)

    c = [cc[x] for x in range(16)]
    for x in range(16):
        nxt = c[x + 1] if x < 15 else jnp.where(half, along(c[0], 1, 64), 0.0)
        hx[x + 1] = harmonic(c[x], nxt)
    hx[0] = along(hx[16], 1, 64)
    for x in range(16):
        hy[x] = harmonic(c[x], jnp.where(last_y, 0.0, along(c[x], 0, 1)))
        hz[x] = harmonic(c[x], jnp.where(last_z, 0.0, along(c[x], 1, 1)))
        dg[x] = diagonal_of(c[x], hx[x + 1], hx[x], hy[x], hz[x])

    def total(acc):
        return jnp.sum(jnp.sum(acc, axis=0, keepdims=True), axis=1, keepdims=True)

    def dot_image():
        acc = jnp.zeros((16, 128), F32)
        for x in range(16):
            v = dire[x]
            vp = dire[x + 1] if x < 15 else along(dire[0], 1, 64)
            vm = dire[x - 1] if x > 0 else along(dire[15], 1, 64)
            image = operate(dg[x], v, hx[x + 1], vp, hx[x], vm, hy[x], hz[x])
            img[x] = image
            acc = acc + v * image
        return total(acc)

    def norm():
        acc = jnp.zeros((16, 128), F32)
        for x in range(16):
            acc = acc + res[x] * res[x]
        return total(acc)

    def step(_, rr):
        alpha = rr / dot_image()
        acc = jnp.zeros((16, 128), F32)
        for x in range(16):
            sol[x] = sol[x] + alpha * dire[x]
            rx = res[x] - alpha * img[x]
            res[x] = rx
            acc = acc + rx * rx
        new = total(acc)
        beta = new / rr
        for x in range(16):
            dire[x] = res[x] + beta * dire[x]
        return new

    gx, gy = lax.axis_index("gx"), lax.axis_index("gy")
    def errors_from(x, row):
        rows = gathered[x, 0:8, :]
        return jnp.where(positions((2, 128), 1) < 64, along(rows, 1, 64)[row:row + 2, :], rows[row + 4:row + 6, :])

    after = jnp.where(gx < 31, errors_from(jnp.minimum(gx + 1, 31), 0), 0.0)
    before = jnp.where(gx > 0, errors_from(jnp.maximum(gx - 1, 0), 2), 0.0)
    lows = elow[0:4, :] + jnp.concatenate([before, after], axis=0)
    finer = matmul(jnp.concatenate([lows, lows], axis=0), doubling(128, 256, 2))
    rr = lax.fori_loop(0, BOTTOM - 1, step, norm(), unroll=True)
    xi = lax.rem(gx, 16)
    alpha = rr / dot_image()
    mine = sol[xi] + alpha * dire[xi]
    mine = jnp.where(gx >= 16, along(mine, 1, 64), mine)
    row = positions((16, 128), 0)
    mine = jnp.sum(jnp.where(row == gy, mine, 0.0), axis=0, keepdims=True)
    coarse = matmul(jnp.broadcast_to(mine, (8, 128)), doubling(128, 256, 4))
    for x in range(4):
        k = 2 * (x // 2)
        for y in range(4):
            add = finer[k + y // 2:k + y // 2 + 1, :] + coarse[0:1, :]
            out[x, y:y + 1, :] = emid[x, y:y + 1, :] + add


def swap(values, axis, far):
    n = lax.axis_size(axis)
    pairs = [(i, i + 1) for i in range(int(far), n - 1, 2)]
    return lax.ppermute(values, axis, pairs + [(j, i) for i, j in pairs])


def shards(phi_start, right_side, coefficient):
    own = [a.reshape(64, 512) for a in (phi_start, right_side, coefficient)]
    near, far = call(
        pack_y, [(8 * NROWS, 512)] * 2, [(64, 512)] * 3 + [(768, 128), (2, 8 * NROWS, 512)],
        n_in=3, copies=9, in_hbm=3, out_hbm=2, limit=64000000)(*own)
    far = swap(far, "gy", True)
    near = swap(near, "gy", False)
    own = call(hold, [(64, 512)] * 3, n_in=3,
               cost=pl.CostEstimate(flops=16_000_000, bytes_accessed=4_000_000, transcendentals=0))(*own)
    *ext, other = call(pack_x, [(192, 512)] * 3 + [(END_ROWS, 512)], [(1536, 128)], n_in=5)(*own, far, near)
    other = swap(other, "gx", True)
    ext = [a.reshape(8, 24, 512) for a in ext]

    def slabs(*n):
        return (*n, 24, 512)

    *inside, cmid, mate = call(
        inner,
        [slabs(2, 3), slabs(1)] + [slabs(2, 4)] * 3 + [slabs(2, 3)] * 2 + [slabs(2, 2), slabs(2), (4, 16, 256), (2, END_ROWS, 512)],
        [(4, 4, 24, 128), (64, 512)], n_in=3,
        cost=pl.CostEstimate(flops=1_000, bytes_accessed=1_000, transcendentals=0),
    )(*ext)
    chips = [[i, i + 1] for i in range(0, lax.axis_size("gx"), 2)]
    mate = lax.all_to_all(mate, "gx", 0, 0, tiled=True, axis_index_groups=chips)
    scratch = [slabs(9)] * 8 + [(4, 8, 24, 128), (128, 512)]
    phi_mate, half = call(
        mate_side, [(4, 8, 512), (8, 16, 256)], scratch, n_in=13,
        cost=pl.CostEstimate(flops=1_000, bytes_accessed=1_000, transcendentals=0),
    )(*ext, *inside, mate)
    phi_other, other_half = call(
        other_side, [(4, 8, 512), (8, 16, 256)], scratch, n_in=13)(*ext, *inside, other)
    phi_fine, emid, spread = call(
        middle, [(8, 8, 512), (4, 4, 256), (16, 16, 128)], [(128, 128)], n_in=5, copies=2, out_hbm=1)(
        half, other_half, cmid, phi_mate, phi_other)
    gathered = lax.all_to_all(spread, "gy", 0, 0, tiled=True)
    elow, cnear, spread = call(
        low, [(8, 128), (16, 128), (32, 32, 128)], [(64, 128), (192, 128), (192, 128)], n_in=1)(gathered.reshape(256, 128))
    gathered = lax.all_to_all(spread, "gx", 0, 0, tiled=True)
    (correction,) = call(bottom, [(4, 4, 256)], [(16, 16, 128), (17, 16, 128)] + [(16, 16, 128)] * 7, n_in=4)(
        gathered, elow, cnear, emid)
    return phi_fine, correction


def solution(mesh):
    return jax.shard_map(
        shards,
        mesh=mesh,
        in_specs=(P("gx", "gy", None),) * 3,
        out_specs=(P("gx", "gy", None),) * 2,
        check_vma=False,
    )
```

```python
import jax
import jax.numpy as jnp
from jax import lax
from jax.experimental import pallas as pl
from jax.experimental.pallas import tpu as pltpu
from jax.sharding import PartitionSpec as P

BOTTOM = 6
RELAX_WEIGHT = 0.8
FLOOR = 1e-3
F32 = jnp.float32
VMEM = pl.BlockSpec(memory_space=pltpu.VMEM)
HBM = pl.BlockSpec(memory_space=pltpu.HBM)


def call(kernel, out_shapes, scratch=(), n_in=0, copies=0, in_hbm=0, out_hbm=0, limit=24 * 1024 * 1024, cost=None):
    semaphores = [pltpu.SemaphoreType.DMA((copies,))] if copies else []
    return pl.pallas_call(
        kernel,
        out_shape=[jax.ShapeDtypeStruct(s, F32) for s in out_shapes],
        in_specs=[HBM] * in_hbm + [VMEM] * (n_in - in_hbm),
        out_specs=[HBM] * out_hbm + [VMEM] * (len(out_shapes) - out_hbm),
        scratch_shapes=[pltpu.VMEM(s, F32) for s in scratch] + semaphores,
        compiler_params=pltpu.CompilerParams(vmem_limit_bytes=limit),
        cost_estimate=cost,
    )


def reciprocal(x):
    r = pl.reciprocal(x, approx=True)
    return r * (2.0 - x * r)


def harmonic(a, b):
    return 2.0 * a * b * reciprocal(jnp.maximum(a + b, FLOOR))


def along(v, axis, step):
    n = v.shape[axis]
    return pltpu.roll(v, (-step) % n, axis)


def is_first():
    return lax.rem(lax.axis_index("gx"), 2) == 0


def positions(shape, axis):
    return lax.broadcasted_iota(jnp.int32, shape, axis)


def halving(rows, cols):
    return (positions((rows, cols), 0) // 2 == positions((rows, cols), 1)).astype(F32)


def doubling(rows, cols, factor):
    return (positions((rows, cols), 1) // factor == positions((rows, cols), 0)).astype(F32)


def matmul(a, b):
    return exact_matmul(a, b)


def exact_matmul(a, ones):
    parts = []
    for _ in range(3):
        parts.append(a.astype(jnp.bfloat16))
        a = a - parts[-1].astype(F32)
    ones = ones.astype(jnp.bfloat16)
    return sum(jnp.dot(p, ones, preferred_element_type=F32) for p in reversed(parts))


def weight(face, centre):
    return jnp.where(face > 0.0, face, centre)


def diagonal_of(c, xp, xm, hy, hz):
    return (weight(xp, c) + weight(xm, c) + weight(hy, c) + weight(along(hy, 0, -1), c)
            + weight(hz, c) + weight(along(hz, 1, -1), c))


def operate(d, v, xp, vp, xm, vm, hy, hz):
    out = d * v - xp * vp - xm * vm
    out = out - hy * along(v, 0, 1) - along(hy * v, 0, -1)
    return out - hz * along(v, 1, 1) - along(hz * v, 1, -1)


def z_face(c):
    nxt = jnp.where(positions(c.shape, 1) < c.shape[1] - 1, along(c, 1, 1), 0.0)
    return harmonic(c, nxt)


NP, NR, NC = 7, 6, 7
NROWS = NP + NR + NC
PHI_TILES = (2, 2, 2, 2, 2, 2, 1)
RHS_TILES = (2, 2, 2, 2, 2, 1)
COEF_TILES = (2, 2, 2, 2, 2, 2, 1, 1)
TILES = (PHI_TILES, RHS_TILES, COEF_TILES)
PHI_MORE = 8 * (sum(PHI_TILES) + sum(RHS_TILES) + sum(COEF_TILES))
COEF_MORE = PHI_MORE + 8
END_ROWS = PHI_MORE + 16
OWN_ROWS = 8 * (len(PHI_TILES) + len(RHS_TILES) + len(COEF_TILES))


def pack_y(phi_in, rhs_in, coef_in, near, far, own_end, phi, rhs, coef, stage, ends, sem):
    loads = [pltpu.make_async_copy(src, dst, sem.at[a])
             for a, (src, dst) in enumerate(((phi_in, phi), (rhs_in, rhs), (coef_in, coef)))]
    for load in loads:
        load.start()
    stores, row = [], 0
    k = 0
    for a, (ref, n) in enumerate(((phi, NP), (rhs, NR), (coef, NC))):
        loads[a].wait()
        slabs = 8 * len(TILES[a])
        first_row = pl.multiple_of(jnp.where(is_first(), 0, 64 - slabs), 8)
        stores.append(pltpu.make_async_copy(ref.at[pl.ds(first_row, slabs)], own_end.at[pl.ds(row, slabs)], sem.at[9 + a]))
        stores[-1].start()
        row += slabs
        for q in range(4):
            lanes = slice(128 * q, 128 * q + 128)
            base = 64 * (4 * a + q)
            stage[base:base + 64, :] = ref[:, lanes]
            for j in range(n):
                rows = slice(8 * (k + j), 8 * (k + j) + 8)
                ends[0, rows, lanes] = stage[pl.ds(base + 8 - n + j, 8, stride=8), :]
                ends[1, rows, lanes] = stage[pl.ds(base + j, 8, stride=8), :]
        for b, dst in enumerate((near, far)):
            part = pl.ds(8 * k, 8 * n)
            src = ends.at[lax.rem(lax.axis_index("gy") + b, 2), part]
            stores.append(pltpu.make_async_copy(src, dst.at[part], sem.at[3 + 2 * a + b]))
            stores[-1].start()
        k += n
    for store in stores:
        store.wait()


def hold(*refs):
    for src, dst in zip(refs[:3], refs[3:]):
        dst[...] = src[...]


def pack_x(phi, rhs, coef, far, near, pe, re, ce, other, stage):
    zero = jnp.zeros((8, 128), F32)
    odd = lax.rem(lax.axis_index("gy"), 2)
    k = 0
    for a, (ref, ext, n) in enumerate(((phi, pe, NP), (rhs, re, NR), (coef, ce, NC))):
        for x in range(8):
            ext[24 * x:24 * x + 8, :] = ref[8 * x:8 * x + 8, :]
        for q in range(4):
            lanes = slice(128 * q, 128 * q + 128)
            base = 128 * (4 * a + q)
            for j in range(n):
                rows = slice(8 * (k + j), 8 * (k + j) + 8)
                stage[pl.ds(base + j + odd * (16 - n), 8, stride=16), :] = near[rows, lanes]
                stage[pl.ds(base + j + (1 - odd) * (16 - n), 8, stride=16), :] = far[rows, lanes]
            for j in range(n, 16 - n):
                stage[pl.ds(base + j, 8, stride=16), :] = zero
            for x in range(8):
                ext[24 * x + 8:24 * x + 24, lanes] = stage[base + 16 * x:base + 16 * x + 16, :]
        k += n
    first = is_first()
    pack_end(other, lambda ext, x, t: ext[pl.ds(pl.multiple_of(24 * x + 8 * t, 8), 8), :], pe, re, ce, first, False)


def pack_end(out, tile, pe, re, ce, is_low, with_own=True):
    top = positions((8, 512), 0) < 4
    row = 0
    for ext, tiles in ((pe, PHI_TILES), (re, RHS_TILES), (ce, COEF_TILES)):
        for k, n in enumerate(tiles):
            x = jnp.where(is_low, k, 7 - k)
            parts = [tile(ext, x, 0)] if with_own else []
            if n == 2:
                parts.append(jnp.where(top, tile(ext, x, 1), tile(ext, x, 2)))
            for part in parts:
                out[row:row + 8, :] = part
                row += 8

    def beyond(ext, k):
        x = jnp.where(is_low, k, 7 - k)
        return jnp.where(top, tile(ext, x, 2), tile(ext, x, 1))

    at = positions((8, 512), 0)
    ends = (at == 0) | (at == 7)
    more = jnp.where(ends, along(beyond(pe, 1), 0, 4), beyond(pe, 0))
    source = beyond(re, 0)
    more = jnp.where(at == 1, along(source, 0, 2), jnp.where(at == 6, along(source, 0, -2), more))
    out[row:row + 8, :] = more
    out[row + 8:row + 16, :] = jnp.where(ends, along(beyond(ce, 1), 0, 4), beyond(ce, 0))


def slab_x(side, t):
    return jnp.where(side == 0, 3 - t, 4 + t)


def first_weights(c, xp, xm):
    hy = harmonic(c, along(c, 0, 1))
    hz = z_face(c)
    d = weight(xm, c) + weight(hy, c) + weight(along(hy, 0, -1), c) + weight(hz, c) + weight(along(hz, 1, -1), c)
    return hy, hz, d if xp is None else d + weight(xp, c)


def inverse(d):
    return RELAX_WEIGHT * reciprocal(jnp.maximum(d, FLOOR))


def pair_sums(sums, place, a, b, scale):
    t = a + b
    t = (t + along(t, 0, 1)) * scale
    for q in range(4):
        sums[q, place] = t[:, 128 * q:128 * q + 128]


def halve_fine(sums, packed, n):
    for k in range(n):
        for q in range(4):
            lanes = slice(128 * q, 128 * q + 128)
            packed[16 * k:16 * k + 8, lanes] = sums[q, k, pl.ds(0, 8, stride=2), :]
            packed[16 * k + 8:16 * k + 12, lanes] = jnp.zeros((4, 128), F32)
            packed[16 * k + 12:16 * k + 16, lanes] = sums[q, k, pl.ds(16, 4, stride=2), :]
    return exact_matmul(packed[...], halving(512, 256)).reshape(n, 16, 256)


def inner(pe, re, ce, hx, hc, hy, hz, dg, rd, p1, p2, res, cmid, mate, sums, packed):
    first = is_first()
    block = mate.at[jnp.where(first, 1, 0)]
    pack_end(block, lambda ext, x, t: ext[x, 8 * t:8 * t + 8, :], pe, re, ce, jnp.logical_not(first))
    hc[0] = harmonic(ce[3], ce[4])

    def start(side, carry):
        for t in range(4):
            x = slab_x(side, t)
            c = ce[x]
            xm = hc[0] if t == 0 else hx[side, t - 1]
            xp = None
            if t < 3:
                xp = harmonic(c, ce[slab_x(side, t + 1)])
                hx[side, t] = xp
            hyt, hzt, d = first_weights(c, xp, xm)
            hy[side, t], hz[side, t], dg[side, t] = hyt, hzt, d
            if t < 3:
                r = inverse(d)
                rd[side, t] = r
                v = pe[x]
                image = operate(d, v, xp, pe[slab_x(side, t + 1)], xm, pe[slab_x(side, t - 1)], hyt, hzt)
                p1[side, t] = v + (re[x] - image) * r
        for q in range(2):
            pair_sums(sums, jnp.where(side == 0, 1 - q, 2 + q),
                      ce[slab_x(side, 2 * q)], ce[slab_x(side, 2 * q + 1)], 0.125)
        return carry

    lax.fori_loop(0, 2, start, 0)

    def image(side, t, p):
        xm, pm = (hc[0], p[1 - side, 0]) if t == 0 else (hx[side, t - 1], p[side, t - 1])
        return operate(dg[side, t], p[side, t], hx[side, t], p[side, t + 1], xm, pm, hy[side, t], hz[side, t])

    def second(side, carry):
        for t in range(2):
            p2[side, t] = p1[side, t] + (re[slab_x(side, t)] - image(side, t, p1)) * rd[side, t]
        return carry

    lax.fori_loop(0, 2, second, 0)

    def third(side, carry):
        res[side] = re[slab_x(side, 0)] - image(side, 0, p2)
        return carry

    lax.fori_loop(0, 2, third, 0)
    cmid[...] = halve_fine(sums, packed, 4)


def one_side(side, received, own_end, pe, re, ce, hx, hc, hy, hz, dg, rd, p1, p2, res, phi, half,
             hxh, hyh, hzh, dgh, rdh, p1h, p2h, resh, sums, packed):
    at = positions((8, 512), 0)
    top = at < 4

    def slabs_of(own, a, more):
        tiles = TILES[a]
        first_row = 8 * sum(sum(t) if own_end is None else sum(t) - len(t) for t in TILES[:a])
        own_row = 8 * sum(len(t) for t in TILES[:a])
        def load(j):
            if j == 0:
                return own[slab_x(side, 3)]
            n = tiles[j - 1]
            if own_end is None:
                row = first_row + 8 * sum(tiles[:j - 1])
                parts = [received[row + 8 * t:row + 8 * t + 8, :] for t in range(n)]
            else:
                row = own_row + 8 * jnp.where(side == 1, j - 1, len(tiles) - j)
                parts = [own_end[pl.ds(pl.multiple_of(row, 8), 8), :]]
                row = first_row + 8 * (j - 1)
                parts += [received[row:row + 8, :]] * (n - 1)
            if n == 1:
                parts += [jnp.zeros((8, 512), F32)] * 2
            elif j <= len(more):
                parts += [jnp.where(top, more[j - 1], parts[1])]
                parts[1] = jnp.where(top, parts[1], more[j - 1])
            else:
                parts += [parts[1]]
            return jnp.concatenate(parts, axis=0)
        return load

    row = received.shape[0] - 16
    more_p, more_c = received[row:row + 8, :], received[row + 8:row + 16, :]
    more_r = jnp.where(top, along(more_p, 0, -2), along(more_p, 0, 2))
    p0h = slabs_of(pe, 0, (more_p, along(more_p, 0, 4)))
    rsh = slabs_of(re, 1, (more_r,))
    ch = slabs_of(ce, 2, (more_c, along(more_c, 0, 4)))
    c = ch(0)
    xp = harmonic(c, ch(1))
    d = dg[side, 3] + weight(xp, c)
    r = inverse(d)
    hxh[0], hyh[0], hzh[0], dgh[0], rdh[0] = xp, hy[side, 3], hz[side, 3], d, r
    v = p0h(0)
    image = operate(d, v, xp, p0h(1), hx[side, 2], pe[slab_x(side, 2)], hy[side, 3], hz[side, 3])
    p1h[0] = v + (rsh(0) - image) * r

    for j in range(1, 7):
        c = ch(j)
        xp, xm = harmonic(c, ch(j + 1)), hxh[j - 1]
        hyj, hzj, d = first_weights(c, xp, xm)
        r = inverse(d)
        hxh[j], hyh[j], hzh[j], dgh[j], rdh[j] = xp, hyj, hzj, d, r
        v = p0h(j)
        image = operate(d, v, xp, p0h(j + 1), xm, p0h(j - 1), hyj, hzj)
        p1h[j] = v + (rsh(j) - image) * r

    image = operate(dg[side, 2], p1[side, 2], hx[side, 2], p1h[0], hx[side, 1], p1[side, 1],
                    hy[side, 2], hz[side, 2])
    p2h[1] = p1[side, 2] + (re[slab_x(side, 2)] - image) * rd[side, 2]
    p2h[0] = p2[side, 1]
    image = operate(dgh[0], p1h[0], hxh[0], p1h[1], hx[side, 2], p1[side, 2],
                    hyh[0], hzh[0])
    p2h[2] = p1h[0] + (rsh(0) - image) * rdh[0]

    for j in range(1, 6):
        v = p1h[j]
        image = operate(dgh[j], v, hxh[j], p1h[j + 1], hxh[j - 1], p1h[j - 1],
                        hyh[j], hzh[j])
        p2h[j + 2] = v + (rsh(j) - image) * rdh[j]
    for t in range(4):
        phi[jnp.where(side == 0, 3 - t, t)] = (p2[side, t] if t < 2 else p2h[t - 1])[0:8, :]

    for t in (1, 2):
        image = operate(dg[side, t], p2h[t - 1], hx[side, t], p2h[t], hx[side, t - 1],
                        p2[side, 0] if t == 1 else p2h[0], hy[side, t], hz[side, t])
        resh[t - 1] = re[slab_x(side, t)] - image
    image = operate(dgh[0], p2h[2], hxh[0], p2h[3], hx[side, 2], p2h[1],
                    hyh[0], hzh[0])
    resh[2] = rsh(0) - image

    for j in range(1, 5):
        image = operate(dgh[j], p2h[j + 2], hxh[j], p2h[j + 3], hxh[j - 1],
                        p2h[j + 1], hyh[j], hzh[j])
        resh[j + 2] = rsh(j) - image
    for q in range(4):
        a = res[side] if q == 0 else resh[2 * q - 1]
        pair_sums(sums, q, a, resh[2 * q], 0.5)
        pair_sums(sums, 4 + q, ch(2 * q + 1), ch(2 * q + 2), 0.125)
    half[...] = halve_fine(sums, packed, 8)


def mate_side(*refs):
    side = jnp.where(is_first(), 1, 0)
    one_side(side, refs[12].at[side], None, *refs[:12], *refs[13:])


def other_side(*refs):
    one_side(jnp.where(is_first(), 0, 1), refs[12], refs[13], *refs[:12], *refs[14:])


def middle(mate, other, cmid, phi_mate, phi_other, phi_out, emid, out, sums, left):
    side = jnp.where(is_first(), 1, 0)
    stores = [pltpu.make_async_copy(src, phi_out.at[pl.ds(4 * at, 4)], left.at[k])
              for k, (src, at) in enumerate(((phi_mate, side), (phi_other, 1 - side)))]
    for store in stores:
        store.start()
    first = is_first()
    lo = [jnp.where(first, other[j], mate[j]) for j in range(8)]
    hi = [jnp.where(first, mate[j], other[j]) for j in range(8)]
    s = lo[3::-1] + hi[0:4]
    c = lo[:3:-1] + [cmid[j] for j in range(4)] + hi[4:8]
    hx = [harmonic(c[j], c[j + 1]) for j in range(1, 10)]
    hy, hz, d, r, e1 = [], [], [], [], []
    for i in range(8):
        ci = c[i + 2]
        hy.append(harmonic(ci, along(ci, 0, 1)))
        hz.append(z_face(ci))
        d.append(diagonal_of(ci, hx[i + 1], hx[i], hy[i], hz[i]))
        r.append(inverse(d[i]))
        e1.append(s[i] * r[i])

    def image(i, e):
        return operate(d[i], e[i], hx[i + 1], e[i + 1], hx[i], e[i - 1], hy[i], hz[i])

    e2 = [None] + [e1[i] + (s[i] - image(i, e1)) * r[i] for i in range(1, 7)] + [None]
    res = [s[i] - image(i, e2) for i in range(2, 6)]
    for x in range(4):
        emid[x] = e2[2 + x][0:4, :]
    groups = [(res[2 * x] + res[2 * x + 1]) * 0.5 for x in range(2)]
    groups += [(c[2 * x] + c[2 * x + 1]) * 0.125 for x in range(6)]
    for g in range(8):
        both = (groups[g] + along(groups[g], 0, 1))[0:8, :]
        sums[8 * g:8 * g + 8, :] = both[:, 0:128]
        sums[64 + 8 * g:72 + 8 * g, :] = both[:, 128:256]

    def rows(y):
        return jnp.concatenate([sums[pl.ds(64 * q + 2 * y, 8, stride=8), :] for q in range(2)], axis=1)

    low0 = matmul(rows(0), halving(256, 128))
    low1 = matmul(rows(1), halving(256, 128))
    for n in range(16):
        out[n, 0:8, :] = low0
        out[n, 8:16, :] = low1
    for store in stores:
        store.wait()


def y_face(c):
    n = c.shape[0]
    return harmonic(c, jnp.where(positions(c.shape, 0) < n - 1, along(c, 0, 1), 0.0))


def low(gathered, elow, cnear, out, scol, ccol, sums):
    for g in range(8):
        for y in range(2):
            ref, k = (scol, g) if g < 2 else (ccol, g - 2)
            ref[pl.ds(32 * k + y, 16, stride=2), :] = gathered[pl.ds(8 * y + g, 16, stride=16), :]
    c = [ccol[32 * j:32 * j + 32, :] for j in range(6)]
    zero = jnp.zeros((32, 128), F32)
    s = [zero, zero, scol[0:32, :], scol[32:64, :], zero, zero]
    hx = [harmonic(c[j], c[j + 1]) for j in range(5)]
    hy, hz, d, r = [None], [None], [None], [None]
    for j in range(1, 5):
        hy.append(y_face(c[j]))
        hz.append(z_face(c[j]))
        d.append(diagonal_of(c[j], hx[j], hx[j - 1], hy[j], hz[j]))
        r.append(inverse(d[j]))
    e1 = [zero, zero, s[2] * r[2], s[3] * r[3], zero, zero]

    def image(j, e):
        return operate(d[j], e[j], hx[j], e[j + 1], hx[j - 1], e[j - 1], hy[j], hz[j])

    e2 = [zero, hx[1] * e1[2] * r[1]]
    e2 += [e1[j] + (s[j] - image(j, e1)) * r[j] for j in (2, 3)]
    e2 += [hx[3] * e1[3] * r[4], zero]
    res = [hx[0] * e2[1]] + [s[j] - image(j, e2) for j in range(1, 5)] + [hx[4] * e2[4]]

    quads = [(res[2] + res[3]) * 0.5, (c[2] + c[3]) * 0.125, (res[0] + res[1]) * 0.5, (res[4] + res[5]) * 0.5]
    quads += [(c[0] + c[1]) * 0.125, (c[4] + c[5]) * 0.125]
    for k in range(6):
        sums[32 * k:32 * k + 32, :] = quads[k] + along(quads[k], 0, 1)
    rows = [sums[pl.ds(32 * k, 16, stride=2), :] for k in range(6)]
    rows = [jnp.concatenate(rows[k:k + 2], axis=1) for k in (0, 2, 4)]
    both = matmul(jnp.concatenate(rows, axis=0), halving(256, 128))
    cnear[...] = both[32:48, :]
    row = positions((32, 128), 0) - 2 * lax.axis_index("gy")
    errors = [jnp.sum(jnp.where(row == y, e2[j], 0.0), axis=0, keepdims=True) for j in (2, 3, 1, 4) for y in range(2)]
    errors = jnp.concatenate(errors, axis=0)
    elow[...] = errors
    for n in range(32):
        out[n] = both[0:32, :]
    send = errors[4:8, :]
    send = jnp.concatenate([along(send, 1, 64), send], axis=0)
    send = jnp.where(positions((8, 128), 1) < 64, both[0:8, :], send)
    gx = lax.axis_index("gx")

    @pl.when(gx > 0)
    def _():
        out[gx - 1, 0:8, :] = send

    @pl.when(gx < 31)
    def _():
        out[gx + 1, 0:8, :] = send


def bottom(gathered, elow, cnear, emid, out, hx, hy, hz, dg, sol, res, dire, img):
    half = positions((16, 128), 1) < 64
    last_z = positions((16, 128), 1) % 64 == 63
    last_y = positions((16, 128), 0) == 15
    gx, gy = lax.axis_index("gx"), lax.axis_index("gy")
    before = jnp.where(half, cnear[...], along(cnear[...], 1, 64))
    after = jnp.where(half, along(cnear[...], 1, 64), cnear[...])
    column = positions((16, 128), 1) // 64 * 16
    c = []
    for x in range(16):
        a, b = gathered[x, 0:16, :], gathered[x + 16, 0:16, :]
        source = jnp.where(half, a, along(b, 1, 64))
        value = jnp.where(half, along(a, 1, 64), b)
        value = jnp.where(column == gx - 1 - x, before, value)
        c.append(jnp.where(column == gx + 1 - x, after, value))
        b = along(gathered[x + 17, 16:32, :], 1, 64) if x < 15 else 0.0
        source = source + jnp.where(half, gathered[x + 1, 16:32, :], b)
        a = along(gathered[x - 1, 16:32, :], 1, 64) if x > 0 else 0.0
        source = source + jnp.where(half, a, gathered[x + 15, 16:32, :])
        res[x] = source
        dire[x] = source
        sol[x] = jnp.zeros((16, 128), F32)
    for x in range(16):
        nxt = c[x + 1] if x < 15 else jnp.where(half, along(c[0], 1, 64), 0.0)
        hx[x + 1] = harmonic(c[x], nxt)
    hx[0] = along(hx[16], 1, 64)
    for x in range(16):
        hy[x] = harmonic(c[x], jnp.where(last_y, 0.0, along(c[x], 0, 1)))
        hz[x] = harmonic(c[x], jnp.where(last_z, 0.0, along(c[x], 1, 1)))
        dg[x] = diagonal_of(c[x], hx[x + 1], hx[x], hy[x], hz[x])

    def total(acc):
        return jnp.sum(jnp.sum(acc, axis=0, keepdims=True), axis=1, keepdims=True)

    def dot_image():
        acc = jnp.zeros((16, 128), F32)
        for x in range(16):
            v = dire[x]
            vp = dire[x + 1] if x < 15 else along(dire[0], 1, 64)
            vm = dire[x - 1] if x > 0 else along(dire[15], 1, 64)
            image = operate(dg[x], v, hx[x + 1], vp, hx[x], vm, hy[x], hz[x])
            img[x] = image
            acc = acc + v * image
        return total(acc)

    def norm():
        acc = jnp.zeros((16, 128), F32)
        for x in range(16):
            acc = acc + res[x] * res[x]
        return total(acc)

    def step(_, rr):
        alpha = rr / dot_image()
        acc = jnp.zeros((16, 128), F32)
        for x in range(16):
            sol[x] = sol[x] + alpha * dire[x]
            rx = res[x] - alpha * img[x]
            res[x] = rx
            acc = acc + rx * rx
        new = total(acc)
        beta = new / rr
        for x in range(16):
            dire[x] = res[x] + beta * dire[x]
        return new

    gx, gy = lax.axis_index("gx"), lax.axis_index("gy")
    def errors_from(x, row):
        rows = gathered[x, 0:8, :]
        return jnp.where(positions((2, 128), 1) < 64, along(rows, 1, 64)[row:row + 2, :], rows[row + 4:row + 6, :])

    after = jnp.where(gx < 31, errors_from(jnp.minimum(gx + 1, 31), 0), 0.0)
    before = jnp.where(gx > 0, errors_from(jnp.maximum(gx - 1, 0), 2), 0.0)
    lows = elow[0:4, :] + jnp.concatenate([before, after], axis=0)
    finer = matmul(jnp.concatenate([lows, lows], axis=0), doubling(128, 256, 2))
    rr = lax.fori_loop(0, BOTTOM - 1, step, norm(), unroll=True)
    xi = lax.rem(gx, 16)
    alpha = rr / dot_image()
    mine = sol[xi] + alpha * dire[xi]
    mine = jnp.where(gx >= 16, along(mine, 1, 64), mine)
    row = positions((16, 128), 0)
    mine = jnp.sum(jnp.where(row == gy, mine, 0.0), axis=0, keepdims=True)
    coarse = matmul(jnp.broadcast_to(mine, (8, 128)), doubling(128, 256, 4))
    for x in range(4):
        k = 2 * (x // 2)
        for y in range(4):
            add = finer[k + y // 2:k + y // 2 + 1, :] + coarse[0:1, :]
            out[x, y:y + 1, :] = emid[x, y:y + 1, :] + add


def swap(values, axis, far):
    n = lax.axis_size(axis)
    pairs = [(i, i + 1) for i in range(int(far), n - 1, 2)]
    return lax.ppermute(values, axis, pairs + [(j, i) for i, j in pairs])


def shards(phi_start, right_side, coefficient):
    own = [a.reshape(64, 512) for a in (phi_start, right_side, coefficient)]
    near, far, own_end = call(
        pack_y, [(8 * NROWS, 512)] * 2 + [(OWN_ROWS, 512)], [(64, 512)] * 3 + [(768, 128), (2, 8 * NROWS, 512)],
        n_in=3, copies=12, in_hbm=3, out_hbm=3, limit=64000000)(*own)
    far = swap(far, "gy", True)
    near = swap(near, "gy", False)
    own_end = swap(own_end, "gx", True)
    own = call(hold, [(64, 512)] * 3, n_in=3,
               cost=pl.CostEstimate(flops=16_000_000, bytes_accessed=4_000_000, transcendentals=0))(*own)
    *ext, other = call(pack_x, [(192, 512)] * 3 + [(END_ROWS - OWN_ROWS, 512)], [(1536, 128)], n_in=5)(*own, far, near)
    other = swap(other, "gx", True)
    ext = [a.reshape(8, 24, 512) for a in ext]

    def slabs(*n):
        return (*n, 24, 512)

    *inside, cmid, mate = call(
        inner,
        [slabs(2, 3), slabs(1)] + [slabs(2, 4)] * 3 + [slabs(2, 3)] * 2 + [slabs(2, 2), slabs(2), (4, 16, 256), (2, END_ROWS, 512)],
        [(4, 4, 24, 128), (64, 512)], n_in=3,
        cost=pl.CostEstimate(flops=1_000, bytes_accessed=1_000, transcendentals=0),
    )(*ext)
    chips = [[i, i + 1] for i in range(0, lax.axis_size("gx"), 2)]
    mate = lax.all_to_all(mate, "gx", 0, 0, tiled=True, axis_index_groups=chips)
    scratch = [slabs(9)] * 8 + [(4, 8, 24, 128), (128, 512)]
    phi_mate, half = call(
        mate_side, [(4, 8, 512), (8, 16, 256)], scratch, n_in=13,
        cost=pl.CostEstimate(flops=1_000, bytes_accessed=1_000, transcendentals=0),
    )(*ext, *inside, mate)
    phi_other, other_half = call(
        other_side, [(4, 8, 512), (8, 16, 256)], scratch, n_in=14)(*ext, *inside, other, own_end)
    phi_fine, emid, spread = call(
        middle, [(8, 8, 512), (4, 4, 256), (16, 16, 128)], [(128, 128)], n_in=5, copies=2, out_hbm=1)(
        half, other_half, cmid, phi_mate, phi_other)
    gathered = lax.all_to_all(spread, "gy", 0, 0, tiled=True)
    elow, cnear, spread = call(
        low, [(8, 128), (16, 128), (32, 32, 128)], [(64, 128), (192, 128), (192, 128)], n_in=1)(gathered.reshape(256, 128))
    gathered = lax.all_to_all(spread, "gx", 0, 0, tiled=True)
    (correction,) = call(bottom, [(4, 4, 256)], [(17, 16, 128)] + [(16, 16, 128)] * 7, n_in=4)(
        gathered, elow, cnear, emid)
    return phi_fine, correction


def solution(mesh):
    return jax.shard_map(
        shards,
        mesh=mesh,
        in_specs=(P("gx", "gy", None),) * 3,
        out_specs=(P("gx", "gy", None),) * 2,
        check_vma=False,
    )
```

```python
import jax
import jax.numpy as jnp
from jax import lax
from jax.experimental import pallas as pl
from jax.experimental.pallas import tpu as pltpu
from jax.sharding import PartitionSpec as P

BOTTOM = 6
RELAX_WEIGHT = 0.8
FLOOR = 1e-3
F32 = jnp.float32
VMEM = pl.BlockSpec(memory_space=pltpu.VMEM)
HBM = pl.BlockSpec(memory_space=pltpu.HBM)


def call(kernel, out_shapes, scratch=(), n_in=0, copies=0, in_hbm=0, out_hbm=0, limit=24 * 1024 * 1024, cost=None):
    semaphores = [pltpu.SemaphoreType.DMA((copies,))] if copies else []
    return pl.pallas_call(
        kernel,
        out_shape=[jax.ShapeDtypeStruct(s, F32) for s in out_shapes],
        in_specs=[HBM] * in_hbm + [VMEM] * (n_in - in_hbm),
        out_specs=[HBM] * out_hbm + [VMEM] * (len(out_shapes) - out_hbm),
        scratch_shapes=[pltpu.VMEM(s, F32) for s in scratch] + semaphores,
        compiler_params=pltpu.CompilerParams(vmem_limit_bytes=limit),
        cost_estimate=cost,
    )


def reciprocal(x):
    r = pl.reciprocal(x, approx=True)
    return r * (2.0 - x * r)


def harmonic(a, b):
    return 2.0 * a * b * reciprocal(jnp.maximum(a + b, FLOOR))


def along(v, axis, step):
    n = v.shape[axis]
    return pltpu.roll(v, (-step) % n, axis)


def is_first():
    return lax.rem(lax.axis_index("gx"), 2) == 0


def positions(shape, axis):
    return lax.broadcasted_iota(jnp.int32, shape, axis)


def halving(rows, cols):
    return (positions((rows, cols), 0) // 2 == positions((rows, cols), 1)).astype(F32)


def doubling(rows, cols, factor):
    return (positions((rows, cols), 1) // factor == positions((rows, cols), 0)).astype(F32)


def matmul(a, b):
    return exact_matmul(a, b)


def exact_matmul(a, ones):
    parts = []
    for _ in range(3):
        parts.append(a.astype(jnp.bfloat16))
        a = a - parts[-1].astype(F32)
    ones = ones.astype(jnp.bfloat16)
    return sum(jnp.dot(p, ones, preferred_element_type=F32) for p in reversed(parts))


def weight(face, centre):
    return jnp.where(face > 0.0, face, centre)


def diagonal_of(c, xp, xm, hy, hz):
    return (weight(xp, c) + weight(xm, c) + weight(hy, c) + weight(along(hy, 0, -1), c)
            + weight(hz, c) + weight(along(hz, 1, -1), c))


def operate(d, v, xp, vp, xm, vm, hy, hz):
    out = d * v - xp * vp - xm * vm
    out = out - hy * along(v, 0, 1) - along(hy * v, 0, -1)
    return out - hz * along(v, 1, 1) - along(hz * v, 1, -1)


def z_face(c):
    nxt = jnp.where(positions(c.shape, 1) < c.shape[1] - 1, along(c, 1, 1), 0.0)
    return harmonic(c, nxt)


NP, NR, NC = 7, 6, 7
NROWS = NP + NR + NC
PHI_TILES = (2, 2, 2, 2, 2, 2, 1)
RHS_TILES = (2, 2, 2, 2, 2, 1)
COEF_TILES = (2, 2, 2, 2, 2, 2, 1, 1)
TILES = (PHI_TILES, RHS_TILES, COEF_TILES)
PHI_MORE = 8 * (sum(PHI_TILES) + sum(RHS_TILES) + sum(COEF_TILES))
COEF_MORE = PHI_MORE + 8
END_ROWS = PHI_MORE + 16
OWN_ROWS = 8 * (len(PHI_TILES) + len(RHS_TILES) + len(COEF_TILES))


def pack_y(phi_in, rhs_in, coef_in, near, far, own_end, phi, rhs, coef, stage, ends, sem):
    loads = [pltpu.make_async_copy(src, dst, sem.at[a])
             for a, (src, dst) in enumerate(((phi_in, phi), (rhs_in, rhs), (coef_in, coef)))]
    for load in loads:
        load.start()
    stores, row = [], 0
    k = 0
    for a, (ref, n) in enumerate(((phi, NP), (rhs, NR), (coef, NC))):
        loads[a].wait()
        slabs = 8 * len(TILES[a])
        first_row = pl.multiple_of(jnp.where(is_first(), 0, 64 - slabs), 8)
        stores.append(pltpu.make_async_copy(ref.at[pl.ds(first_row, slabs)], own_end.at[pl.ds(row, slabs)], sem.at[9 + a]))
        stores[-1].start()
        row += slabs
        for q in range(4):
            lanes = slice(128 * q, 128 * q + 128)
            base = 64 * (4 * a + q)
            stage[base:base + 64, :] = ref[:, lanes]
            for j in range(n):
                rows = slice(8 * (k + j), 8 * (k + j) + 8)
                ends[0, rows, lanes] = stage[pl.ds(base + 8 - n + j, 8, stride=8), :]
                ends[1, rows, lanes] = stage[pl.ds(base + j, 8, stride=8), :]
        for b, dst in enumerate((near, far)):
            part = pl.ds(8 * k, 8 * n)
            src = ends.at[lax.rem(lax.axis_index("gy") + b, 2), part]
            stores.append(pltpu.make_async_copy(src, dst.at[part], sem.at[3 + 2 * a + b]))
            stores[-1].start()
        k += n
    for store in stores:
        store.wait()


def hold(*refs):
    for src, dst in zip(refs[:3], refs[3:]):
        dst[...] = src[...]


def pack_x(phi, rhs, coef, _own_end, far, near, pe, re, ce, other, mate, stage):
    zero = jnp.zeros((8, 128), F32)
    odd = lax.rem(lax.axis_index("gy"), 2)
    k = 0
    for a, (ref, ext, n) in enumerate(((phi, pe, NP), (rhs, re, NR), (coef, ce, NC))):
        for x in range(8):
            ext[24 * x:24 * x + 8, :] = ref[8 * x:8 * x + 8, :]
        for q in range(4):
            lanes = slice(128 * q, 128 * q + 128)
            base = 128 * (4 * a + q)
            for j in range(n):
                rows = slice(8 * (k + j), 8 * (k + j) + 8)
                stage[pl.ds(base + j + odd * (16 - n), 8, stride=16), :] = near[rows, lanes]
                stage[pl.ds(base + j + (1 - odd) * (16 - n), 8, stride=16), :] = far[rows, lanes]
            for j in range(n, 16 - n):
                stage[pl.ds(base + j, 8, stride=16), :] = zero
            for x in range(8):
                ext[24 * x + 8:24 * x + 24, lanes] = stage[base + 16 * x:base + 16 * x + 16, :]
        k += n
    first = is_first()
    pack_end(other, lambda ext, x, t: ext[pl.ds(pl.multiple_of(24 * x + 8 * t, 8), 8), :], pe, re, ce, first, False)
    pack_end(mate, lambda ext, x, t: ext[pl.ds(pl.multiple_of(24 * x + 8 * t, 8), 8), :], pe, re, ce, jnp.logical_not(first))


def pack_end(out, tile, pe, re, ce, is_low, with_own=True):
    top = positions((8, 512), 0) < 4
    row = 0
    for ext, tiles in ((pe, PHI_TILES), (re, RHS_TILES), (ce, COEF_TILES)):
        for k, n in enumerate(tiles):
            x = jnp.where(is_low, k, 7 - k)
            parts = [tile(ext, x, 0)] if with_own else []
            if n == 2:
                parts.append(jnp.where(top, tile(ext, x, 1), tile(ext, x, 2)))
            for part in parts:
                out[row:row + 8, :] = part
                row += 8

    def beyond(ext, k):
        x = jnp.where(is_low, k, 7 - k)
        return jnp.where(top, tile(ext, x, 2), tile(ext, x, 1))

    at = positions((8, 512), 0)
    ends = (at == 0) | (at == 7)
    more = jnp.where(ends, along(beyond(pe, 1), 0, 4), beyond(pe, 0))
    source = beyond(re, 0)
    more = jnp.where(at == 1, along(source, 0, 2), jnp.where(at == 6, along(source, 0, -2), more))
    out[row:row + 8, :] = more
    out[row + 8:row + 16, :] = jnp.where(ends, along(beyond(ce, 1), 0, 4), beyond(ce, 0))


def slab_x(side, t):
    return jnp.where(side == 0, 3 - t, 4 + t)


def first_weights(c, xp, xm):
    hy = harmonic(c, along(c, 0, 1))
    hz = z_face(c)
    d = weight(xm, c) + weight(hy, c) + weight(along(hy, 0, -1), c) + weight(hz, c) + weight(along(hz, 1, -1), c)
    return hy, hz, d if xp is None else d + weight(xp, c)


def inverse(d):
    return RELAX_WEIGHT * reciprocal(jnp.maximum(d, FLOOR))


def pair_sums(sums, place, a, b, scale):
    t = a + b
    t = (t + along(t, 0, 1)) * scale
    for q in range(4):
        sums[q, place] = t[:, 128 * q:128 * q + 128]


def halve_fine(sums, packed, n):
    for k in range(n):
        for q in range(4):
            lanes = slice(128 * q, 128 * q + 128)
            packed[16 * k:16 * k + 8, lanes] = sums[q, k, pl.ds(0, 8, stride=2), :]
            packed[16 * k + 8:16 * k + 12, lanes] = jnp.zeros((4, 128), F32)
            packed[16 * k + 12:16 * k + 16, lanes] = sums[q, k, pl.ds(16, 4, stride=2), :]
    return exact_matmul(packed[...], halving(512, 256)).reshape(n, 16, 256)


def inner(pe, re, ce, hx, hc, hy, hz, dg, rd, p1, p2, res, cmid, sums, packed):
    hc[0] = harmonic(ce[3], ce[4])

    def start(side, carry):
        for t in range(4):
            x = slab_x(side, t)
            c = ce[x]
            xm = hc[0] if t == 0 else hx[side, t - 1]
            xp = None
            if t < 3:
                xp = harmonic(c, ce[slab_x(side, t + 1)])
                hx[side, t] = xp
            hyt, hzt, d = first_weights(c, xp, xm)
            hy[side, t], hz[side, t], dg[side, t] = hyt, hzt, d
            if t < 3:
                r = inverse(d)
                rd[side, t] = r
                v = pe[x]
                image = operate(d, v, xp, pe[slab_x(side, t + 1)], xm, pe[slab_x(side, t - 1)], hyt, hzt)
                p1[side, t] = v + (re[x] - image) * r
        for q in range(2):
            pair_sums(sums, jnp.where(side == 0, 1 - q, 2 + q),
                      ce[slab_x(side, 2 * q)], ce[slab_x(side, 2 * q + 1)], 0.125)
        return carry

    lax.fori_loop(0, 2, start, 0)

    def image(side, t, p):
        xm, pm = (hc[0], p[1 - side, 0]) if t == 0 else (hx[side, t - 1], p[side, t - 1])
        return operate(dg[side, t], p[side, t], hx[side, t], p[side, t + 1], xm, pm, hy[side, t], hz[side, t])

    def second(side, carry):
        for t in range(2):
            p2[side, t] = p1[side, t] + (re[slab_x(side, t)] - image(side, t, p1)) * rd[side, t]
        return carry

    lax.fori_loop(0, 2, second, 0)

    def third(side, carry):
        res[side] = re[slab_x(side, 0)] - image(side, 0, p2)
        return carry

    lax.fori_loop(0, 2, third, 0)
    cmid[...] = halve_fine(sums, packed, 4)


def one_side(side, received, own_end, pe, re, ce, hx, hc, hy, hz, dg, rd, p1, p2, res, phi, half,
             hxh, hyh, hzh, dgh, rdh, p1h, p2h, resh, sums, packed):
    at = positions((8, 512), 0)
    top = at < 4

    def slabs_of(own, a, more):
        tiles = TILES[a]
        first_row = 8 * sum(sum(t) if own_end is None else sum(t) - len(t) for t in TILES[:a])
        own_row = 8 * sum(len(t) for t in TILES[:a])
        def load(j):
            if j == 0:
                return own[slab_x(side, 3)]
            n = tiles[j - 1]
            if own_end is None:
                row = first_row + 8 * sum(tiles[:j - 1])
                parts = [received[row + 8 * t:row + 8 * t + 8, :] for t in range(n)]
            else:
                row = own_row + 8 * jnp.where(side == 1, j - 1, len(tiles) - j)
                parts = [own_end[pl.ds(pl.multiple_of(row, 8), 8), :]]
                row = first_row + 8 * (j - 1)
                parts += [received[row:row + 8, :]] * (n - 1)
            if n == 1:
                parts += [jnp.zeros((8, 512), F32)] * 2
            elif j <= len(more):
                parts += [jnp.where(top, more[j - 1], parts[1])]
                parts[1] = jnp.where(top, parts[1], more[j - 1])
            else:
                parts += [parts[1]]
            return jnp.concatenate(parts, axis=0)
        return load

    row = received.shape[0] - 16
    more_p, more_c = received[row:row + 8, :], received[row + 8:row + 16, :]
    more_r = jnp.where(top, along(more_p, 0, -2), along(more_p, 0, 2))
    p0h = slabs_of(pe, 0, (more_p, along(more_p, 0, 4)))
    rsh = slabs_of(re, 1, (more_r,))
    ch = slabs_of(ce, 2, (more_c, along(more_c, 0, 4)))
    c = ch(0)
    xp = harmonic(c, ch(1))
    d = dg[side, 3] + weight(xp, c)
    r = inverse(d)
    hxh[0], hyh[0], hzh[0], dgh[0], rdh[0] = xp, hy[side, 3], hz[side, 3], d, r
    v = p0h(0)
    image = operate(d, v, xp, p0h(1), hx[side, 2], pe[slab_x(side, 2)], hy[side, 3], hz[side, 3])
    p1h[0] = v + (rsh(0) - image) * r

    for j in range(1, 7):
        c = ch(j)
        xp, xm = harmonic(c, ch(j + 1)), hxh[j - 1]
        hyj, hzj, d = first_weights(c, xp, xm)
        r = inverse(d)
        hxh[j], hyh[j], hzh[j], dgh[j], rdh[j] = xp, hyj, hzj, d, r
        v = p0h(j)
        image = operate(d, v, xp, p0h(j + 1), xm, p0h(j - 1), hyj, hzj)
        p1h[j] = v + (rsh(j) - image) * r

    image = operate(dg[side, 2], p1[side, 2], hx[side, 2], p1h[0], hx[side, 1], p1[side, 1],
                    hy[side, 2], hz[side, 2])
    p2h[1] = p1[side, 2] + (re[slab_x(side, 2)] - image) * rd[side, 2]
    p2h[0] = p2[side, 1]
    image = operate(dgh[0], p1h[0], hxh[0], p1h[1], hx[side, 2], p1[side, 2],
                    hyh[0], hzh[0])
    p2h[2] = p1h[0] + (rsh(0) - image) * rdh[0]

    for j in range(1, 6):
        v = p1h[j]
        image = operate(dgh[j], v, hxh[j], p1h[j + 1], hxh[j - 1], p1h[j - 1],
                        hyh[j], hzh[j])
        p2h[j + 2] = v + (rsh(j) - image) * rdh[j]
    for t in range(4):
        phi[jnp.where(side == 0, 3 - t, t)] = (p2[side, t] if t < 2 else p2h[t - 1])[0:8, :]

    for t in (1, 2):
        image = operate(dg[side, t], p2h[t - 1], hx[side, t], p2h[t], hx[side, t - 1],
                        p2[side, 0] if t == 1 else p2h[0], hy[side, t], hz[side, t])
        resh[t - 1] = re[slab_x(side, t)] - image
    image = operate(dgh[0], p2h[2], hxh[0], p2h[3], hx[side, 2], p2h[1],
                    hyh[0], hzh[0])
    resh[2] = rsh(0) - image

    for j in range(1, 5):
        image = operate(dgh[j], p2h[j + 2], hxh[j], p2h[j + 3], hxh[j - 1],
                        p2h[j + 1], hyh[j], hzh[j])
        resh[j + 2] = rsh(j) - image
    for q in range(4):
        a = res[side] if q == 0 else resh[2 * q - 1]
        pair_sums(sums, q, a, resh[2 * q], 0.5)
        pair_sums(sums, 4 + q, ch(2 * q + 1), ch(2 * q + 2), 0.125)
    half[...] = halve_fine(sums, packed, 8)


def mate_side(*refs):
    side = jnp.where(is_first(), 1, 0)
    one_side(side, refs[12], None, *refs[:12], *refs[14:])


def other_side(*refs):
    one_side(jnp.where(is_first(), 0, 1), refs[12], refs[13], *refs[:12], *refs[15:])


def middle(mate, other, cmid, phi_mate, phi_other, phi_out, emid, out, sums, left):
    side = jnp.where(is_first(), 1, 0)
    stores = [pltpu.make_async_copy(src, phi_out.at[pl.ds(4 * at, 4)], left.at[k])
              for k, (src, at) in enumerate(((phi_mate, side), (phi_other, 1 - side)))]
    for store in stores:
        store.start()
    first = is_first()
    lo = [jnp.where(first, other[j], mate[j]) for j in range(8)]
    hi = [jnp.where(first, mate[j], other[j]) for j in range(8)]
    s = lo[3::-1] + hi[0:4]
    c = lo[:3:-1] + [cmid[j] for j in range(4)] + hi[4:8]
    hx = [harmonic(c[j], c[j + 1]) for j in range(1, 10)]
    hy, hz, d, r, e1 = [], [], [], [], []
    for i in range(8):
        ci = c[i + 2]
        hy.append(harmonic(ci, along(ci, 0, 1)))
        hz.append(z_face(ci))
        d.append(diagonal_of(ci, hx[i + 1], hx[i], hy[i], hz[i]))
        r.append(inverse(d[i]))
        e1.append(s[i] * r[i])

    def image(i, e):
        return operate(d[i], e[i], hx[i + 1], e[i + 1], hx[i], e[i - 1], hy[i], hz[i])

    e2 = [None] + [e1[i] + (s[i] - image(i, e1)) * r[i] for i in range(1, 7)] + [None]
    res = [s[i] - image(i, e2) for i in range(2, 6)]
    for x in range(4):
        emid[x] = e2[2 + x][0:4, :]
    groups = [(res[2 * x] + res[2 * x + 1]) * 0.5 for x in range(2)]
    groups += [(c[2 * x] + c[2 * x + 1]) * 0.125 for x in range(6)]
    for g in range(8):
        both = (groups[g] + along(groups[g], 0, 1))[0:8, :]
        sums[8 * g:8 * g + 8, :] = both[:, 0:128]
        sums[64 + 8 * g:72 + 8 * g, :] = both[:, 128:256]

    def rows(y):
        return jnp.concatenate([sums[pl.ds(64 * q + 2 * y, 8, stride=8), :] for q in range(2)], axis=1)

    low0 = matmul(rows(0), halving(256, 128))
    low1 = matmul(rows(1), halving(256, 128))
    for n in range(16):
        out[n, 0:8, :] = low0
        out[n, 8:16, :] = low1
    for store in stores:
        store.wait()


def y_face(c):
    n = c.shape[0]
    return harmonic(c, jnp.where(positions(c.shape, 0) < n - 1, along(c, 0, 1), 0.0))


def low(gathered, elow, cnear, out, scol, ccol, sums):
    for g in range(8):
        for y in range(2):
            ref, k = (scol, g) if g < 2 else (ccol, g - 2)
            ref[pl.ds(32 * k + y, 16, stride=2), :] = gathered[pl.ds(8 * y + g, 16, stride=16), :]
    c = [ccol[32 * j:32 * j + 32, :] for j in range(6)]
    zero = jnp.zeros((32, 128), F32)
    s = [zero, zero, scol[0:32, :], scol[32:64, :], zero, zero]
    hx = [harmonic(c[j], c[j + 1]) for j in range(5)]
    hy, hz, d, r = [None], [None], [None], [None]
    for j in range(1, 5):
        hy.append(y_face(c[j]))
        hz.append(z_face(c[j]))
        d.append(diagonal_of(c[j], hx[j], hx[j - 1], hy[j], hz[j]))
        r.append(inverse(d[j]))
    e1 = [zero, zero, s[2] * r[2], s[3] * r[3], zero, zero]

    def image(j, e):
        return operate(d[j], e[j], hx[j], e[j + 1], hx[j - 1], e[j - 1], hy[j], hz[j])

    e2 = [zero, hx[1] * e1[2] * r[1]]
    e2 += [e1[j] + (s[j] - image(j, e1)) * r[j] for j in (2, 3)]
    e2 += [hx[3] * e1[3] * r[4], zero]
    res = [hx[0] * e2[1]] + [s[j] - image(j, e2) for j in range(1, 5)] + [hx[4] * e2[4]]

    quads = [(res[2] + res[3]) * 0.5, (c[2] + c[3]) * 0.125, (res[0] + res[1]) * 0.5, (res[4] + res[5]) * 0.5]
    quads += [(c[0] + c[1]) * 0.125, (c[4] + c[5]) * 0.125]
    for k in range(6):
        sums[32 * k:32 * k + 32, :] = quads[k] + along(quads[k], 0, 1)
    rows = [sums[pl.ds(32 * k, 16, stride=2), :] for k in range(6)]
    rows = [jnp.concatenate(rows[k:k + 2], axis=1) for k in (0, 2, 4)]
    both = matmul(jnp.concatenate(rows, axis=0), halving(256, 128))
    cnear[...] = both[32:48, :]
    row = positions((32, 128), 0) - 2 * lax.axis_index("gy")
    errors = [jnp.sum(jnp.where(row == y, e2[j], 0.0), axis=0, keepdims=True) for j in (2, 3, 1, 4) for y in range(2)]
    errors = jnp.concatenate(errors, axis=0)
    elow[...] = errors
    for n in range(32):
        out[n] = both[0:32, :]
    send = errors[4:8, :]
    send = jnp.concatenate([along(send, 1, 64), send], axis=0)
    send = jnp.where(positions((8, 128), 1) < 64, both[0:8, :], send)
    gx = lax.axis_index("gx")

    @pl.when(gx > 0)
    def _():
        out[gx - 1, 0:8, :] = send

    @pl.when(gx < 31)
    def _():
        out[gx + 1, 0:8, :] = send


def bottom(gathered, elow, cnear, emid, out, hx, hy, hz, dg, sol, res, dire, img):
    half = positions((16, 128), 1) < 64
    last_z = positions((16, 128), 1) % 64 == 63
    last_y = positions((16, 128), 0) == 15
    gx, gy = lax.axis_index("gx"), lax.axis_index("gy")
    before = jnp.where(half, cnear[...], along(cnear[...], 1, 64))
    after = jnp.where(half, along(cnear[...], 1, 64), cnear[...])
    column = positions((16, 128), 1) // 64 * 16
    c = []
    for x in range(16):
        a, b = gathered[x, 0:16, :], gathered[x + 16, 0:16, :]
        source = jnp.where(half, a, along(b, 1, 64))
        value = jnp.where(half, along(a, 1, 64), b)
        value = jnp.where(column == gx - 1 - x, before, value)
        c.append(jnp.where(column == gx + 1 - x, after, value))
        b = along(gathered[x + 17, 16:32, :], 1, 64) if x < 15 else 0.0
        source = source + jnp.where(half, gathered[x + 1, 16:32, :], b)
        a = along(gathered[x - 1, 16:32, :], 1, 64) if x > 0 else 0.0
        source = source + jnp.where(half, a, gathered[x + 15, 16:32, :])
        res[x] = source
        dire[x] = source
        sol[x] = jnp.zeros((16, 128), F32)
    for x in range(16):
        nxt = c[x + 1] if x < 15 else jnp.where(half, along(c[0], 1, 64), 0.0)
        hx[x + 1] = harmonic(c[x], nxt)
    hx[0] = along(hx[16], 1, 64)
    for x in range(16):
        hy[x] = harmonic(c[x], jnp.where(last_y, 0.0, along(c[x], 0, 1)))
        hz[x] = harmonic(c[x], jnp.where(last_z, 0.0, along(c[x], 1, 1)))
        dg[x] = diagonal_of(c[x], hx[x + 1], hx[x], hy[x], hz[x])

    def total(acc):
        return jnp.sum(jnp.sum(acc, axis=0, keepdims=True), axis=1, keepdims=True)

    def dot_image():
        acc = jnp.zeros((16, 128), F32)
        for x in range(16):
            v = dire[x]
            vp = dire[x + 1] if x < 15 else along(dire[0], 1, 64)
            vm = dire[x - 1] if x > 0 else along(dire[15], 1, 64)
            image = operate(dg[x], v, hx[x + 1], vp, hx[x], vm, hy[x], hz[x])
            img[x] = image
            acc = acc + v * image
        return total(acc)

    def norm():
        acc = jnp.zeros((16, 128), F32)
        for x in range(16):
            acc = acc + res[x] * res[x]
        return total(acc)

    def step(_, rr):
        alpha = rr / dot_image()
        acc = jnp.zeros((16, 128), F32)
        for x in range(16):
            sol[x] = sol[x] + alpha * dire[x]
            rx = res[x] - alpha * img[x]
            res[x] = rx
            acc = acc + rx * rx
        new = total(acc)
        beta = new / rr
        for x in range(16):
            dire[x] = res[x] + beta * dire[x]
        return new

    gx, gy = lax.axis_index("gx"), lax.axis_index("gy")
    def errors_from(x, row):
        rows = gathered[x, 0:8, :]
        return jnp.where(positions((2, 128), 1) < 64, along(rows, 1, 64)[row:row + 2, :], rows[row + 4:row + 6, :])

    after = jnp.where(gx < 31, errors_from(jnp.minimum(gx + 1, 31), 0), 0.0)
    before = jnp.where(gx > 0, errors_from(jnp.maximum(gx - 1, 0), 2), 0.0)
    lows = elow[0:4, :] + jnp.concatenate([before, after], axis=0)
    finer = matmul(jnp.concatenate([lows, lows], axis=0), doubling(128, 256, 2))
    rr = lax.fori_loop(0, BOTTOM - 1, step, norm(), unroll=True)
    xi = lax.rem(gx, 16)
    alpha = rr / dot_image()
    mine = sol[xi] + alpha * dire[xi]
    mine = jnp.where(gx >= 16, along(mine, 1, 64), mine)
    row = positions((16, 128), 0)
    mine = jnp.sum(jnp.where(row == gy, mine, 0.0), axis=0, keepdims=True)
    coarse = matmul(jnp.broadcast_to(mine, (8, 128)), doubling(128, 256, 4))
    for x in range(4):
        k = 2 * (x // 2)
        for y in range(4):
            add = finer[k + y // 2:k + y // 2 + 1, :] + coarse[0:1, :]
            out[x, y:y + 1, :] = emid[x, y:y + 1, :] + add


def swap(values, axis, far):
    n = lax.axis_size(axis)
    pairs = [(i, i + 1) for i in range(int(far), n - 1, 2)]
    return lax.ppermute(values, axis, pairs + [(j, i) for i, j in pairs])


def shards(phi_start, right_side, coefficient):
    own = [a.reshape(64, 512) for a in (phi_start, right_side, coefficient)]
    near, far, own_end = call(
        pack_y, [(8 * NROWS, 512)] * 2 + [(OWN_ROWS, 512)], [(64, 512)] * 3 + [(768, 128), (2, 8 * NROWS, 512)],
        n_in=3, copies=12, in_hbm=3, out_hbm=3, limit=64000000)(*own)
    far = swap(far, "gy", True)
    near = swap(near, "gy", False)
    own_end = swap(own_end, "gx", True)
    own = call(hold, [(64, 512)] * 3, n_in=3,
               cost=pl.CostEstimate(flops=16_000_000, bytes_accessed=4_000_000, transcendentals=0))(*own)
    *ext, other, mate = call(pack_x, [(192, 512)] * 3 + [(END_ROWS - OWN_ROWS, 512), (END_ROWS, 512)], [(1536, 128)], n_in=6)(*own, own_end, far, near)
    other = swap(other, "gx", True)
    mate = swap(mate, "gx", False)
    ext = [a.reshape(8, 24, 512) for a in ext]

    def slabs(*n):
        return (*n, 24, 512)

    *inside, cmid = call(
        inner,
        [slabs(2, 3), slabs(1)] + [slabs(2, 4)] * 3 + [slabs(2, 3)] * 2 + [slabs(2, 2), slabs(2), (4, 16, 256)],
        [(4, 4, 24, 128), (64, 512)], n_in=3,
        cost=pl.CostEstimate(flops=16_000_000, bytes_accessed=4_000_000, transcendentals=0),
    )(*ext)
    scratch = [slabs(9)] * 8 + [(4, 8, 24, 128), (128, 512)]
    phi_mate, half = call(
        mate_side, [(4, 8, 512), (8, 16, 256)], scratch, n_in=14,
        cost=pl.CostEstimate(flops=1_000, bytes_accessed=1_000, transcendentals=0),
    )(*ext, *inside, mate, other)
    phi_other, other_half = call(
        other_side, [(4, 8, 512), (8, 16, 256)], scratch, n_in=15)(*ext, *inside, other, own_end, phi_mate)
    phi_fine, emid, spread = call(
        middle, [(8, 8, 512), (4, 4, 256), (16, 16, 128)], [(128, 128)], n_in=5, copies=2, out_hbm=1)(
        half, other_half, cmid, phi_mate, phi_other)
    gathered = lax.all_to_all(spread, "gy", 0, 0, tiled=True)
    elow, cnear, spread = call(
        low, [(8, 128), (16, 128), (32, 32, 128)], [(64, 128), (192, 128), (192, 128)], n_in=1)(gathered.reshape(256, 128))
    gathered = lax.all_to_all(spread, "gx", 0, 0, tiled=True)
    (correction,) = call(bottom, [(4, 4, 256)], [(17, 16, 128)] + [(16, 16, 128)] * 7, n_in=4)(
        gathered, elow, cnear, emid)
    return phi_fine, correction


def solution(mesh):
    return jax.shard_map(
        shards,
        mesh=mesh,
        in_specs=(P("gx", "gy", None),) * 3,
        out_specs=(P("gx", "gy", None),) * 2,
        check_vma=False,
    )
```
